32 devices in a mesh: dp: 4 (over y, x), expert: 8 (over z, core).
Axes of the slice: x: 2, y: 2, z: 4, core: 2. Of those that a mesh axis runs over, the one named last changes fastest.
Arguments:
- tokens: bfloat16 [4096, 3584], P('expert', 'dp'), may hold values from -6 to 6
- grad_out: bfloat16 [4096, 3584], P('expert', 'dp'), may hold values from -1.796875 to 1.796875
- expert_ids: int32 [4096, 8], P('expert'), may hold values from 0 to 255, as said below
- gates: float32 [4096, 8], P('expert'), may hold values from 0.25 to 2.5
- w_gate: bfloat16 [8, 3584, 1024], P('expert', 'dp'), may hold values from -0.09375 to 0.09375
- w_up: bfloat16 [8, 3584, 1024], P('expert', 'dp'), may hold values from -0.09375 to 0.09375
- w_down: bfloat16 [8, 1024, 3584], P('expert', None, 'dp'), may hold values from -0.1875 to 0.1875
Outputs:
- mixed: bfloat16 [4096, 3584], P('expert', 'dp')
- grad_tokens: bfloat16 [4096, 3584], P('expert', 'dp')
- grad_gate: bfloat16 [8, 3584, 1024], P('expert', 'dp')
- grad_up: bfloat16 [8, 3584, 1024], P('expert', 'dp')
- grad_down: bfloat16 [8, 1024, 3584], P('expert', None, 'dp')
The draws below stay inside these ranges and needn't reach their ends.
Inputs may be any that keep to these rules, and one draw needn't show every extreme that they name: `expert_ids`: each row names 8 different experts, at most one of them below 8. Within each aligned block of 512 rows no expert below 8 is named by more than 32 rows, and one such expert, the same in every block, is named by exactly 32 rows of every block.
All inputs are finite; a program needn't handle non-finite values.
Results may differ from the reference program's by a relative error of at most 0.029.
Values may be sent and summed in bfloat16 or wider, within the bound.
No kernel may reach another device: no remote copies, remote signals or barrier semaphores. Data moves between devices by JAX's collectives and lax.ppermute only.
A program may use at most 64 MiB of HBM per device.

```python
import math
import jax
import jax.numpy as jnp
from jax import lax

D = 3584
HID = 1024
N_ROUTED = 256
TOPK = 8
TOK_E = 512
CAP = 32
EXPERTS = 8
TOKENS = 4096
SLOTS = 256
FEAT_DEV = 896
N_DP = 4


def draw_expert_ids(key, part):
    key_hot, key_pref, key_blocks = jax.random.split(key, 3)
    hot_expert = jax.random.randint(key_hot, (), 0, EXPERTS)
    preference = jax.random.permutation(key_pref, EXPERTS)
    spread = (N_ROUTED - EXPERTS) // TOPK

    def one_block(block_key):
        key_order, key_first, key_second, key_drop, key_base, key_place = jax.random.split(block_key, 6)
        shuffled = jax.random.permutation(key_order, TOK_E)
        is_hot = shuffled < CAP
        first_draw = jax.random.randint(key_first, (TOK_E,), 0, EXPERTS)
        second_draw = jax.random.randint(key_second, (TOK_E,), 0, EXPERTS)
        chosen = preference[jnp.minimum(first_draw, second_draw)]
        chosen = jnp.where(is_hot, hot_expert, chosen)
        one_hot = (chosen[:, None] == jnp.arange(EXPERTS)[None, :]).astype(jnp.int32)
        position = jnp.sum((jnp.cumsum(one_hot, axis=0) - one_hot) * one_hot, axis=1)
        dropped = jax.random.randint(key_drop, (TOK_E,), 0, 8) == 0
        kept_pick = is_hot | (chosen != hot_expert) & (position < CAP) & jnp.logical_not(dropped)
        offset_base = jax.random.randint(key_base, (TOK_E,), 0, spread)
        outside = EXPERTS + offset_base[:, None] + spread * jnp.arange(TOPK)[None, :]
        place_index = jax.random.randint(key_place, (TOK_E,), 0, TOPK)
        at_place = jnp.arange(TOPK)[None, :] == place_index[:, None]
        return jnp.where(at_place & kept_pick[:, None], chosen[:, None], outside).astype(jnp.int32)
    block_keys = jax.random.split(key_blocks, TOKENS // TOK_E)
    return jax.vmap(one_block)(block_keys).reshape(TOKENS, TOPK)


def block_levels(own_key, extent, cuts, low, high):
    def one(axis_at, parts):
        draws = jax.random.uniform(jax.random.fold_in(jax.random.fold_in(own_key, 6), axis_at), (parts,), jnp.float32, low / len(cuts), high / len(cuts))
        return jnp.repeat(jnp.exp(draws), extent[axis_at] // parts).reshape((-1,) + (1,) * (len(extent) - axis_at - 1))

    gain = one(*cuts[0])
    for cut in cuts[1:]:
        gain = gain * one(*cut)
    return gain


def scatter_about(stream_key, extent, deviation, limit, cuts=(), held_as=jnp.bfloat16):
    gain = block_levels(stream_key, extent, cuts, -0.22, 0.18) if cuts else 1.0
    result = jax.random.normal(stream_key, extent, jnp.float32) * deviation * gain
    return jnp.minimum(jnp.maximum(result, -limit), limit).astype(held_as)


def setup_inputs(seed: int = 0) -> dict:
    seeds = jax.random.split(jax.random.key(seed), 8)
    return {
        "tokens": scatter_about(seeds[0], (TOKENS, D), 1.0, 6.0, ((0, 8), (1, 4))),
        "grad_out": scatter_about(seeds[1], (TOKENS, D), 0.3, 1.796875, ((0, 8), (1, 4))),
        "expert_ids": draw_expert_ids(jax.random.fold_in(seeds[7], 71), 0),
        "gates": jnp.clip(jnp.exp(math.log(2.5) - 2.3025851 * jax.random.uniform(seeds[3], (TOKENS, TOPK), jnp.float32) ** block_levels(seeds[3], (TOKENS, TOPK), ((0, 8),), -0.2, 0.2)), 0.25, 2.5),
        "w_gate": scatter_about(seeds[4], (EXPERTS, D, HID), D ** -0.5, 0.09375, ((0, 8), (1, 4))),
        "w_up": scatter_about(seeds[5], (EXPERTS, D, HID), D ** -0.5, 0.09375, ((0, 8), (1, 4))),
        "w_down": scatter_about(seeds[6], (EXPERTS, HID, D), HID ** -0.5, 0.1875, ((0, 8), (2, 4))),
    }


def swish_gate(value):
    return value * jax.nn.sigmoid(value)


def swish_slope(value):
    logistic = jax.nn.sigmoid(value)
    return logistic * (1.0 + value * (1.0 - logistic))


def grouped_rounded_sum(partial_terms):
    rounded = lax.optimization_barrier(partial_terms.astype(jnp.bfloat16))
    return jnp.sum(rounded.astype(jnp.float32), axis=0)


def reference(tokens, grad_out, expert_ids, gates, w_gate, w_up, w_down):
    in_window = expert_ids < EXPERTS
    routed = jnp.any(in_window, axis=1)
    chosen = jnp.sum(jnp.where(in_window, expert_ids, 0), axis=1).astype(jnp.int32)
    weight_tok = jnp.sum(jnp.where(in_window, gates, jnp.zeros_like(gates)), axis=1)
    one_hot = ((chosen[:, None] == jnp.arange(EXPERTS, dtype=jnp.int32)[None, :]) & routed[:, None]).astype(jnp.int32)
    one_hot = one_hot.reshape(TOKENS // TOK_E, TOK_E, EXPERTS)
    position = jnp.sum((jnp.cumsum(one_hot, axis=1) - one_hot) * one_hot, axis=2).reshape(TOKENS).astype(jnp.int32)
    slot_index = (jnp.arange(TOKENS, dtype=jnp.int32) // TOK_E) * CAP + position
    flat_index = jnp.where(routed, chosen * SLOTS + slot_index, EXPERTS * SLOTS).astype(jnp.int32)
    row_table = jnp.full((EXPERTS * SLOTS,), TOKENS, jnp.int32)
    row_table = row_table.at[flat_index].set(jnp.arange(TOKENS, dtype=jnp.int32), mode="drop").reshape(EXPERTS, SLOTS)
    scaled = (weight_tok[:, None] * grad_out.astype(jnp.float32)).astype(jnp.bfloat16)

    def per_expert(pieces):
        table_rows, gate_mat, up_mat, down_mat = pieces
        expert_rows = jnp.take(tokens, table_rows, axis=0, mode="fill", fill_value=0)
        grad_rows_in = jnp.take(scaled, table_rows, axis=0, mode="fill", fill_value=0)
        grouped_rows = expert_rows.reshape(SLOTS, N_DP, FEAT_DEV).astype(jnp.float32)
        gate_groups = gate_mat.reshape(N_DP, FEAT_DEV, HID).astype(jnp.float32)
        up_groups = up_mat.reshape(N_DP, FEAT_DEV, HID).astype(jnp.float32)
        gate_pre = grouped_rounded_sum(jnp.einsum("snf,nfh->nsh", grouped_rows, gate_groups))
        up_pre = grouped_rounded_sum(jnp.einsum("snf,nfh->nsh", grouped_rows, up_groups))
        activation = (swish_gate(gate_pre) * up_pre).astype(jnp.bfloat16)
        expert_out = jnp.dot(activation, down_mat, preferred_element_type=jnp.float32).astype(jnp.bfloat16)
        grad_down = jnp.dot(activation.T, grad_rows_in, preferred_element_type=jnp.float32).astype(jnp.bfloat16)
        grouped_grads = grad_rows_in.reshape(SLOTS, N_DP, FEAT_DEV).astype(jnp.float32)
        down_groups = down_mat.reshape(HID, N_DP, FEAT_DEV).astype(jnp.float32)
        grad_act = grouped_rounded_sum(jnp.einsum("snf,hnf->nsh", grouped_grads, down_groups))
        grad_gate_pre = (grad_act * up_pre * swish_slope(gate_pre)).astype(jnp.bfloat16)
        grad_up_pre = (grad_act * swish_gate(gate_pre)).astype(jnp.bfloat16)
        grad_gate = jnp.dot(expert_rows.T, grad_gate_pre, preferred_element_type=jnp.float32).astype(jnp.bfloat16)
        grad_up = jnp.dot(expert_rows.T, grad_up_pre, preferred_element_type=jnp.float32).astype(jnp.bfloat16)
        row_grad = (jnp.dot(grad_gate_pre, gate_mat.T, preferred_element_type=jnp.float32)
                    + jnp.dot(grad_up_pre, up_mat.T, preferred_element_type=jnp.float32)).astype(jnp.bfloat16)
        return expert_out, row_grad, grad_gate, grad_up, grad_down

    expert_out, row_grad, grad_gate, grad_up, grad_down = lax.map(per_expert, (row_table, w_gate, w_up, w_down))
    token_out = jnp.take(expert_out.reshape(EXPERTS * SLOTS, D), flat_index, axis=0, mode="fill", fill_value=0)
    mixed = (weight_tok[:, None] * token_out.astype(jnp.float32)).astype(jnp.bfloat16)
    grad_tokens = jnp.take(row_grad.reshape(EXPERTS * SLOTS, D), flat_index, axis=0, mode="fill", fill_value=0)
    return (mixed, grad_tokens, grad_gate, grad_up, grad_down)
```

```python
import functools

import jax
import jax.numpy as jnp
from jax import lax
from jax.experimental import pallas as pl
from jax.experimental.pallas import tpu as pltpu
from jax.sharding import PartitionSpec as P

F32 = jnp.float32
BF16 = jnp.bfloat16
VMEM_LIMIT = 24 * 1024 * 1024


def mm(left, right, dims):
    return lax.dot_general(left, right, (dims, ((), ())), preferred_element_type=F32)


def call(kernel, out_shape, flops=0, moved=0, **kwargs):
    return pl.pallas_call(
        kernel,
        out_shape=out_shape,
        cost_estimate=pl.CostEstimate(flops=flops, bytes_accessed=moved, transcendentals=0),
        compiler_params=pltpu.CompilerParams(vmem_limit_bytes=VMEM_LIMIT),
        **kwargs,
    )


def route_kernel(experts, capacity, ids_ref, gates_ref, tokens_ref, pick_ref, weight_ref, send_ref):
    ids = ids_ref[...]
    tok_rows = ids.shape[1]
    slots = pick_ref.shape[0]
    inside = ids < experts
    routed = jnp.max(inside.astype(jnp.int32), axis=0, keepdims=True)
    chosen = jnp.sum(jnp.where(inside, ids, 0), axis=0, keepdims=True)
    weight = jnp.sum(jnp.where(inside, gates_ref[...], 0.0), axis=0, keepdims=True)
    key = jnp.where(routed > 0, chosen, experts)
    hot = lax.broadcasted_iota(jnp.int32, (experts, tok_rows), 0) == key
    earlier = lax.broadcasted_iota(jnp.int32, (tok_rows, tok_rows), 0) < lax.broadcasted_iota(
        jnp.int32, (tok_rows, tok_rows), 1
    )
    before = mm(hot.astype(F32).astype(BF16), earlier.astype(F32).astype(BF16), ((1,), (0,)))
    position = jnp.sum(jnp.where(hot, before, 0.0), axis=0, keepdims=True).astype(jnp.int32)
    slot = jnp.where(routed > 0, chosen * capacity + position, slots)
    pick = lax.broadcasted_iota(jnp.int32, (slots, tok_rows), 0) == slot
    weight_ref[...] = jnp.sum(jnp.where(pick, weight, 0.0), axis=1, keepdims=True)
    pick = pick.astype(F32).astype(BF16)
    pick_ref[...] = pick
    send_ref[...] = mm(pick, tokens_ref[...], ((1,), (0,))).astype(BF16)


def gather_scaled_kernel(pick_ref, weight_ref, grad_ref, send_ref):
    rows = mm(pick_ref[...], grad_ref[...], ((1,), (0,)))
    send_ref[...] = (weight_ref[...] * rows).astype(BF16)


def gate_up_kernel(rows_ref, gate_ref, up_ref, out_ref):
    rows = rows_ref[...]
    dp, _, chunk, cols = out_ref.shape
    for at, mat in enumerate((gate_ref, up_ref)):
        part = mm(rows, mat[...], ((1,), (0,))).astype(BF16)
        out_ref[:, at] = part.reshape(dp, chunk, cols)


def grad_act_kernel(grads_ref, down_ref, out_ref):
    dp, chunk, cols = out_ref.shape
    part = mm(grads_ref[...], down_ref[...], ((1,), (1,))).astype(BF16)
    out_ref[...] = part.reshape(dp, chunk, cols)


def group_sum(ref, *at):
    total = ref[(0, *at)].astype(F32)
    for group in range(1, ref.shape[0]):
        total = total + ref[(group, *at)].astype(F32)
    return total


def logistic(value):
    return 1.0 / (1.0 + jnp.exp(-value))


def act_kernel(sums_ref, act_ref):
    gate = group_sum(sums_ref, 0)
    up = group_sum(sums_ref, 1)
    act_ref[...] = (gate * logistic(gate) * up).astype(BF16)


def grad_pre_kernel(sums_ref, grad_ref, out_ref):
    gate = group_sum(sums_ref, 0)
    up = group_sum(sums_ref, 1)
    grad = group_sum(grad_ref)
    soft = logistic(gate)
    out_ref[0] = (grad * up * (soft * (1.0 + gate * (1.0 - soft)))).astype(BF16)
    out_ref[1] = (grad * (gate * soft)).astype(BF16)


def expert_out_kernel(act_ref, down_ref, out_ref):
    dp, chunk, hidden = act_ref.shape
    act = act_ref[...].reshape(dp * chunk, hidden)
    out_ref[...] = mm(act, down_ref[...], ((1,), (0,))).astype(BF16)


def row_grad_kernel(pre_ref, gate_ref, up_ref, out_ref):
    dp, _, chunk, hidden = pre_ref.shape
    gate_pre = pre_ref[:, 0].reshape(dp * chunk, hidden)
    up_pre = pre_ref[:, 1].reshape(dp * chunk, hidden)
    total = mm(gate_pre, gate_ref[...], ((1,), (1,))) + mm(up_pre, up_ref[...], ((1,), (1,)))
    out_ref[...] = total.astype(BF16)


def scatter_scaled_kernel(pick_ref, weight_ref, back_ref, out_ref):
    scaled = (weight_ref[...] * back_ref[...].astype(F32)).astype(BF16)
    out_ref[...] = mm(pick_ref[...], scaled, ((0,), (0,))).astype(BF16)


def scatter_kernel(pick_ref, back_ref, out_ref):
    out_ref[...] = mm(pick_ref[...], back_ref[...], ((0,), (0,))).astype(BF16)


def exchange(value, axis):
    return lax.all_to_all(value, axis, split_axis=0, concat_axis=0, tiled=True)


def spread(value, axis):
    size = lax.axis_size(axis)
    return exchange(jnp.broadcast_to(value[None], (size, *value.shape)), axis)


def body(tokens, grad_out, expert_ids, gates, w_gate, w_up, w_down):
    experts = lax.axis_size("expert")
    dp = lax.axis_size("dp")
    tok_rows, features = tokens.shape
    capacity = tok_rows // 16
    slots = experts * capacity
    hidden = w_gate.shape[2]
    chunk = slots // dp
    gate_mat, up_mat, down_mat = w_gate[0], w_up[0], w_down[0]
    shape = jax.ShapeDtypeStruct
    product = 2 * slots * features * hidden
    weights = 2 * features * hidden

    pick, weight, send_tokens = call(
        functools.partial(route_kernel, experts, capacity),
        (
            shape((slots, tok_rows), BF16),
            shape((slots, 1), F32),
            shape((slots, features), BF16),
        ),
        2 * slots * tok_rows * features,
        4 * tok_rows * features,
    )(expert_ids.T, gates.T, tokens)
    rows = exchange(send_tokens.reshape(experts, capacity, features), "expert")
    rows = rows.reshape(slots, features)
    send_grads = call(
        gather_scaled_kernel,
        shape((slots, features), BF16),
        2 * slots * tok_rows * features,
        4 * tok_rows * features,
    )(pick, weight, grad_out)
    grads = exchange(send_grads.reshape(experts, capacity, features), "expert")
    grads = grads.reshape(slots, features)

    tiles = 4 if hidden % 512 == 0 else 1
    cols = hidden // tiles
    part_pre = call(
        gate_up_kernel,
        shape((dp, 2, chunk, hidden), BF16),
        2 * product,
        2 * weights,
        grid=(tiles,),
        in_specs=[
            pl.BlockSpec((slots, features), lambda i: (0, 0)),
            pl.BlockSpec((features, cols), lambda i: (0, i)),
            pl.BlockSpec((features, cols), lambda i: (0, i)),
        ],
        out_specs=pl.BlockSpec((dp, 2, chunk, cols), lambda i: (0, 0, 0, i)),
    )(rows, gate_mat, up_mat)
    sums = exchange(part_pre, "dp")
    part_grad = call(
        grad_act_kernel,
        shape((dp, chunk, hidden), BF16),
        product,
        weights,
        grid=(tiles,),
        in_specs=[
            pl.BlockSpec((slots, features), lambda i: (0, 0)),
            pl.BlockSpec((cols, features), lambda i: (i, 0)),
        ],
        out_specs=pl.BlockSpec((dp, chunk, cols), lambda i: (0, 0, i)),
    )(grads, down_mat)
    act_mine = call(act_kernel, shape((chunk, hidden), BF16), 0, 4 * dp * chunk * hidden)(sums)
    act = spread(act_mine, "dp")
    grad_sums = exchange(part_grad, "dp")
    expert_out = call(
        expert_out_kernel, shape((slots, features), BF16), product, weights
    )(act, down_mat)
    back_out = exchange(expert_out.reshape(experts, capacity, features), "expert")
    pre_mine = call(
        grad_pre_kernel, shape((2, chunk, hidden), BF16), 0, 6 * dp * chunk * hidden
    )(sums, grad_sums)
    pre = spread(pre_mine, "dp")
    row_grad = call(
        row_grad_kernel, shape((slots, features), BF16), 2 * product, 2 * weights
    )(pre, gate_mat, up_mat)
    back_grad = exchange(row_grad.reshape(experts, capacity, features), "expert")

    act_rows = act.reshape(slots, hidden)
    grad_down = mm(act_rows, grads, ((0,), (0,))).astype(BF16)
    grad_gate = mm(rows, pre[:, 0].reshape(slots, hidden), ((0,), (0,))).astype(BF16)
    grad_up = mm(rows, pre[:, 1].reshape(slots, hidden), ((0,), (0,))).astype(BF16)

    full = shape((tok_rows, features), BF16)
    mixed = call(
        scatter_scaled_kernel, full, 2 * slots * tok_rows * features, 4 * tok_rows * features
    )(pick, weight, back_out.reshape(slots, features))
    grad_tokens = call(
        scatter_kernel, full, 2 * slots * tok_rows * features, 4 * tok_rows * features
    )(pick, back_grad.reshape(slots, features))
    return (mixed, grad_tokens, grad_gate[None], grad_up[None], grad_down[None])


def solution(mesh):
    placed = (
        P("expert", "dp"),
        P("expert", "dp"),
        P("expert", None),
        P("expert", None),
        P("expert", "dp", None),
        P("expert", "dp", None),
        P("expert", None, "dp"),
    )
    return jax.shard_map(
        body,
        mesh=mesh,
        in_specs=placed,
        out_specs=(
            P("expert", "dp"),
            P("expert", "dp"),
            P("expert", "dp", None),
            P("expert", "dp", None),
            P("expert", None, "dp"),
        ),
        check_vma=False,
    )
```

```python
import functools

import jax
import jax.numpy as jnp
from jax import lax
from jax.experimental import pallas as pl
from jax.experimental.pallas import tpu as pltpu
from jax.sharding import PartitionSpec as P

F32 = jnp.float32
BF16 = jnp.bfloat16
VMEM_LIMIT = 24 * 1024 * 1024


def mm(left, right, dims):
    return lax.dot_general(left, right, (dims, ((), ())), preferred_element_type=F32)


def call(kernel, out_shape, flops=0, moved=0, **kwargs):
    return pl.pallas_call(
        kernel,
        out_shape=out_shape,
        cost_estimate=pl.CostEstimate(flops=flops, bytes_accessed=moved, transcendentals=0),
        compiler_params=pltpu.CompilerParams(vmem_limit_bytes=VMEM_LIMIT),
        **kwargs,
    )


def route_kernel(experts, capacity, ids_ref, gates_ref, tokens_ref, pick_ref, weight_ref, send_ref):
    ids = ids_ref[...]
    tok_rows = ids.shape[1]
    slots = pick_ref.shape[0]
    inside = ids < experts
    routed = jnp.max(inside.astype(jnp.int32), axis=0, keepdims=True)
    chosen = jnp.sum(jnp.where(inside, ids, 0), axis=0, keepdims=True)
    weight = jnp.sum(jnp.where(inside, gates_ref[...], 0.0), axis=0, keepdims=True)
    key = jnp.where(routed > 0, chosen, experts)
    hot = lax.broadcasted_iota(jnp.int32, (experts, tok_rows), 0) == key
    earlier = lax.broadcasted_iota(jnp.int32, (tok_rows, tok_rows), 0) < lax.broadcasted_iota(
        jnp.int32, (tok_rows, tok_rows), 1
    )
    before = mm(hot.astype(F32).astype(BF16), earlier.astype(F32).astype(BF16), ((1,), (0,)))
    position = jnp.sum(jnp.where(hot, before, 0.0), axis=0, keepdims=True).astype(jnp.int32)
    slot = jnp.where(routed > 0, chosen * capacity + position, slots)
    pick = lax.broadcasted_iota(jnp.int32, (slots, tok_rows), 0) == slot
    weight_ref[...] = jnp.sum(jnp.where(pick, weight, 0.0), axis=1, keepdims=True)
    pick = pick.astype(F32).astype(BF16)
    pick_ref[...] = pick
    send_ref[...] = mm(pick, tokens_ref[...], ((1,), (0,))).astype(BF16)


def gather_scaled_kernel(pick_ref, weight_ref, grad_ref, send_ref):
    rows = mm(pick_ref[...], grad_ref[...], ((1,), (0,)))
    send_ref[...] = (weight_ref[...] * rows).astype(BF16)


def local_order(ref, chunks):
    mine = lax.axis_index("dp")
    chunk = ref.shape[0] // chunks
    return [
        ref[pl.ds(pl.multiple_of((mine ^ k) * chunk, chunk), chunk), :] for k in range(chunks)
    ]


def gate_up_kernel(dp, rows_ref, gate_ref, up_ref, local_ref, *out_refs):
    rows = jnp.concatenate(local_order(rows_ref, dp), axis=0)
    local_ref[...] = rows
    chunk = rows.shape[0] // dp
    for at, mat in enumerate((gate_ref, up_ref)):
        part = mm(rows, mat[...], ((1,), (0,))).astype(BF16)
        for k, out_ref in enumerate(out_refs):
            out_ref[at] = part[k * chunk : (k + 1) * chunk]


def grad_act_kernel(dp, grads_ref, down_ref, local_ref, *out_refs):
    rows = jnp.concatenate(local_order(grads_ref, dp), axis=0)
    local_ref[...] = rows
    chunk = rows.shape[0] // dp
    part = mm(rows, down_ref[...], ((1,), (1,))).astype(BF16)
    for k, out_ref in enumerate(out_refs):
        out_ref[...] = part[k * chunk : (k + 1) * chunk]


def group_sum(refs, *at):
    total = refs[0][at].astype(F32)
    for ref in refs[1:]:
        total = total + ref[at].astype(F32)
    return total


def logistic(value):
    return 1.0 / (1.0 + jnp.exp(-value))


def act_kernel(dp, *refs):
    gate = group_sum(refs[:dp], 0)
    up = group_sum(refs[:dp], 1)
    refs[dp][...] = (gate * logistic(gate) * up).astype(BF16)


def grad_pre_kernel(dp, *refs):
    gate = group_sum(refs[:dp], 0)
    up = group_sum(refs[:dp], 1)
    grad = group_sum(refs[dp : 2 * dp], Ellipsis)
    out_ref = refs[2 * dp]
    soft = logistic(gate)
    out_ref[0] = (grad * up * (soft * (1.0 + gate * (1.0 - soft)))).astype(BF16)
    out_ref[1] = (grad * (gate * soft)).astype(BF16)


def store_natural(out_ref, rows, dp):
    mine = lax.axis_index("dp")
    chunk = rows.shape[0] // dp
    for k in range(dp):
        out_ref[pl.ds(pl.multiple_of((mine ^ k) * chunk, chunk), chunk), :] = rows[
            k * chunk : (k + 1) * chunk
        ]


def expert_out_kernel(dp, *refs):
    down_ref, act_ref, out_ref = refs[dp:]
    act = jnp.concatenate([ref[...] for ref in refs[:dp]], axis=0)
    act_ref[...] = act
    store_natural(out_ref, mm(act, down_ref[...], ((1,), (0,))).astype(BF16), dp)


def row_grad_kernel(dp, *refs):
    gate_ref, up_ref, gate_pre_ref, up_pre_ref, out_ref = refs[dp:]
    gate_pre = jnp.concatenate([ref[0] for ref in refs[:dp]], axis=0)
    up_pre = jnp.concatenate([ref[1] for ref in refs[:dp]], axis=0)
    gate_pre_ref[...] = gate_pre
    up_pre_ref[...] = up_pre
    total = mm(gate_pre, gate_ref[...], ((1,), (1,))) + mm(up_pre, up_ref[...], ((1,), (1,)))
    store_natural(out_ref, total.astype(BF16), dp)


def scatter_scaled_kernel(pick_ref, weight_ref, back_ref, out_ref):
    scaled = (weight_ref[...] * back_ref[...].astype(F32)).astype(BF16)
    out_ref[...] = mm(pick_ref[...], scaled, ((0,), (0,))).astype(BF16)


def scatter_kernel(pick_ref, back_ref, out_ref):
    out_ref[...] = mm(pick_ref[...], back_ref[...], ((0,), (0,))).astype(BF16)


def exchange(value, axis):
    return lax.all_to_all(value, axis, split_axis=0, concat_axis=0, tiled=True)


def trade(values):
    size = lax.axis_size("dp")
    return [values[0]] + [
        lax.ppermute(values[k], "dp", [(i, i ^ k) for i in range(size)]) for k in range(1, size)
    ]


def body(tokens, grad_out, expert_ids, gates, w_gate, w_up, w_down):
    experts = lax.axis_size("expert")
    dp = lax.axis_size("dp")
    tok_rows, features = tokens.shape
    capacity = tok_rows // 16
    slots = experts * capacity
    hidden = w_gate.shape[2]
    chunk = slots // dp
    gate_mat, up_mat, down_mat = w_gate[0], w_up[0], w_down[0]
    shape = jax.ShapeDtypeStruct
    product = 2 * slots * features * hidden
    weights = 2 * features * hidden

    pick, weight, send_tokens = call(
        functools.partial(route_kernel, experts, capacity),
        (
            shape((slots, tok_rows), BF16),
            shape((slots, 1), F32),
            shape((slots, features), BF16),
        ),
        2 * slots * tok_rows * features,
        4 * tok_rows * features,
    )(expert_ids.T, gates.T, tokens)
    rows = exchange(send_tokens.reshape(experts, capacity, features), "expert")
    rows = rows.reshape(slots, features)
    send_grads = call(
        gather_scaled_kernel,
        shape((slots, features), BF16),
        2 * slots * tok_rows * features,
        4 * tok_rows * features,
    )(pick, weight, grad_out)
    grads = exchange(send_grads.reshape(experts, capacity, features), "expert")
    grads = grads.reshape(slots, features)

    sized = shape((slots, features), BF16)
    rows, *part_pre = call(
        functools.partial(gate_up_kernel, dp),
        (sized, *[shape((2, chunk, hidden), BF16)] * dp),
        2 * product,
        2 * weights,
    )(rows, gate_mat, up_mat)
    sums = trade(part_pre)
    grads, *part_grad = call(
        functools.partial(grad_act_kernel, dp),
        (sized, *[shape((chunk, hidden), BF16)] * dp),
        product,
        weights,
    )(grads, down_mat)
    act_mine = call(
        functools.partial(act_kernel, dp),
        shape((chunk, hidden), BF16),
        0,
        4 * dp * chunk * hidden,
    )(*sums)
    acts = trade([act_mine] * dp)
    grad_sums = trade(part_grad)
    act, expert_out = call(
        functools.partial(expert_out_kernel, dp),
        (shape((slots, hidden), BF16), sized),
        product,
        weights,
    )(*acts, down_mat)
    back_out = exchange(expert_out.reshape(experts, capacity, features), "expert")
    pre_mine = call(
        functools.partial(grad_pre_kernel, dp),
        shape((2, chunk, hidden), BF16),
        0,
        6 * dp * chunk * hidden,
    )(*sums, *grad_sums)
    pre = trade([pre_mine] * dp)
    gate_pre, up_pre, row_grad = call(
        functools.partial(row_grad_kernel, dp),
        (*[shape((slots, hidden), BF16)] * 2, sized),
        2 * product,
        2 * weights,
    )(*pre, gate_mat, up_mat)
    back_grad = exchange(row_grad.reshape(experts, capacity, features), "expert")

    grad_down = mm(act, grads, ((0,), (0,))).astype(BF16)
    grad_gate = mm(rows, gate_pre, ((0,), (0,))).astype(BF16)
    grad_up = mm(rows, up_pre, ((0,), (0,))).astype(BF16)

    full = shape((tok_rows, features), BF16)
    mixed = call(
        scatter_scaled_kernel, full, 2 * slots * tok_rows * features, 4 * tok_rows * features
    )(pick, weight, back_out.reshape(slots, features))
    grad_tokens = call(
        scatter_kernel, full, 2 * slots * tok_rows * features, 4 * tok_rows * features
    )(pick, back_grad.reshape(slots, features))
    return (mixed, grad_tokens, grad_gate[None], grad_up[None], grad_down[None])


def solution(mesh):
    placed = (
        P("expert", "dp"),
        P("expert", "dp"),
        P("expert", None),
        P("expert", None),
        P("expert", "dp", None),
        P("expert", "dp", None),
        P("expert", None, "dp"),
    )
    return jax.shard_map(
        body,
        mesh=mesh,
        in_specs=placed,
        out_specs=(
            P("expert", "dp"),
            P("expert", "dp"),
            P("expert", "dp", None),
            P("expert", "dp", None),
            P("expert", None, "dp"),
        ),
        check_vma=False,
    )
```

```python
import functools

import jax
import jax.numpy as jnp
from jax import lax
from jax.experimental import pallas as pl
from jax.experimental.pallas import tpu as pltpu
from jax.sharding import PartitionSpec as P

F32 = jnp.float32
BF16 = jnp.bfloat16
VMEM_LIMIT = 24 * 1024 * 1024


def mm(left, right, dims):
    return lax.dot_general(left, right, (dims, ((), ())), preferred_element_type=F32)


def call(kernel, out_shape, flops=0, moved=0, **kwargs):
    return pl.pallas_call(
        kernel,
        out_shape=out_shape,
        cost_estimate=pl.CostEstimate(flops=flops, bytes_accessed=moved, transcendentals=0),
        compiler_params=pltpu.CompilerParams(vmem_limit_bytes=VMEM_LIMIT),
        **kwargs,
    )


def split_rows(refs, value):
    rows = value.shape[0] // len(refs)
    for k, ref in enumerate(refs):
        ref[...] = value[k * rows : (k + 1) * rows]


def join_rows(refs):
    return jnp.concatenate([ref[...] for ref in refs], axis=0)


def route_kernel(experts, ids_ref, gates_ref, tokens_ref, pick_ref, weight_ref, *send_refs):
    ids = ids_ref[...]
    tok_rows = ids.shape[1]
    slots = pick_ref.shape[0]
    inside = ids < experts
    routed = jnp.max(inside.astype(jnp.int32), axis=0, keepdims=True)
    chosen = jnp.sum(jnp.where(inside, ids, 0), axis=0, keepdims=True)
    weight = jnp.sum(jnp.where(inside, gates_ref[...], 0.0), axis=0, keepdims=True)
    key = jnp.where(routed > 0, chosen ^ lax.axis_index("expert"), experts)
    hot = lax.broadcasted_iota(jnp.int32, (experts, tok_rows), 0) == key
    earlier = lax.broadcasted_iota(jnp.int32, (tok_rows, tok_rows), 0) < lax.broadcasted_iota(
        jnp.int32, (tok_rows, tok_rows), 1
    )
    before = mm(hot.astype(F32).astype(BF16), earlier.astype(F32).astype(BF16), ((1,), (0,)))
    position = jnp.sum(jnp.where(hot, before, 0.0), axis=0, keepdims=True).astype(jnp.int32)
    slot = jnp.where(routed > 0, key * (slots // experts) + position, slots)
    pick = lax.broadcasted_iota(jnp.int32, (slots, tok_rows), 0) == slot
    weight_ref[...] = jnp.sum(jnp.where(pick, weight, 0.0), axis=1, keepdims=True)
    pick = pick.astype(F32).astype(BF16)
    pick_ref[...] = pick
    split_rows(send_refs, mm(pick, tokens_ref[...], ((1,), (0,))).astype(BF16))


def gather_scaled_kernel(pick_ref, weight_ref, grad_ref, *send_refs):
    rows = mm(pick_ref[...], grad_ref[...], ((1,), (0,)))
    split_rows(send_refs, (weight_ref[...] * rows).astype(BF16))


def chunk_rows(rows, dp, k):
    chunk = rows // dp
    mine = lax.axis_index("dp")
    return pl.ds(pl.multiple_of((mine ^ k) * chunk, chunk), chunk)


def local_order(refs, scratch, dp):
    scratch[...] = join_rows(refs)
    rows = scratch.shape[0]
    return jnp.concatenate([scratch[chunk_rows(rows, dp, k), :] for k in range(dp)], axis=0)


def gate_up_kernel(dp, experts, *refs):
    gate_ref, up_ref, local_ref = refs[experts : experts + 3]
    out_refs = refs[experts + 3 : experts + 3 + dp]
    rows = local_order(refs[:experts], refs[-1], dp)
    local_ref[...] = rows
    chunk = rows.shape[0] // dp
    for at, mat in enumerate((gate_ref, up_ref)):
        part = mm(rows, mat[...], ((1,), (0,))).astype(BF16)
        for k, out_ref in enumerate(out_refs):
            out_ref[at] = part[k * chunk : (k + 1) * chunk]


def grad_act_kernel(dp, experts, *refs):
    down_ref, local_ref = refs[experts : experts + 2]
    out_refs = refs[experts + 2 : experts + 2 + dp]
    rows = local_order(refs[:experts], refs[-1], dp)
    local_ref[...] = rows
    split_rows(out_refs, mm(rows, down_ref[...], ((1,), (1,))).astype(BF16))


def group_sum(refs, *at):
    total = refs[0][at].astype(F32)
    for ref in refs[1:]:
        total = total + ref[at].astype(F32)
    return total


def logistic(value):
    return 1.0 / (1.0 + jnp.exp(-value))


def act_kernel(dp, *refs):
    gate = group_sum(refs[:dp], 0)
    up = group_sum(refs[:dp], 1)
    refs[dp][...] = (gate * logistic(gate) * up).astype(BF16)


def grad_pre_kernel(dp, *refs):
    gate = group_sum(refs[:dp], 0)
    up = group_sum(refs[:dp], 1)
    grad = group_sum(refs[dp : 2 * dp], Ellipsis)
    out_ref = refs[2 * dp]
    soft = logistic(gate)
    out_ref[0] = (grad * up * (soft * (1.0 + gate * (1.0 - soft)))).astype(BF16)
    out_ref[1] = (grad * (gate * soft)).astype(BF16)


def send_back(out_refs, scratch, rows, dp):
    chunk = rows.shape[0] // dp
    for k in range(dp):
        scratch[chunk_rows(rows.shape[0], dp, k), :] = rows[k * chunk : (k + 1) * chunk]
    split_rows(out_refs, scratch[...])


def expert_out_kernel(dp, *refs):
    down_ref, act_ref, *out_refs, scratch = refs[dp:]
    act = join_rows(refs[:dp])
    act_ref[...] = act
    send_back(out_refs, scratch, mm(act, down_ref[...], ((1,), (0,))).astype(BF16), dp)


def row_grad_kernel(dp, *refs):
    gate_ref, up_ref, gate_pre_ref, up_pre_ref, *out_refs, scratch = refs[dp:]
    gate_pre = jnp.concatenate([ref[0] for ref in refs[:dp]], axis=0)
    up_pre = jnp.concatenate([ref[1] for ref in refs[:dp]], axis=0)
    gate_pre_ref[...] = gate_pre
    up_pre_ref[...] = up_pre
    total = mm(gate_pre, gate_ref[...], ((1,), (1,))) + mm(up_pre, up_ref[...], ((1,), (1,)))
    send_back(out_refs, scratch, total.astype(BF16), dp)


def scatter_scaled_kernel(pick_ref, weight_ref, *refs):
    scaled = (weight_ref[...] * join_rows(refs[:-1]).astype(F32)).astype(BF16)
    refs[-1][...] = mm(pick_ref[...], scaled, ((0,), (0,))).astype(BF16)


def scatter_kernel(pick_ref, *refs):
    refs[-1][...] = mm(pick_ref[...], join_rows(refs[:-1]), ((0,), (0,))).astype(BF16)


def trade(values, axis):
    size = lax.axis_size(axis)
    return [values[0]] + [
        lax.ppermute(values[k], axis, [(i, i ^ k) for i in range(size)]) for k in range(1, size)
    ]


def body(tokens, grad_out, expert_ids, gates, w_gate, w_up, w_down):
    experts = lax.axis_size("expert")
    dp = lax.axis_size("dp")
    tok_rows, features = tokens.shape
    capacity = tok_rows // 16
    slots = experts * capacity
    hidden = w_gate.shape[2]
    chunk = slots // dp
    gate_mat, up_mat, down_mat = w_gate[0], w_up[0], w_down[0]
    shape = jax.ShapeDtypeStruct
    product = 2 * slots * features * hidden
    weights = 2 * features * hidden

    blocks = [shape((capacity, features), BF16)] * experts
    sized = shape((slots, features), BF16)
    wide = shape((slots, hidden), BF16)
    in_order = [pltpu.VMEM((slots, features), BF16)]

    pick, weight, *send_tokens = call(
        functools.partial(route_kernel, experts),
        (shape((slots, tok_rows), BF16), shape((slots, 1), F32), *blocks),
        2 * slots * tok_rows * features,
        4 * tok_rows * features,
    )(expert_ids.T, gates.T, tokens)
    rows = trade(send_tokens, "expert")
    send_grads = call(
        gather_scaled_kernel,
        blocks,
        2 * slots * tok_rows * features,
        4 * tok_rows * features,
    )(pick, weight, grad_out)
    grads = trade(send_grads, "expert")

    rows, *part_pre = call(
        functools.partial(gate_up_kernel, dp, experts),
        (sized, *[shape((2, chunk, hidden), BF16)] * dp),
        2 * product,
        2 * weights,
        scratch_shapes=in_order,
    )(*rows, gate_mat, up_mat)
    sums = trade(part_pre, "dp")
    grads, *part_grad = call(
        functools.partial(grad_act_kernel, dp, experts),
        (sized, *[shape((chunk, hidden), BF16)] * dp),
        product,
        weights,
        scratch_shapes=in_order,
    )(*grads, down_mat)
    grad_sums = trade(part_grad, "dp")
    sums, part_grad = lax.optimization_barrier((sums, part_grad))
    act_mine = call(
        functools.partial(act_kernel, dp),
        shape((chunk, hidden), BF16),
        0,
        4 * dp * chunk * hidden,
    )(*sums)
    acts = trade([act_mine] * dp, "dp")
    pre_mine = call(
        functools.partial(grad_pre_kernel, dp),
        shape((2, chunk, hidden), BF16),
        0,
        6 * dp * chunk * hidden,
    )(*sums, *grad_sums)
    pre = trade([pre_mine] * dp, "dp")
    act, *expert_out = call(
        functools.partial(expert_out_kernel, dp),
        (wide, *blocks),
        product,
        weights,
        scratch_shapes=in_order,
    )(*acts, down_mat)
    back_out = trade(expert_out, "expert")
    gate_pre, up_pre, *row_grad = call(
        functools.partial(row_grad_kernel, dp),
        (wide, wide, *blocks),
        2 * product,
        2 * weights,
        scratch_shapes=in_order,
    )(*pre, gate_mat, up_mat)
    back_grad = trade(row_grad, "expert")

    grad_down = mm(act, grads, ((0,), (0,))).astype(BF16)
    grad_gate = mm(rows, gate_pre, ((0,), (0,))).astype(BF16)
    grad_up = mm(rows, up_pre, ((0,), (0,))).astype(BF16)

    full = shape((tok_rows, features), BF16)
    mixed = call(
        scatter_scaled_kernel, full, 2 * slots * tok_rows * features, 4 * tok_rows * features
    )(pick, weight, *back_out)
    grad_tokens = call(
        scatter_kernel, full, 2 * slots * tok_rows * features, 4 * tok_rows * features
    )(pick, *back_grad)
    return (mixed, grad_tokens, grad_gate[None], grad_up[None], grad_down[None])


def solution(mesh):
    placed = (
        P("expert", "dp"),
        P("expert", "dp"),
        P("expert", None),
        P("expert", None),
        P("expert", "dp", None),
        P("expert", "dp", None),
        P("expert", None, "dp"),
    )
    return jax.shard_map(
        body,
        mesh=mesh,
        in_specs=placed,
        out_specs=(
            P("expert", "dp"),
            P("expert", "dp"),
            P("expert", "dp", None),
            P("expert", "dp", None),
            P("expert", None, "dp"),
        ),
        check_vma=False,
    )
```

```python
import functools

import jax
import jax.numpy as jnp
from jax import lax
from jax.experimental import pallas as pl
from jax.experimental.pallas import tpu as pltpu
from jax.sharding import PartitionSpec as P

F32 = jnp.float32
BF16 = jnp.bfloat16
MIB = 1024 * 1024
VMEM_LIMIT = 24 * MIB
ROUTE_LIMIT = 59 * MIB


def mm(left, right, dims):
    return lax.dot_general(left, right, (dims, ((), ())), preferred_element_type=F32)


def call(kernel, out_shape, flops=0, moved=0, limit=VMEM_LIMIT, **kwargs):
    return pl.pallas_call(
        kernel,
        out_shape=out_shape,
        cost_estimate=pl.CostEstimate(flops=flops, bytes_accessed=moved, transcendentals=0),
        compiler_params=pltpu.CompilerParams(vmem_limit_bytes=limit),
        **kwargs,
    )


def split_rows(refs, value):
    rows = value.shape[0] // len(refs)
    for k, ref in enumerate(refs):
        ref[...] = value[k * rows : (k + 1) * rows]


def join_rows(refs):
    return jnp.concatenate([ref[...] for ref in refs], axis=0)


def split_cores(keep_ref, swap_ref, value, *at):
    half, rows = keep_ref.shape[-3:-1]
    for k in range(half):
        keep_ref[(*at, k)] = value[2 * k * rows : (2 * k + 1) * rows]
        swap_ref[(*at, k)] = value[(2 * k + 1) * rows : (2 * k + 2) * rows]


def route_kernel(
    experts, ids_ref, gates_ref, tokens_ref, grad_ref, pick_ref, weight_ref, keep_ref, swap_ref
):
    ids = ids_ref[...]
    tok_rows = ids.shape[1]
    slots = pick_ref.shape[0]
    inside = ids < experts
    routed = jnp.max(inside.astype(jnp.int32), axis=0, keepdims=True)
    chosen = jnp.sum(jnp.where(inside, ids, 0), axis=0, keepdims=True)
    weight = jnp.sum(jnp.where(inside, gates_ref[...], 0.0), axis=0, keepdims=True)
    key = jnp.where(routed > 0, chosen ^ lax.axis_index("expert"), experts)
    hot = lax.broadcasted_iota(jnp.int32, (experts, tok_rows), 0) == key
    earlier = lax.broadcasted_iota(jnp.int32, (tok_rows, tok_rows), 0) < lax.broadcasted_iota(
        jnp.int32, (tok_rows, tok_rows), 1
    )
    before = mm(hot.astype(F32).astype(BF16), earlier.astype(F32).astype(BF16), ((1,), (0,)))
    position = jnp.sum(jnp.where(hot, before, 0.0), axis=0, keepdims=True).astype(jnp.int32)
    slot = jnp.where(routed > 0, key * (slots // experts) + position, slots)
    pick = lax.broadcasted_iota(jnp.int32, (slots, tok_rows), 0) == slot
    slot_weight = jnp.sum(jnp.where(pick, weight, 0.0), axis=1, keepdims=True)
    weight_ref[...] = slot_weight
    pick = pick.astype(F32).astype(BF16)
    pick_ref[...] = pick
    rows = mm(pick, tokens_ref[...], ((1,), (0,))).astype(BF16)
    split_cores(keep_ref, swap_ref, rows, 0)
    rows = (slot_weight * mm(pick, grad_ref[...], ((1,), (0,)))).astype(BF16)
    split_cores(keep_ref, swap_ref, rows, 1)


def load_kernel(from_ref, to_ref):
    to_ref[...] = from_ref[...]


def pack_kernel(half, keep_ref, swap_ref, near_ref, *far_refs):
    for at in range(2):
        near_ref[at, 0] = keep_ref[at, 1]
        near_ref[at, 1] = swap_ref[at, 1]
        for k in range(2, half):
            far_refs[at * (half - 2) + k - 2][0] = keep_ref[at, k]
            far_refs[at * (half - 2) + k - 2][1] = swap_ref[at, k]


def pack_out_kernel(keep_ref, swap_ref, *far_refs):
    for k, far_ref in enumerate(far_refs):
        far_ref[0] = keep_ref[k + 2]
        far_ref[1] = swap_ref[k + 2]


def pack_last_kernel(out_keep_ref, out_swap_ref, keep_ref, swap_ref, near_ref, *far_refs):
    near_ref[0, 0] = out_keep_ref[1]
    near_ref[0, 1] = out_swap_ref[1]
    near_ref[1, 0] = keep_ref[1]
    near_ref[1, 1] = swap_ref[1]
    pack_out_kernel(keep_ref, swap_ref, *far_refs)


def pieces(at, keep_ref, swap_ref, near_ref, far_refs):
    found = [keep_ref[at + (0,)], swap_ref[at + (0,)]]
    found += [near_ref[at + (0,)], near_ref[at + (1,)]]
    for ref in far_refs:
        found += [ref[0], ref[1]]
    return found


def chunk_rows(rows, dp, k):
    chunk = rows // dp
    mine = lax.axis_index("dp")
    return pl.ds(pl.multiple_of((mine ^ k) * chunk, chunk), chunk)


def local_order(found, scratch, dp):
    scratch[...] = jnp.concatenate(found, axis=0)
    rows = scratch.shape[0]
    return jnp.concatenate([scratch[chunk_rows(rows, dp, k), :] for k in range(dp)], axis=0)


def gate_up_kernel(half, keep_ref, swap_ref, near_ref, *refs):
    far_refs, refs = refs[: half - 2], refs[half - 2 :]
    gate_ref, up_ref, local_ref, *out_refs, scratch = refs
    dp = len(out_refs)
    rows = local_order(pieces((0,), keep_ref, swap_ref, near_ref, far_refs), scratch, dp)
    local_ref[...] = rows
    chunk = rows.shape[0] // dp
    for at, mat in enumerate((gate_ref, up_ref)):
        part = mm(rows, mat[...], ((1,), (0,))).astype(BF16)
        for k, out_ref in enumerate(out_refs):
            out_ref[at] = part[k * chunk : (k + 1) * chunk]


def grad_act_kernel(half, keep_ref, swap_ref, near_ref, *refs):
    far_refs, refs = refs[: half - 2], refs[half - 2 :]
    down_ref, local_ref, *out_refs, scratch = refs
    dp = len(out_refs)
    rows = local_order(pieces((1,), keep_ref, swap_ref, near_ref, far_refs), scratch, dp)
    local_ref[...] = rows
    split_rows(out_refs, mm(rows, down_ref[...], ((1,), (1,))).astype(BF16))


def group_sum(refs, *at):
    total = refs[0][at].astype(F32)
    for ref in refs[1:]:
        total = total + ref[at].astype(F32)
    return total


def logistic(value):
    return 1.0 / (1.0 + jnp.exp(-value))


def act_kernel(dp, *refs):
    gate = group_sum(refs[:dp], 0)
    up = group_sum(refs[:dp], 1)
    refs[dp][...] = (gate * logistic(gate) * up).astype(BF16)


def grad_pre_kernel(dp, *refs):
    gate = group_sum(refs[:dp], 0)
    up = group_sum(refs[:dp], 1)
    grad = group_sum(refs[dp : 2 * dp], Ellipsis)
    out_ref = refs[2 * dp]
    soft = logistic(gate)
    out_ref[0] = (grad * up * (soft * (1.0 + gate * (1.0 - soft)))).astype(BF16)
    out_ref[1] = (grad * (gate * soft)).astype(BF16)


def send_back(keep_ref, swap_ref, scratch, rows, dp):
    chunk = rows.shape[0] // dp
    for k in range(dp):
        scratch[chunk_rows(rows.shape[0], dp, k), :] = rows[k * chunk : (k + 1) * chunk]
    split_cores(keep_ref, swap_ref, scratch[...])


def expert_out_kernel(dp, *refs):
    down_ref, act_ref, keep_ref, swap_ref, scratch = refs[dp:]
    act = join_rows(refs[:dp])
    act_ref[...] = act
    rows = mm(act, down_ref[...], ((1,), (0,))).astype(BF16)
    send_back(keep_ref, swap_ref, scratch, rows, dp)


def row_grad_kernel(dp, *refs):
    gate_ref, up_ref, gate_pre_ref, up_pre_ref, keep_ref, swap_ref, scratch = refs[dp:]
    gate_pre = jnp.concatenate([ref[0] for ref in refs[:dp]], axis=0)
    up_pre = jnp.concatenate([ref[1] for ref in refs[:dp]], axis=0)
    gate_pre_ref[...] = gate_pre
    up_pre_ref[...] = up_pre
    total = mm(gate_pre, gate_ref[...], ((1,), (1,))) + mm(up_pre, up_ref[...], ((1,), (1,)))
    send_back(keep_ref, swap_ref, scratch, total.astype(BF16), dp)


def scatter_scaled_kernel(pick_ref, weight_ref, keep_ref, swap_ref, near_ref, *refs):
    found = [keep_ref[0], swap_ref[0], near_ref[0, 0], near_ref[0, 1]]
    for ref in refs[:-1]:
        found += [ref[0], ref[1]]
    back = jnp.concatenate(found, axis=0).astype(F32)
    scaled = (weight_ref[...] * back).astype(BF16)
    refs[-1][...] = mm(pick_ref[...], scaled, ((0,), (0,))).astype(BF16)


def scatter_kernel(pick_ref, keep_ref, swap_ref, near_ref, *refs):
    found = [keep_ref[0], swap_ref[0], near_ref[1, 0], near_ref[1, 1]]
    for ref in refs[:-1]:
        found += [ref[0], ref[1]]
    back = jnp.concatenate(found, axis=0)
    refs[-1][...] = mm(pick_ref[...], back, ((0,), (0,))).astype(BF16)


def partner(value, axis, k):
    size = lax.axis_size(axis)
    return lax.ppermute(value, axis, [(i, i ^ k) for i in range(size)])


def trade(values):
    return [values[0]] + [partner(value, "dp", k + 1) for k, value in enumerate(values[1:])]


def whole(array):
    return pl.BlockSpec(array.shape, lambda i: (0,) * len(array.shape))


def body(tokens, grad_out, expert_ids, gates, w_gate, w_up, w_down):
    experts = lax.axis_size("expert")
    dp = lax.axis_size("dp")
    tok_rows, features = tokens.shape
    capacity = tok_rows // 16
    slots = experts * capacity
    hidden = w_gate.shape[2]
    chunk = slots // dp
    gate_mat, up_mat, down_mat = w_gate[0], w_up[0], w_down[0]
    shape = jax.ShapeDtypeStruct
    product = 2 * slots * features * hidden
    weights = 2 * features * hidden

    half = experts // 2
    sized = shape((slots, features), BF16)
    wide = shape((slots, hidden), BF16)
    both = shape((2, half, capacity, features), BF16)
    one = shape((half, capacity, features), BF16)
    near = shape((2, 2, capacity, features), BF16)
    far = [shape((2, capacity, features), BF16)] * (half - 2)
    in_order = [pltpu.VMEM((slots, features), BF16)]

    ins = (expert_ids.T, gates.T, tokens, grad_out)
    outs = (shape((slots, tok_rows), BF16), shape((slots, 1), F32), both, both)
    pick, weight, keep, swap = call(
        functools.partial(route_kernel, experts),
        outs,
        4 * slots * tok_rows * features,
        8 * tok_rows * features,
        limit=ROUTE_LIMIT,
        grid=(1,),
        in_specs=[whole(array) for array in ins],
        out_specs=tuple(whole(array) for array in outs),
    )(*ins)
    swap_to, up_mat = lax.optimization_barrier((swap, up_mat))
    swap = partner(swap_to, "expert", 1)
    up_mat = call(load_kernel, shape(up_mat.shape, BF16), 0, 2 * weights)(up_mat)
    swap, up_mat = lax.optimization_barrier((swap, up_mat))
    near_to, *far_to = call(functools.partial(pack_kernel, half), (near, *far, *far), 0, 8 * slots)(
        keep, swap
    )
    near_in = partner(near_to, "expert", 2)
    far_in = [
        partner(value, "expert", 2 * (2 + k % (half - 2))) for k, value in enumerate(far_to)
    ]
    rows, *part_pre = call(
        functools.partial(gate_up_kernel, half),
        (sized, *[shape((2, chunk, hidden), BF16)] * dp),
        2 * product,
        2 * weights,
        scratch_shapes=in_order,
    )(keep, swap, near_in, *far_in[: half - 2], gate_mat, up_mat)
    sums = trade(part_pre)
    grads, *part_grad = call(
        functools.partial(grad_act_kernel, half),
        (sized, *[shape((chunk, hidden), BF16)] * dp),
        product,
        weights,
        scratch_shapes=in_order,
    )(keep, swap, near_in, *far_in[half - 2 :], down_mat)
    grad_sums = trade(part_grad)
    sums, part_grad = lax.optimization_barrier((sums, part_grad))
    act_mine = call(
        functools.partial(act_kernel, dp),
        shape((chunk, hidden), BF16),
        0,
        4 * dp * chunk * hidden,
    )(*sums)
    acts = trade([act_mine] * dp)
    pre_mine = call(
        functools.partial(grad_pre_kernel, dp),
        shape((2, chunk, hidden), BF16),
        0,
        6 * dp * chunk * hidden,
    )(*sums, *grad_sums)
    pre = trade([pre_mine] * dp)
    act, out_keep, out_swap = call(
        functools.partial(expert_out_kernel, dp),
        (wide, one, one),
        product,
        weights,
        scratch_shapes=in_order,
    )(*acts, down_mat)
    out_swap = partner(out_swap, "expert", 1)
    out_far = call(pack_out_kernel, far, 0, 8 * slots)(out_keep, out_swap)
    out_far = [partner(value, "expert", 2 * (2 + k)) for k, value in enumerate(out_far)]
    gate_pre, up_pre, grad_keep, grad_swap = call(
        functools.partial(row_grad_kernel, dp),
        (wide, wide, one, one),
        2 * product,
        2 * weights,
        scratch_shapes=in_order,
    )(*pre, gate_mat, up_mat)
    grad_swap = partner(grad_swap, "expert", 1)
    grad_swap, out_far = lax.optimization_barrier((grad_swap, out_far))
    near_back, *grad_far = call(pack_last_kernel, (near, *far), 0, 8 * slots)(
        out_keep, out_swap, grad_keep, grad_swap
    )
    near_back = partner(near_back, "expert", 2)
    grad_far = [partner(value, "expert", 2 * (2 + k)) for k, value in enumerate(grad_far)]

    grad_down = mm(act, grads, ((0,), (0,))).astype(BF16)
    grad_gate = mm(rows, gate_pre, ((0,), (0,))).astype(BF16)
    grad_up = mm(rows, up_pre, ((0,), (0,))).astype(BF16)

    full = shape((tok_rows, features), BF16)
    mixed = call(
        scatter_scaled_kernel, full, 2 * slots * tok_rows * features, 4 * tok_rows * features
    )(pick, weight, out_keep, out_swap, near_back, *out_far)
    grad_tokens = call(
        scatter_kernel, full, 2 * slots * tok_rows * features, 4 * tok_rows * features
    )(pick, grad_keep, grad_swap, near_back, *grad_far)
    return (mixed, grad_tokens, grad_gate[None], grad_up[None], grad_down[None])


def solution(mesh):
    placed = (
        P("expert", "dp"),
        P("expert", "dp"),
        P("expert", None),
        P("expert", None),
        P("expert", "dp", None),
        P("expert", "dp", None),
        P("expert", None, "dp"),
    )
    return jax.shard_map(
        body,
        mesh=mesh,
        in_specs=placed,
        out_specs=(
            P("expert", "dp"),
            P("expert", "dp"),
            P("expert", "dp", None),
            P("expert", "dp", None),
            P("expert", None, "dp"),
        ),
        check_vma=False,
    )
```

```python
import functools

import jax
import jax.numpy as jnp
from jax import lax
from jax.experimental import pallas as pl
from jax.experimental.pallas import tpu as pltpu
from jax.sharding import PartitionSpec as P

F32 = jnp.float32
BF16 = jnp.bfloat16
MIB = 1024 * 1024
VMEM_LIMIT = 24 * MIB
ROUTE_LIMIT = 59 * MIB


def mm(left, right, dims):
    return lax.dot_general(left, right, (dims, ((), ())), preferred_element_type=F32)


def call(kernel, out_shape, flops=0, moved=0, limit=VMEM_LIMIT, **kwargs):
    return pl.pallas_call(
        kernel,
        out_shape=out_shape,
        cost_estimate=pl.CostEstimate(flops=flops, bytes_accessed=moved, transcendentals=0),
        compiler_params=pltpu.CompilerParams(vmem_limit_bytes=limit),
        **kwargs,
    )


def split_rows(refs, value):
    rows = value.shape[0] // len(refs)
    for k, ref in enumerate(refs):
        ref[...] = value[k * rows : (k + 1) * rows]


def join_rows(refs):
    return jnp.concatenate([ref[...] for ref in refs], axis=0)


def split_cores(keep_ref, swap_ref, value, *at):
    half, rows = keep_ref.shape[-3:-1]
    for k in range(half):
        keep_ref[(*at, k)] = value[2 * k * rows : (2 * k + 1) * rows]
        swap_ref[(*at, k)] = value[(2 * k + 1) * rows : (2 * k + 2) * rows]


def route_kernel(
    experts, ids_ref, gates_ref, tokens_ref, grad_ref, pick_ref, weight_ref, keep_ref, swap_ref
):
    ids = ids_ref[...]
    tok_rows = ids.shape[1]
    slots = pick_ref.shape[0]
    inside = ids < experts
    routed = jnp.max(inside.astype(jnp.int32), axis=0, keepdims=True)
    chosen = jnp.sum(jnp.where(inside, ids, 0), axis=0, keepdims=True)
    weight = jnp.sum(jnp.where(inside, gates_ref[...], 0.0), axis=0, keepdims=True)
    key = jnp.where(routed > 0, chosen ^ lax.axis_index("expert"), experts)
    hot = lax.broadcasted_iota(jnp.int32, (experts, tok_rows), 0) == key
    earlier = lax.broadcasted_iota(jnp.int32, (tok_rows, tok_rows), 0) < lax.broadcasted_iota(
        jnp.int32, (tok_rows, tok_rows), 1
    )
    before = mm(hot.astype(F32).astype(BF16), earlier.astype(F32).astype(BF16), ((1,), (0,)))
    position = jnp.sum(jnp.where(hot, before, 0.0), axis=0, keepdims=True).astype(jnp.int32)
    slot = jnp.where(routed > 0, key * (slots // experts) + position, slots)
    pick = lax.broadcasted_iota(jnp.int32, (slots, tok_rows), 0) == slot
    slot_weight = jnp.sum(jnp.where(pick, weight, 0.0), axis=1, keepdims=True)
    weight_ref[...] = slot_weight
    pick = pick.astype(F32).astype(BF16)
    pick_ref[...] = pick
    rows = mm(pick, tokens_ref[...], ((1,), (0,))).astype(BF16)
    split_cores(keep_ref, swap_ref, rows, 0)
    rows = (slot_weight * mm(pick, grad_ref[...], ((1,), (0,)))).astype(BF16)
    split_cores(keep_ref, swap_ref, rows, 1)


def load_kernel(from_ref, to_ref):
    to_ref[...] = from_ref[...]


def pack_kernel(half, keep_ref, swap_ref, near_ref, *far_refs):
    for at in range(2):
        near_ref[at, 0] = keep_ref[at, 1]
        near_ref[at, 1] = swap_ref[at, 1]
        for k in range(2, half):
            far_refs[at * (half - 2) + k - 2][0] = keep_ref[at, k]
            far_refs[at * (half - 2) + k - 2][1] = swap_ref[at, k]


def pack_back_kernel(keep_ref, swap_ref, *out_refs):
    for k, out_ref in enumerate(out_refs):
        out_ref[0] = keep_ref[k + 1]
        out_ref[1] = swap_ref[k + 1]


def pieces(at, keep_ref, swap_ref, near_ref, far_refs):
    found = [keep_ref[at + (0,)], swap_ref[at + (0,)]]
    found += [near_ref[at + (0,)], near_ref[at + (1,)]]
    for ref in far_refs:
        found += [ref[0], ref[1]]
    return found


def chunk_rows(rows, dp, k):
    chunk = rows // dp
    mine = lax.axis_index("dp")
    return pl.ds(pl.multiple_of((mine ^ k) * chunk, chunk), chunk)


def local_order(found, scratch, dp):
    scratch[...] = jnp.concatenate(found, axis=0)
    rows = scratch.shape[0]
    return jnp.concatenate([scratch[chunk_rows(rows, dp, k), :] for k in range(dp)], axis=0)


def gate_up_kernel(half, keep_ref, swap_ref, near_ref, *refs):
    far_refs, refs = refs[: half - 2], refs[half - 2 :]
    gate_ref, up_ref, local_ref, *out_refs, scratch = refs
    dp = len(out_refs)
    rows = local_order(pieces((0,), keep_ref, swap_ref, near_ref, far_refs), scratch, dp)
    local_ref[...] = rows
    chunk = rows.shape[0] // dp
    for at, mat in enumerate((gate_ref, up_ref)):
        part = mm(rows, mat[...], ((1,), (0,))).astype(BF16)
        for k, out_ref in enumerate(out_refs):
            out_ref[at] = part[k * chunk : (k + 1) * chunk]


def grad_act_kernel(half, keep_ref, swap_ref, near_ref, *refs):
    far_refs, refs = refs[: half - 2], refs[half - 2 :]
    down_ref, local_ref, *out_refs, scratch = refs
    dp = len(out_refs)
    rows = local_order(pieces((1,), keep_ref, swap_ref, near_ref, far_refs), scratch, dp)
    local_ref[...] = rows
    split_rows(out_refs, mm(rows, down_ref[...], ((1,), (1,))).astype(BF16))


def group_sum(refs, *at):
    total = refs[0][at].astype(F32)
    for ref in refs[1:]:
        total = total + ref[at].astype(F32)
    return total


def logistic(value):
    return 1.0 / (1.0 + jnp.exp(-value))


def act_kernel(dp, *refs):
    gate = group_sum(refs[:dp], 0)
    up = group_sum(refs[:dp], 1)
    refs[dp][...] = (gate * logistic(gate) * up).astype(BF16)


def grad_pre_kernel(dp, *refs):
    gate = group_sum(refs[:dp], 0)
    up = group_sum(refs[:dp], 1)
    grad = group_sum(refs[dp : 2 * dp], Ellipsis)
    out_ref = refs[2 * dp]
    soft = logistic(gate)
    out_ref[0] = (grad * up * (soft * (1.0 + gate * (1.0 - soft)))).astype(BF16)
    out_ref[1] = (grad * (gate * soft)).astype(BF16)


def send_back(keep_ref, swap_ref, scratch, rows, dp):
    chunk = rows.shape[0] // dp
    for k in range(dp):
        scratch[chunk_rows(rows.shape[0], dp, k), :] = rows[k * chunk : (k + 1) * chunk]
    split_cores(keep_ref, swap_ref, scratch[...])


def expert_out_kernel(dp, *refs):
    down_ref, act_ref, keep_ref, swap_ref, scratch = refs[dp:]
    act = join_rows(refs[:dp])
    act_ref[...] = act
    rows = mm(act, down_ref[...], ((1,), (0,))).astype(BF16)
    send_back(keep_ref, swap_ref, scratch, rows, dp)


def row_grad_kernel(dp, *refs):
    gate_ref, up_ref, gate_pre_ref, up_pre_ref, keep_ref, swap_ref, scratch = refs[dp:]
    gate_pre = jnp.concatenate([ref[0] for ref in refs[:dp]], axis=0)
    up_pre = jnp.concatenate([ref[1] for ref in refs[:dp]], axis=0)
    gate_pre_ref[...] = gate_pre
    up_pre_ref[...] = up_pre
    total = mm(gate_pre, gate_ref[...], ((1,), (1,))) + mm(up_pre, up_ref[...], ((1,), (1,)))
    send_back(keep_ref, swap_ref, scratch, total.astype(BF16), dp)


def returned(keep_ref, swap_ref, refs):
    found = [keep_ref[0], swap_ref[0]]
    for ref in refs:
        found += [ref[0], ref[1]]
    return jnp.concatenate(found, axis=0)


def scatter_scaled_kernel(pick_ref, weight_ref, keep_ref, swap_ref, *refs):
    back = returned(keep_ref, swap_ref, refs[:-1]).astype(F32)
    scaled = (weight_ref[...] * back).astype(BF16)
    refs[-1][...] = mm(pick_ref[...], scaled, ((0,), (0,))).astype(BF16)


def scatter_kernel(pick_ref, keep_ref, swap_ref, *refs):
    back = returned(keep_ref, swap_ref, refs[:-1])
    refs[-1][...] = mm(pick_ref[...], back, ((0,), (0,))).astype(BF16)


def partner(value, axis, k):
    size = lax.axis_size(axis)
    return lax.ppermute(value, axis, [(i, i ^ k) for i in range(size)])


def trade(values):
    return [values[0]] + [partner(value, "dp", k + 1) for k, value in enumerate(values[1:])]


def whole(array):
    return pl.BlockSpec(array.shape, lambda i: (0,) * len(array.shape))


def body(tokens, grad_out, expert_ids, gates, w_gate, w_up, w_down):
    experts = lax.axis_size("expert")
    dp = lax.axis_size("dp")
    tok_rows, features = tokens.shape
    capacity = tok_rows // 16
    slots = experts * capacity
    hidden = w_gate.shape[2]
    chunk = slots // dp
    gate_mat, up_mat, down_mat = w_gate[0], w_up[0], w_down[0]
    shape = jax.ShapeDtypeStruct
    product = 2 * slots * features * hidden
    weights = 2 * features * hidden

    half = experts // 2
    sized = shape((slots, features), BF16)
    wide = shape((slots, hidden), BF16)
    both = shape((2, half, capacity, features), BF16)
    one = shape((half, capacity, features), BF16)
    near = shape((2, 2, capacity, features), BF16)
    far = [shape((2, capacity, features), BF16)] * (half - 2)
    in_order = [pltpu.VMEM((slots, features), BF16)]

    ins = (expert_ids.T, gates.T, tokens, grad_out)
    outs = (shape((slots, tok_rows), BF16), shape((slots, 1), F32), both, both)
    pick, weight, keep, swap = call(
        functools.partial(route_kernel, experts),
        outs,
        4 * slots * tok_rows * features,
        8 * tok_rows * features,
        limit=ROUTE_LIMIT,
        grid=(1,),
        in_specs=[whole(array) for array in ins],
        out_specs=tuple(whole(array) for array in outs),
    )(*ins)
    swap_to, up_mat = lax.optimization_barrier((swap, up_mat))
    swap = partner(swap_to, "expert", 1)
    up_mat = call(load_kernel, shape(up_mat.shape, BF16), 0, 2 * weights)(up_mat)
    swap, up_mat = lax.optimization_barrier((swap, up_mat))
    near_to, *far_to = call(functools.partial(pack_kernel, half), (near, *far, *far), 0, 8 * slots)(
        keep, swap
    )
    far_rows = [partner(far_to[k], "expert", 2 * (2 + k)) for k in reversed(range(half - 2))][::-1]
    near_in = partner(near_to, "expert", 2)
    far_grads = [partner(far_to[half - 2 + k], "expert", 2 * (2 + k)) for k in range(half - 2)]
    rows, *part_pre = call(
        functools.partial(gate_up_kernel, half),
        (sized, *[shape((2, chunk, hidden), BF16)] * dp),
        2 * product,
        2 * weights,
        scratch_shapes=in_order,
    )(keep, swap, near_in, *far_rows, gate_mat, up_mat)
    sums = trade(part_pre)
    act_mine = call(
        functools.partial(act_kernel, dp),
        shape((chunk, hidden), BF16),
        0,
        4 * dp * chunk * hidden,
    )(*sums)
    acts = trade([act_mine] * dp)
    far_grads, act_mine = lax.optimization_barrier((far_grads, act_mine))
    grads, *part_grad = call(
        functools.partial(grad_act_kernel, half),
        (sized, *[shape((chunk, hidden), BF16)] * dp),
        product,
        weights,
        scratch_shapes=in_order,
    )(keep, swap, near_in, *far_grads, down_mat)
    grad_sums = trade(part_grad)
    pre_mine = call(
        functools.partial(grad_pre_kernel, dp),
        shape((2, chunk, hidden), BF16),
        0,
        6 * dp * chunk * hidden,
    )(*sums, *grad_sums)
    pre = trade([pre_mine] * dp)
    act, out_keep, out_swap = call(
        functools.partial(expert_out_kernel, dp),
        (wide, one, one),
        product,
        weights,
        scratch_shapes=in_order,
    )(*acts, down_mat)
    back = [far[0]] * (half - 1)
    out_swap = partner(out_swap, "expert", 1)
    out_near, *out_far = call(pack_back_kernel, back, 0, 8 * slots)(out_keep, out_swap)
    out_far = [partner(value, "expert", 2 * (2 + k)) for k, value in enumerate(out_far)]
    pre, out_far = lax.optimization_barrier((pre, out_far))
    gate_pre, up_pre, grad_keep, grad_swap = call(
        functools.partial(row_grad_kernel, dp),
        (wide, wide, one, one),
        2 * product,
        2 * weights,
        scratch_shapes=in_order,
    )(*pre, gate_mat, up_mat)
    grad_swap, out_near = lax.optimization_barrier((grad_swap, out_near))
    grad_swap = partner(grad_swap, "expert", 1)
    out_near = partner(out_near, "expert", 2)
    grad_back = call(pack_back_kernel, back, 0, 8 * slots)(grad_keep, grad_swap)
    grad_back = [
        partner(grad_back[k], "expert", 2 * (1 + k)) for k in reversed(range(half - 1))
    ][::-1]

    grad_down = mm(act, grads, ((0,), (0,))).astype(BF16)
    grad_gate = mm(rows, gate_pre, ((0,), (0,))).astype(BF16)
    grad_up = mm(rows, up_pre, ((0,), (0,))).astype(BF16)

    full = shape((tok_rows, features), BF16)
    mixed = call(
        scatter_scaled_kernel, full, 2 * slots * tok_rows * features, 4 * tok_rows * features
    )(pick, weight, out_keep, out_swap, out_near, *out_far)
    grad_tokens = call(
        scatter_kernel, full, 2 * slots * tok_rows * features, 4 * tok_rows * features
    )(pick, grad_keep, grad_swap, *grad_back)
    return (mixed, grad_tokens, grad_gate[None], grad_up[None], grad_down[None])


def solution(mesh):
    placed = (
        P("expert", "dp"),
        P("expert", "dp"),
        P("expert", None),
        P("expert", None),
        P("expert", "dp", None),
        P("expert", "dp", None),
        P("expert", None, "dp"),
    )
    return jax.shard_map(
        body,
        mesh=mesh,
        in_specs=placed,
        out_specs=(
            P("expert", "dp"),
            P("expert", "dp"),
            P("expert", "dp", None),
            P("expert", "dp", None),
            P("expert", None, "dp"),
        ),
        check_vma=False,
    )
```

```python
import functools

import jax
import jax.numpy as jnp
from jax import lax
from jax.experimental import pallas as pl
from jax.experimental.pallas import tpu as pltpu
from jax.sharding import PartitionSpec as P

F32 = jnp.float32
BF16 = jnp.bfloat16
MIB = 1024 * 1024
VMEM_LIMIT = 24 * MIB
ROUTE_LIMIT = 59 * MIB


def mm(left, right, dims):
    return lax.dot_general(left, right, (dims, ((), ())), preferred_element_type=F32)


def call(kernel, out_shape, flops=0, moved=0, limit=VMEM_LIMIT, **kwargs):
    return pl.pallas_call(
        kernel,
        out_shape=out_shape,
        cost_estimate=pl.CostEstimate(flops=flops, bytes_accessed=moved, transcendentals=0),
        compiler_params=pltpu.CompilerParams(vmem_limit_bytes=limit),
        **kwargs,
    )


def split_rows(refs, value):
    rows = value.shape[0] // len(refs)
    for k, ref in enumerate(refs):
        ref[...] = value[k * rows : (k + 1) * rows]


def join_rows(refs):
    return jnp.concatenate([ref[...] for ref in refs], axis=0)


def split_cores(keep_ref, swap_ref, value, *at):
    half, rows = keep_ref.shape[-3:-1]
    for k in range(half):
        keep_ref[(*at, k)] = value[2 * k * rows : (2 * k + 1) * rows]
        swap_ref[(*at, k)] = value[(2 * k + 1) * rows : (2 * k + 2) * rows]


def route_kernel(experts, *refs):
    pick_ref, weight_ref, keep_ref, swap_ref = refs[4:8]
    ids_ref, gates_ref, tokens_ref, grad_ref, sems = refs[8:]
    copies = [
        pltpu.make_async_copy(refs[k], refs[8 + k], sems.at[k]) for k in range(4)
    ]
    for copy in copies:
        copy.start()
    copies[0].wait()
    copies[1].wait()
    ids = ids_ref[...]
    tok_rows = ids.shape[1]
    slots = pick_ref.shape[0]
    inside = ids < experts
    routed = jnp.max(inside.astype(jnp.int32), axis=0, keepdims=True)
    chosen = jnp.sum(jnp.where(inside, ids, 0), axis=0, keepdims=True)
    weight = jnp.sum(jnp.where(inside, gates_ref[...], 0.0), axis=0, keepdims=True)
    key = jnp.where(routed > 0, chosen ^ lax.axis_index("expert"), experts)
    hot = lax.broadcasted_iota(jnp.int32, (experts, tok_rows), 0) == key
    earlier = lax.broadcasted_iota(jnp.int32, (tok_rows, tok_rows), 0) < lax.broadcasted_iota(
        jnp.int32, (tok_rows, tok_rows), 1
    )
    before = mm(hot.astype(F32).astype(BF16), earlier.astype(F32).astype(BF16), ((1,), (0,)))
    position = jnp.sum(jnp.where(hot, before, 0.0), axis=0, keepdims=True).astype(jnp.int32)
    slot = jnp.where(routed > 0, key * (slots // experts) + position, slots)
    pick = lax.broadcasted_iota(jnp.int32, (slots, tok_rows), 0) == slot
    slot_weight = jnp.sum(jnp.where(pick, weight, 0.0), axis=1, keepdims=True)
    weight_ref[...] = slot_weight
    pick = pick.astype(F32).astype(BF16)
    pick_ref[...] = pick
    copies[2].wait()
    rows = mm(pick, tokens_ref[...], ((1,), (0,))).astype(BF16)
    split_cores(keep_ref, swap_ref, rows, 0)
    copies[3].wait()
    rows = (slot_weight * mm(pick, grad_ref[...], ((1,), (0,)))).astype(BF16)
    split_cores(keep_ref, swap_ref, rows, 1)


def load_kernel(from_ref, to_ref):
    to_ref[...] = from_ref[...]


def pack_kernel(half, keep_ref, swap_ref, near_ref, *far_refs):
    for at in range(2):
        near_ref[at, 0] = keep_ref[at, 1]
        near_ref[at, 1] = swap_ref[at, 1]
        for k in range(2, half):
            far_refs[at * (half - 2) + k - 2][0] = keep_ref[at, k]
            far_refs[at * (half - 2) + k - 2][1] = swap_ref[at, k]


def pack_back_kernel(keep_ref, swap_ref, *out_refs):
    for k, out_ref in enumerate(out_refs):
        out_ref[0] = keep_ref[k + 1]
        out_ref[1] = swap_ref[k + 1]


def pieces(at, keep_ref, swap_ref, near_ref, far_refs):
    found = [keep_ref[at + (0,)], swap_ref[at + (0,)]]
    found += [near_ref[at + (0,)], near_ref[at + (1,)]]
    for ref in far_refs:
        found += [ref[0], ref[1]]
    return found


def chunk_rows(rows, dp, k):
    chunk = rows // dp
    mine = lax.axis_index("dp")
    return pl.ds(pl.multiple_of((mine ^ k) * chunk, chunk), chunk)


def local_order(found, scratch, dp):
    scratch[...] = jnp.concatenate(found, axis=0)
    rows = scratch.shape[0]
    return jnp.concatenate([scratch[chunk_rows(rows, dp, k), :] for k in range(dp)], axis=0)


def gate_up_kernel(half, keep_ref, swap_ref, near_ref, *refs):
    far_refs, refs = refs[: half - 2], refs[half - 2 :]
    gate_ref, up_ref, local_ref, *out_refs, scratch = refs
    dp = len(out_refs)
    rows = local_order(pieces((0,), keep_ref, swap_ref, near_ref, far_refs), scratch, dp)
    local_ref[...] = rows
    chunk = rows.shape[0] // dp
    for at, mat in enumerate((gate_ref, up_ref)):
        part = mm(rows, mat[...], ((1,), (0,))).astype(BF16)
        for k, out_ref in enumerate(out_refs):
            out_ref[at] = part[k * chunk : (k + 1) * chunk]


def grad_act_kernel(half, keep_ref, swap_ref, near_ref, *refs):
    far_refs, refs = refs[: half - 2], refs[half - 2 :]
    down_ref, local_ref, *out_refs, scratch = refs
    dp = len(out_refs)
    rows = local_order(pieces((1,), keep_ref, swap_ref, near_ref, far_refs), scratch, dp)
    local_ref[...] = rows
    split_rows(out_refs, mm(rows, down_ref[...], ((1,), (1,))).astype(BF16))


def group_sum(refs, *at):
    total = refs[0][at].astype(F32)
    for ref in refs[1:]:
        total = total + ref[at].astype(F32)
    return total


def logistic(value):
    return 1.0 / (1.0 + jnp.exp(-value))


def act_kernel(dp, *refs):
    gate = group_sum(refs[:dp], 0)
    up = group_sum(refs[:dp], 1)
    refs[dp][...] = (gate * logistic(gate) * up).astype(BF16)


def grad_pre_kernel(dp, *refs):
    gate = group_sum(refs[:dp], 0)
    up = group_sum(refs[:dp], 1)
    grad = group_sum(refs[dp : 2 * dp], Ellipsis)
    out_ref = refs[2 * dp]
    soft = logistic(gate)
    out_ref[0] = (grad * up * (soft * (1.0 + gate * (1.0 - soft)))).astype(BF16)
    out_ref[1] = (grad * (gate * soft)).astype(BF16)


def send_back(keep_ref, swap_ref, scratch, rows, dp):
    chunk = rows.shape[0] // dp
    for k in range(dp):
        scratch[chunk_rows(rows.shape[0], dp, k), :] = rows[k * chunk : (k + 1) * chunk]
    split_cores(keep_ref, swap_ref, scratch[...])


def expert_out_kernel(dp, *refs):
    down_ref, act_ref, keep_ref, swap_ref, scratch = refs[dp:]
    act = join_rows(refs[:dp])
    act_ref[...] = act
    rows = mm(act, down_ref[...], ((1,), (0,))).astype(BF16)
    send_back(keep_ref, swap_ref, scratch, rows, dp)


def row_grad_kernel(dp, *refs):
    gate_ref, up_ref, gate_pre_ref, up_pre_ref, keep_ref, swap_ref, scratch = refs[dp:]
    gate_pre = jnp.concatenate([ref[0] for ref in refs[:dp]], axis=0)
    up_pre = jnp.concatenate([ref[1] for ref in refs[:dp]], axis=0)
    gate_pre_ref[...] = gate_pre
    up_pre_ref[...] = up_pre
    total = mm(gate_pre, gate_ref[...], ((1,), (1,))) + mm(up_pre, up_ref[...], ((1,), (1,)))
    send_back(keep_ref, swap_ref, scratch, total.astype(BF16), dp)


def returned(keep_ref, swap_ref, refs):
    found = [keep_ref[0], swap_ref[0]]
    for ref in refs:
        found += [ref[0], ref[1]]
    return jnp.concatenate(found, axis=0)


def scatter_scaled_kernel(pick_ref, weight_ref, keep_ref, swap_ref, *refs):
    back = returned(keep_ref, swap_ref, refs[:-1]).astype(F32)
    scaled = (weight_ref[...] * back).astype(BF16)
    refs[-1][...] = mm(pick_ref[...], scaled, ((0,), (0,))).astype(BF16)


def scatter_kernel(pick_ref, keep_ref, swap_ref, *refs):
    back = returned(keep_ref, swap_ref, refs[:-1])
    refs[-1][...] = mm(pick_ref[...], back, ((0,), (0,))).astype(BF16)


def partner(value, axis, k):
    size = lax.axis_size(axis)
    return lax.ppermute(value, axis, [(i, i ^ k) for i in range(size)])


def trade(values):
    far_first = reversed(range(1, len(values)))
    return [values[0]] + [partner(values[k], "dp", k) for k in far_first][::-1]


def body(tokens, grad_out, expert_ids, gates, w_gate, w_up, w_down):
    experts = lax.axis_size("expert")
    dp = lax.axis_size("dp")
    tok_rows, features = tokens.shape
    capacity = tok_rows // 16
    slots = experts * capacity
    hidden = w_gate.shape[2]
    chunk = slots // dp
    gate_mat, up_mat, down_mat = w_gate[0], w_up[0], w_down[0]
    shape = jax.ShapeDtypeStruct
    product = 2 * slots * features * hidden
    weights = 2 * features * hidden

    half = experts // 2
    sized = shape((slots, features), BF16)
    wide = shape((slots, hidden), BF16)
    both = shape((2, half, capacity, features), BF16)
    one = shape((half, capacity, features), BF16)
    near = shape((2, 2, capacity, features), BF16)
    far = [shape((2, capacity, features), BF16)] * (half - 2)
    in_order = [pltpu.VMEM((slots, features), BF16)]

    ins = (expert_ids.T, gates.T, tokens, grad_out)
    outs = (shape((slots, tok_rows), BF16), shape((slots, 1), F32), both, both)
    pick, weight, keep, swap = call(
        functools.partial(route_kernel, experts),
        outs,
        4 * slots * tok_rows * features,
        8 * tok_rows * features,
        limit=ROUTE_LIMIT,
        in_specs=[pl.BlockSpec(memory_space=pl.ANY)] * 4,
        scratch_shapes=[
            *[pltpu.VMEM(array.shape, array.dtype) for array in ins],
            pltpu.SemaphoreType.DMA((4,)),
        ],
    )(*ins)
    swap_to, up_mat = lax.optimization_barrier((swap, up_mat))
    swap = partner(swap_to, "expert", 1)
    up_mat = call(load_kernel, shape(up_mat.shape, BF16), 0, 2 * weights)(up_mat)
    swap, up_mat = lax.optimization_barrier((swap, up_mat))
    near_to, *far_to = call(functools.partial(pack_kernel, half), (near, *far, *far), 0, 8 * slots)(
        keep, swap
    )
    far_rows = [partner(far_to[k], "expert", 2 * (2 + k)) for k in reversed(range(half - 2))][::-1]
    near_in = partner(near_to, "expert", 2)
    far_grads = [partner(far_to[half - 2 + k], "expert", 2 * (2 + k)) for k in range(half - 2)]
    rows, *part_pre = call(
        functools.partial(gate_up_kernel, half),
        (sized, *[shape((2, chunk, hidden), BF16)] * dp),
        2 * product,
        2 * weights,
        scratch_shapes=in_order,
    )(keep, swap, near_in, *far_rows, gate_mat, up_mat)
    sums = trade(part_pre)[::-1]
    act_mine = call(
        functools.partial(act_kernel, dp),
        shape((chunk, hidden), BF16),
        0,
        4 * dp * chunk * hidden,
    )(*sums)
    acts = trade([act_mine] * dp)
    far_grads, act_mine = lax.optimization_barrier((far_grads, act_mine))
    grads, *part_grad = call(
        functools.partial(grad_act_kernel, half),
        (sized, *[shape((chunk, hidden), BF16)] * dp),
        product,
        weights,
        scratch_shapes=in_order,
    )(keep, swap, near_in, *far_grads, down_mat)
    grad_sums = trade(part_grad)[::-1]
    pre_mine = call(
        functools.partial(grad_pre_kernel, dp),
        shape((2, chunk, hidden), BF16),
        0,
        6 * dp * chunk * hidden,
    )(*sums, *grad_sums)
    pre = trade([pre_mine] * dp)
    act, out_keep, out_swap = call(
        functools.partial(expert_out_kernel, dp),
        (wide, one, one),
        product,
        weights,
        scratch_shapes=in_order,
    )(*acts, down_mat)
    back = [far[0]] * (half - 1)
    out_swap = partner(out_swap, "expert", 1)
    out_near, *out_far = call(pack_back_kernel, back, 0, 8 * slots)(out_keep, out_swap)
    out_far = [partner(value, "expert", 2 * (2 + k)) for k, value in enumerate(out_far)]
    pre, out_far = lax.optimization_barrier((pre, out_far))
    gate_pre, up_pre, grad_keep, grad_swap = call(
        functools.partial(row_grad_kernel, dp),
        (wide, wide, one, one),
        2 * product,
        2 * weights,
        scratch_shapes=in_order,
    )(*pre, gate_mat, up_mat)
    grad_swap = partner(grad_swap, "expert", 1)
    out_near = partner(out_near, "expert", 2)
    grad_swap, gate_pre, up_pre = lax.optimization_barrier((grad_swap, gate_pre, up_pre))
    grad_back = call(pack_back_kernel, back, 0, 8 * slots)(grad_keep, grad_swap)
    grad_back = [
        partner(grad_back[k], "expert", 2 * (1 + k)) for k in reversed(range(half - 1))
    ][::-1]

    grad_down = mm(act, grads, ((0,), (0,))).astype(BF16)
    grad_gate = mm(rows, gate_pre, ((0,), (0,))).astype(BF16)
    grad_up = mm(rows, up_pre, ((0,), (0,))).astype(BF16)

    full = shape((tok_rows, features), BF16)
    mixed = call(
        scatter_scaled_kernel, full, 2 * slots * tok_rows * features, 4 * tok_rows * features
    )(pick, weight, out_keep, out_swap, out_near, *out_far)
    grad_tokens = call(
        scatter_kernel, full, 2 * slots * tok_rows * features, 4 * tok_rows * features
    )(pick, grad_keep, grad_swap, *grad_back)
    return (mixed, grad_tokens, grad_gate[None], grad_up[None], grad_down[None])


def solution(mesh):
    placed = (
        P("expert", "dp"),
        P("expert", "dp"),
        P("expert", None),
        P("expert", None),
        P("expert", "dp", None),
        P("expert", "dp", None),
        P("expert", None, "dp"),
    )
    return jax.shard_map(
        body,
        mesh=mesh,
        in_specs=placed,
        out_specs=(
            P("expert", "dp"),
            P("expert", "dp"),
            P("expert", "dp", None),
            P("expert", "dp", None),
            P("expert", None, "dp"),
        ),
        check_vma=False,
    )
```

```python
import functools

import jax
import jax.numpy as jnp
from jax import lax
from jax.experimental import pallas as pl
from jax.experimental.pallas import tpu as pltpu
from jax.sharding import PartitionSpec as P

F32 = jnp.float32
BF16 = jnp.bfloat16
MIB = 1024 * 1024
ANY = pl.BlockSpec(memory_space=pl.ANY)
VMEM_LIMIT = 24 * MIB
ROUTE_LIMIT = 59 * MIB


def mm(left, right, dims):
    return lax.dot_general(left, right, (dims, ((), ())), preferred_element_type=F32)


def call(kernel, out_shape, flops=0, limit=VMEM_LIMIT, **kwargs):
    return pl.pallas_call(
        kernel,
        out_shape=out_shape,
        cost_estimate=pl.CostEstimate(flops=flops, bytes_accessed=flops // 256, transcendentals=0),
        compiler_params=pltpu.CompilerParams(vmem_limit_bytes=limit),
        **kwargs,
    )


def split_rows(refs, value):
    rows = value.shape[0] // len(refs)
    for k, ref in enumerate(refs):
        ref[...] = value[k * rows : (k + 1) * rows]


def join_rows(refs):
    return jnp.concatenate([ref[...] for ref in refs], axis=0)


def split_cores(keep_ref, swap_ref, value, *at):
    half, rows = keep_ref.shape[-3:-1]
    for k in range(half):
        keep_ref[(*at, k)] = value[2 * k * rows : (2 * k + 1) * rows]
        swap_ref[(*at, k)] = value[(2 * k + 1) * rows : (2 * k + 2) * rows]


def route_kernel(experts, *refs):
    pick_ref, weight_ref, keep_ref, swap_ref = refs[4:8]
    ids_ref, gates_ref, tokens_ref, grad_ref, sems = refs[8:]
    copies = [
        pltpu.make_async_copy(refs[k], refs[8 + k], sems.at[k]) for k in range(4)
    ]
    for copy in copies:
        copy.start()
    copies[0].wait()
    copies[1].wait()
    ids = ids_ref[...]
    tok_rows = ids.shape[1]
    slots = pick_ref.shape[0]
    inside = ids < experts
    routed = jnp.max(inside.astype(jnp.int32), axis=0, keepdims=True)
    chosen = jnp.sum(jnp.where(inside, ids, 0), axis=0, keepdims=True)
    weight = jnp.sum(jnp.where(inside, gates_ref[...], 0.0), axis=0, keepdims=True)
    key = jnp.where(routed > 0, chosen ^ lax.axis_index("expert"), experts)
    hot = lax.broadcasted_iota(jnp.int32, (experts, tok_rows), 0) == key
    earlier = lax.broadcasted_iota(jnp.int32, (tok_rows, tok_rows), 0) < lax.broadcasted_iota(
        jnp.int32, (tok_rows, tok_rows), 1
    )
    before = mm(hot.astype(F32).astype(BF16), earlier.astype(F32).astype(BF16), ((1,), (0,)))
    position = jnp.sum(jnp.where(hot, before, 0.0), axis=0, keepdims=True).astype(jnp.int32)
    slot = jnp.where(routed > 0, key * (slots // experts) + position, slots)
    pick = lax.broadcasted_iota(jnp.int32, (slots, tok_rows), 0) == slot
    slot_weight = jnp.sum(jnp.where(pick, weight, 0.0), axis=1, keepdims=True)
    weight_ref[...] = slot_weight
    pick = pick.astype(F32).astype(BF16)
    pick_ref[...] = pick
    copies[2].wait()
    rows = mm(pick, tokens_ref[...], ((1,), (0,))).astype(BF16)
    split_cores(keep_ref, swap_ref, rows, 0)
    copies[3].wait()
    rows = (slot_weight * mm(pick, grad_ref[...], ((1,), (0,)))).astype(BF16)
    split_cores(keep_ref, swap_ref, rows, 1)


def load_kernel(from_ref, to_ref):
    to_ref[...] = from_ref[...]


def pack_kernel(half, keep_ref, swap_ref, near_ref, *far_refs):
    for at in range(2):
        near_ref[at, 0] = keep_ref[at, 1]
        near_ref[at, 1] = swap_ref[at, 1]
        for k in range(2, half):
            far_refs[at * (half - 2) + k - 2][0] = keep_ref[at, k]
            far_refs[at * (half - 2) + k - 2][1] = swap_ref[at, k]


def pack_back_kernel(first, keep_ref, swap_ref, *refs):
    out_refs = refs[-(keep_ref.shape[0] - first) :]
    for k, out_ref in enumerate(out_refs):
        out_ref[0] = keep_ref[k + first]
        out_ref[1] = swap_ref[k + first]


def near_pieces(at, keep_ref, swap_ref, near_ref):
    return [keep_ref[at, 0], swap_ref[at, 0], near_ref[at, 0], near_ref[at, 1]]


def pair_pieces(refs):
    return [ref[k] for ref in refs for k in range(2)]


def part_rows(rows, dp, k):
    part = rows // dp
    mine = lax.axis_index("dp")
    return pl.ds(pl.multiple_of((mine ^ k) * part, part), part)


def local_order(found, scratch, dp):
    scratch[...] = jnp.concatenate(found, axis=0)
    rows = scratch.shape[0]
    return [scratch[part_rows(rows, dp, k), :] for k in range(dp)]


def natural_order(parts, scratch):
    for k, part in enumerate(parts):
        scratch[part_rows(scratch.shape[0], len(parts), k), :] = part
    return scratch[...]


def gate_up_kernel(dp, first, *refs):
    count = 1 if first else dp
    gate_ref, up_ref, local_ref, *out_refs, scratch = refs[-count - 4 :]
    refs = refs[: -count - 4]
    if first:
        found = near_pieces(0, *refs[:3]) + pair_pieces(refs[3:])
    else:
        found = pair_pieces(refs[1:])
    rows = jnp.concatenate(local_order(found, scratch, dp), axis=0)
    local_ref[...] = rows
    part = rows.shape[0] // dp
    for at, mat in enumerate((gate_ref, up_ref)):
        sums = mm(rows, mat[...], ((1,), (0,))).astype(BF16)
        for k in range(dp):
            if first:
                out_refs[0][lax.axis_index("dp") ^ k, at] = sums[k * part : (k + 1) * part]
            else:
                out_refs[k][at] = sums[k * part : (k + 1) * part]


def grad_act_kernel(dp, early, keep_ref, swap_ref, near_ref, *refs):
    down_ref, local_ref, *out_refs, early_scratch, late_scratch = refs[-dp - 4 :]
    far_refs = refs[: -dp - 4]
    found = near_pieces(1, keep_ref, swap_ref, near_ref) + pair_pieces(far_refs[:early])
    rows = local_order(found, early_scratch, dp)
    rows += local_order(pair_pieces(far_refs[early:]), late_scratch, dp)
    rows = jnp.concatenate(rows, axis=0)
    local_ref[...] = rows
    sums = mm(rows, down_ref[...], ((1,), (1,))).astype(BF16)
    part = sums.shape[0] // (2 * dp)
    for k, out_ref in enumerate(out_refs):
        out_ref[0] = sums[k * part : (k + 1) * part]
        out_ref[1] = sums[(dp + k) * part : (dp + k + 1) * part]


def group_sum(pieces):
    total = pieces[0].astype(F32)
    for piece in pieces[1:]:
        total = total + piece.astype(F32)
    return total


def received(refs, dp):
    if len(refs) == 1:
        return [refs[0].at[k] for k in range(dp)]
    return refs


def logistic(value):
    return 1.0 / (1.0 + jnp.exp(-value))


def act_kernel(dp, *refs):
    for at, sums in enumerate((refs[:1], refs[1 : dp + 1])):
        sums = received(sums, dp)
        gate = group_sum([ref[0] for ref in sums])
        up = group_sum([ref[1] for ref in sums])
        refs[-1][at] = (gate * logistic(gate) * up).astype(BF16)


def grad_pre_kernel(dp, at, count, *refs):
    sums = received(refs[:count], dp)
    out_ref = refs[-1]
    gate = group_sum([ref[0] for ref in sums])
    up = group_sum([ref[1] for ref in sums])
    grad = group_sum([ref[at] for ref in refs[count : count + dp]])
    soft = logistic(gate)
    gate_pre = (grad * up * (soft * (1.0 + gate * (1.0 - soft)))).astype(BF16)
    up_pre = (grad * (gate * soft)).astype(BF16)
    copies = [out_ref] if count > 1 else received([out_ref], dp)
    for copy in copies:
        copy[0] = gate_pre
        copy[1] = up_pre


def store_cores(keep_ref, swap_ref, value, first):
    rows = keep_ref.shape[1]
    for k in range(value.shape[0] // (2 * rows)):
        keep_ref[first + k] = value[2 * k * rows : (2 * k + 1) * rows]
        swap_ref[first + k] = value[(2 * k + 1) * rows : (2 * k + 2) * rows]


def expert_out_kernel(dp, *refs):
    down_ref = refs[dp]
    act_ref, keep_ref, swap_ref, early_scratch, late_scratch = refs[-5:]
    act = jnp.concatenate([ref[at] for at in range(2) for ref in refs[:dp]], axis=0)
    act_ref[...] = act
    rows = mm(act, down_ref[...], ((1,), (0,))).astype(BF16)
    part = rows.shape[0] // (2 * dp)
    parts = [rows[k * part : (k + 1) * part] for k in range(2 * dp)]
    store_cores(keep_ref, swap_ref, natural_order(parts[:dp], early_scratch), 0)
    half = keep_ref.shape[0] // 2
    store_cores(keep_ref, swap_ref, natural_order(parts[dp:], late_scratch), half)


def row_grad_kernel(dp, count, *refs):
    gate_ref, up_ref = refs[count : count + 2]
    gate_pre_ref, up_pre_ref, keep_ref, swap_ref, scratch = refs[-5:]
    if count > 1:
        pre = refs[:dp]
    else:
        pre = [refs[0].at[lax.axis_index("dp") ^ k] for k in range(dp)]
    gate_pre = jnp.concatenate([ref[0] for ref in pre], axis=0)
    up_pre = jnp.concatenate([ref[1] for ref in pre], axis=0)
    gate_pre_ref[...] = gate_pre
    up_pre_ref[...] = up_pre
    total = mm(gate_pre, gate_ref[...], ((1,), (1,))) + mm(up_pre, up_ref[...], ((1,), (1,)))
    rows = total.astype(BF16)
    part = rows.shape[0] // dp
    parts = [rows[k * part : (k + 1) * part] for k in range(dp)]
    store_cores(keep_ref, swap_ref, natural_order(parts, scratch), 0)


def grads_kernel(count, cuts, *refs):
    left_refs, refs = refs[:cuts], refs[cuts:]
    left = jnp.concatenate([ref[...] for ref in left_refs], axis=0).T
    right_refs, out_refs = refs[: -count], refs[-count:]
    each = len(right_refs) // count
    for k, out_ref in enumerate(out_refs):
        right = jnp.concatenate([ref[...] for ref in right_refs[k * each : (k + 1) * each]], axis=0)
        out_ref[...] = mm(left, right, ((1,), (0,))).astype(BF16)


def pairs_after(blocks, refs):
    return jnp.concatenate(blocks + pair_pieces(refs), axis=0)


def scatter_scaled_kernel(pick_ref, weight_ref, keep_ref, swap_ref, *refs):
    back = pairs_after([keep_ref[0], swap_ref[0]], refs[:-1])
    scaled = (weight_ref[...] * back.astype(F32)).astype(BF16)
    refs[-1][...] = mm(pick_ref[...], scaled, ((0,), (0,))).astype(BF16)


def scatter_kernel(pick_ref, keep_ref, swap_ref, *refs):
    back = pairs_after([keep_ref[0], swap_ref[0]], refs[:-1])
    refs[-1][...] = mm(pick_ref[...], back, ((0,), (0,))).astype(BF16)


def partner(value, axis, k):
    size = lax.axis_size(axis)
    return lax.ppermute(value, axis, [(i, i ^ k) for i in range(size)])


def exchange(value):
    return lax.all_to_all(value, "dp", split_axis=0, concat_axis=0, tiled=True)


def trade(values):
    far_first = reversed(range(1, len(values)))
    return [values[0]] + [partner(values[k], "dp", k) for k in far_first][::-1]


def body(tokens, grad_out, expert_ids, gates, w_gate, w_up, w_down):
    experts = lax.axis_size("expert")
    dp = lax.axis_size("dp")
    tok_rows, features = tokens.shape
    capacity = tok_rows // 16
    slots = experts * capacity
    hidden = w_gate.shape[2]
    chunk = slots // dp
    gate_mat, up_mat, down_mat = w_gate[0], w_up[0], w_down[0]
    shape = jax.ShapeDtypeStruct

    half = experts // 2
    early = half // 2 - 2
    part = slots // (2 * dp)
    product = 2 * slots * features * hidden
    sized = shape((slots, features), BF16)
    cut = shape((slots // 2, features), BF16)
    wide = shape((slots, hidden), BF16)
    cut_wide = shape((slots // 2, hidden), BF16)
    both = shape((2, half, capacity, features), BF16)
    one = shape((half, capacity, features), BF16)
    cut_one = shape((half // 2, capacity, features), BF16)
    near = shape((2, 2, capacity, features), BF16)
    pair = shape((2, capacity, features), BF16)
    far = [pair] * (half - 2)
    mine = shape((2, part, hidden), BF16)
    in_order = pltpu.VMEM((slots // 2, features), BF16)

    ins = (expert_ids.T, gates.T, tokens, grad_out)
    outs = (shape((slots, tok_rows), BF16), shape((slots, 1), F32), both, both)
    pick, weight, keep, swap = call(
        functools.partial(route_kernel, experts),
        outs,
        limit=ROUTE_LIMIT,
        in_specs=[ANY] * 4,
        scratch_shapes=[
            *[pltpu.VMEM(array.shape, array.dtype) for array in ins],
            pltpu.SemaphoreType.DMA((4,)),
        ],
    )(*ins)
    swap_to, up_mat = lax.optimization_barrier((swap, up_mat))
    swap = partner(swap_to, "expert", 1)
    up_mat = call(load_kernel, shape(up_mat.shape, BF16))(up_mat)
    swap, up_mat = lax.optimization_barrier((swap, up_mat))
    near_to, *far_to = call(functools.partial(pack_kernel, half), (near, *far, *far))(
        keep, swap
    )
    near_in = partner(near_to, "expert", 2)
    far_rows = [partner(far_to[k], "expert", 2 * (2 + k)) for k in range(half - 2)]
    far_grads = [partner(far_to[half - 2 + k], "expert", 2 * (2 + k)) for k in range(half - 2)]

    def gate_up(first, *found):
        return call(
            functools.partial(gate_up_kernel, dp, first),
            (cut, *([shape((dp, 2, part, hidden), BF16)] if first else [mine] * dp)),
            product,
            in_specs=[pl.BlockSpec() if first else ANY] + [pl.BlockSpec()] * (len(found) + 1),
            scratch_shapes=[in_order],
        )(*found, gate_mat, up_mat)

    rows_early, sums = gate_up(True, keep, swap, near_in, *far_rows[:early])
    sums_early = [exchange(sums)]
    rows_late, *sums = gate_up(False, rows_early, *far_rows[early:])
    sums_late = trade(sums)
    grads, *part_grad = call(
        functools.partial(grad_act_kernel, dp, early),
        (sized, *[shape((2, part, hidden), BF16)] * dp),
        product,
        scratch_shapes=[in_order, in_order],
    )(keep, swap, near_in, *far_grads, down_mat)
    grad_sums = trade(part_grad)
    act_mine = call(
        functools.partial(act_kernel, dp),
        shape((2, part, hidden), BF16),
        in_specs=[pl.BlockSpec()] * (dp + 1) + [ANY],
    )(*sums_early, *sums_late, grads)
    acts = trade([act_mine] * dp)
    act, out_keep, out_swap = call(
        functools.partial(expert_out_kernel, dp),
        (wide, one, one),
        product,
        in_specs=[pl.BlockSpec()] * (dp + 1) + [ANY] * (dp - 1),
        scratch_shapes=[in_order, in_order],
    )(*acts, down_mat, *grad_sums[1:])
    out_swap = partner(out_swap, "expert", 1)
    out_near_to, *out_far = call(functools.partial(pack_back_kernel, 1), [pair] * (half - 1))(
        out_keep, out_swap
    )
    out_far = [partner(value, "expert", 2 * (2 + k)) for k, value in enumerate(out_far)]

    def grad_pre(at, sums, *after):
        return call(
            functools.partial(grad_pre_kernel, dp, at, len(sums)),
            mine if at else shape((dp, 2, part, hidden), BF16),
            in_specs=[pl.BlockSpec()] * (len(sums) + dp) + [ANY] * len(after),
        )(*sums, *grad_sums, *after)

    def row_grad(pre, *after):
        return call(
            functools.partial(row_grad_kernel, dp, len(pre)),
            (cut_wide, cut_wide, cut_one, cut_one),
            product,
            in_specs=[pl.BlockSpec()] * (len(pre) + 2) + [ANY] * len(after),
            scratch_shapes=[in_order],
        )(*pre, gate_mat, up_mat, *after)

    pre_late = grad_pre(1, sums_late)
    pre_early = [exchange(grad_pre(0, sums_early, pre_late))]
    pre_late = trade([pre_late] * dp)
    gate_late, up_late, keep_late, swap_late = row_grad(pre_late, out_near_to)
    swap_late = partner(swap_late, "expert", 1)
    gate_early, up_early, keep_early, swap_early = row_grad(pre_early)
    late_to = call(
        functools.partial(pack_back_kernel, 0),
        [pair] * (half // 2),
        in_specs=[pl.BlockSpec()] * 2 + [ANY] * (len(out_far) + 1),
    )(keep_late, swap_late, *out_far, keep_early)
    late_back = [
        partner(value, "expert", 2 * (half // 2 + k)) for k, value in enumerate(late_to)
    ]
    swap_early = partner(swap_early, "expert", 1)
    out_near = partner(out_near_to, "expert", 2)
    early_to = call(functools.partial(pack_back_kernel, 1), [pair] * (half // 2 - 1))(
        keep_early, swap_early
    )
    early_back = [partner(value, "expert", 2 * (1 + k)) for k, value in enumerate(early_to)]

    (grad_down,) = call(
        functools.partial(grads_kernel, 1, 1), [shape((hidden, features), BF16)], product
    )(act, grads)
    grad_gate, grad_up = call(
        functools.partial(grads_kernel, 2, 2), [shape((features, hidden), BF16)] * 2, 2 * product
    )(rows_early, rows_late, gate_early, gate_late, up_early, up_late)

    full = shape((tok_rows, features), BF16)
    mixed = call(
        scatter_scaled_kernel, full
    )(pick, weight, out_keep, out_swap, out_near, *out_far)
    grad_tokens = call(
        scatter_kernel, full
    )(pick, keep_early, swap_early, *early_back, *late_back)
    return (mixed, grad_tokens, grad_gate[None], grad_up[None], grad_down[None])


def solution(mesh):
    placed = (
        P("expert", "dp"),
        P("expert", "dp"),
        P("expert", None),
        P("expert", None),
        P("expert", "dp", None),
        P("expert", "dp", None),
        P("expert", None, "dp"),
    )
    return jax.shard_map(
        body,
        mesh=mesh,
        in_specs=placed,
        out_specs=(
            P("expert", "dp"),
            P("expert", "dp"),
            P("expert", "dp", None),
            P("expert", "dp", None),
            P("expert", None, "dp"),
        ),
        check_vma=False,
    )
```

```python
import functools

import jax
import jax.numpy as jnp
from jax import lax
from jax.experimental import pallas as pl
from jax.experimental.pallas import tpu as pltpu
from jax.sharding import PartitionSpec as P

F32 = jnp.float32
BF16 = jnp.bfloat16
MIB = 1024 * 1024
ANY = pl.BlockSpec(memory_space=pl.ANY)
HERE = pl.BlockSpec()
VMEM_LIMIT = 24 * MIB
ROUTE_LIMIT = 59 * MIB


def mm(left, right, dims):
    return lax.dot_general(left, right, (dims, ((), ())), preferred_element_type=F32)


def call(kernel, out_shape, flops=0, moved=0, limit=VMEM_LIMIT, **kwargs):
    return pl.pallas_call(
        kernel,
        out_shape=out_shape,
        cost_estimate=pl.CostEstimate(flops=flops, bytes_accessed=moved, transcendentals=0),
        compiler_params=pltpu.CompilerParams(vmem_limit_bytes=limit),
        **kwargs,
    )


def split_rows(refs, value):
    rows = value.shape[0] // len(refs)
    for k, ref in enumerate(refs):
        ref[...] = value[k * rows : (k + 1) * rows]


def join_rows(refs):
    return jnp.concatenate([ref[...] for ref in refs], axis=0)


def split_cores(keep_ref, swap_ref, value, *at):
    half, rows = keep_ref.shape[-3:-1]
    for k in range(half):
        keep_ref[(*at, k)] = value[2 * k * rows : (2 * k + 1) * rows]
        swap_ref[(*at, k)] = value[(2 * k + 1) * rows : (2 * k + 2) * rows]


def route_kernel(experts, *refs):
    pick_ref, weight_ref, keep_ref, swap_ref = refs[4:8]
    ids_ref, gates_ref, tokens_ref, grad_ref, sems = refs[8:]
    copies = [
        pltpu.make_async_copy(refs[k], refs[8 + k], sems.at[k]) for k in range(4)
    ]
    for copy in copies:
        copy.start()
    copies[0].wait()
    copies[1].wait()
    ids = ids_ref[...]
    tok_rows = ids.shape[1]
    slots = pick_ref.shape[0]
    inside = ids < experts
    routed = jnp.max(inside.astype(jnp.int32), axis=0, keepdims=True)
    chosen = jnp.sum(jnp.where(inside, ids, 0), axis=0, keepdims=True)
    weight = jnp.sum(jnp.where(inside, gates_ref[...], 0.0), axis=0, keepdims=True)
    key = jnp.where(routed > 0, chosen ^ lax.axis_index("expert"), experts)
    hot = lax.broadcasted_iota(jnp.int32, (experts, tok_rows), 0) == key
    earlier = lax.broadcasted_iota(jnp.int32, (tok_rows, tok_rows), 0) < lax.broadcasted_iota(
        jnp.int32, (tok_rows, tok_rows), 1
    )
    before = mm(hot.astype(F32).astype(BF16), earlier.astype(F32).astype(BF16), ((1,), (0,)))
    position = jnp.sum(jnp.where(hot, before, 0.0), axis=0, keepdims=True).astype(jnp.int32)
    slot = jnp.where(routed > 0, key * (slots // experts) + position, slots)
    pick = lax.broadcasted_iota(jnp.int32, (slots, tok_rows), 0) == slot
    slot_weight = jnp.sum(jnp.where(pick, weight, 0.0), axis=1, keepdims=True)
    weight_ref[...] = slot_weight
    pick = pick.astype(F32).astype(BF16)
    pick_ref[...] = pick
    copies[2].wait()
    rows = mm(pick, tokens_ref[...], ((1,), (0,))).astype(BF16)
    split_cores(keep_ref, swap_ref, rows, 0)
    copies[3].wait()
    rows = (slot_weight * mm(pick, grad_ref[...], ((1,), (0,)))).astype(BF16)
    split_cores(keep_ref, swap_ref, rows, 1)


def load_kernel(from_ref, to_ref):
    to_ref[...] = from_ref[...]


def pack_kernel(half, keep_ref, swap_ref, near_ref, *far_refs):
    for at in range(2):
        near_ref[at, 0] = keep_ref[at, 1]
        near_ref[at, 1] = swap_ref[at, 1]
        for k in range(2, half):
            far_refs[at * (half - 2) + k - 2][0] = keep_ref[at, k]
            far_refs[at * (half - 2) + k - 2][1] = swap_ref[at, k]


def pack_back_kernel(keep_ref, swap_ref, *out_refs):
    for k, out_ref in enumerate(out_refs):
        out_ref[0] = keep_ref[k + 1]
        out_ref[1] = swap_ref[k + 1]


def pieces(at, keep_ref, swap_ref, *refs):
    far_refs, near_ref = refs[:-1], refs[-1]
    found = [keep_ref[at, 0], swap_ref[at, 0], near_ref[at, 0], near_ref[at, 1]]
    for ref in far_refs[::-1]:
        found += [ref[0], ref[1]]
    return found


def chunk_rows(rows, dp, k):
    chunk = rows // dp
    mine = lax.axis_index("dp")
    return pl.ds(pl.multiple_of((mine ^ k) * chunk, chunk), chunk)


def local_order(found, scratch, dp):
    scratch[...] = jnp.concatenate(found, axis=0)
    rows = scratch.shape[0]
    return jnp.concatenate([scratch[chunk_rows(rows, dp, k), :] for k in range(dp)], axis=0)


def gate_up_kernel(half, *refs):
    gate_ref, up_ref, local_ref, *out_refs, scratch = refs[half + 1 :]
    dp = len(out_refs)
    rows = local_order(pieces(0, *refs[: half + 1]), scratch, dp)
    local_ref[...] = rows
    chunk = rows.shape[0] // dp
    for at, mat in enumerate((gate_ref, up_ref)):
        part = mm(rows, mat[...], ((1,), (0,))).astype(BF16)
        for k, out_ref in enumerate(out_refs):
            out_ref[at] = part[k * chunk : (k + 1) * chunk]


def grad_act_kernel(half, *refs):
    down_ref, local_ref, *out_refs, scratch = refs[half + 1 :]
    dp = len(out_refs)
    rows = local_order(pieces(1, *refs[: half + 1]), scratch, dp)
    local_ref[...] = rows
    split_rows(out_refs, mm(rows, down_ref[...], ((1,), (1,))).astype(BF16))


def group_sum(refs, *at):
    total = refs[0][at].astype(F32)
    for ref in refs[1:]:
        total = total + ref[at].astype(F32)
    return total


def logistic(value):
    return 1.0 / (1.0 + jnp.exp(-value))


def act_kernel(dp, *refs):
    gate = group_sum(refs[:dp], 0)
    up = group_sum(refs[:dp], 1)
    refs[dp][...] = (gate * logistic(gate) * up).astype(BF16)


def grad_pre_kernel(dp, *refs):
    gate = group_sum(refs[:dp], 0)
    up = group_sum(refs[:dp], 1)
    grad = group_sum(refs[dp : 2 * dp], Ellipsis)
    out_ref = refs[2 * dp]
    soft = logistic(gate)
    out_ref[0] = (grad * up * (soft * (1.0 + gate * (1.0 - soft)))).astype(BF16)
    out_ref[1] = (grad * (gate * soft)).astype(BF16)


def send_back(keep_ref, swap_ref, scratch, rows, dp):
    chunk = rows.shape[0] // dp
    for k in range(dp):
        scratch[chunk_rows(rows.shape[0], dp, k), :] = rows[k * chunk : (k + 1) * chunk]
    split_cores(keep_ref, swap_ref, scratch[...])


def expert_out_kernel(dp, *refs):
    down_ref, act_ref, keep_ref, swap_ref, scratch = refs[dp:]
    act = join_rows(refs[:dp])
    act_ref[...] = act
    rows = mm(act, down_ref[...], ((1,), (0,))).astype(BF16)
    send_back(keep_ref, swap_ref, scratch, rows, dp)


def row_grad_kernel(dp, *refs):
    gate_ref, up_ref, gate_pre_ref, up_pre_ref, keep_ref, swap_ref, scratch = refs[dp:]
    gate_pre = jnp.concatenate([ref[0] for ref in refs[:dp]], axis=0)
    up_pre = jnp.concatenate([ref[1] for ref in refs[:dp]], axis=0)
    gate_pre_ref[...] = gate_pre
    up_pre_ref[...] = up_pre
    total = mm(gate_pre, gate_ref[...], ((1,), (1,))) + mm(up_pre, up_ref[...], ((1,), (1,)))
    send_back(keep_ref, swap_ref, scratch, total.astype(BF16), dp)


def returned(keep_ref, swap_ref, refs):
    found = [keep_ref[0], swap_ref[0]]
    for ref in refs[::-1]:
        found += [ref[0], ref[1]]
    return jnp.concatenate(found, axis=0)


def scatter_scaled_kernel(half, pick_ref, weight_ref, *refs):
    back = returned(*refs[:2], refs[2 : half + 1]).astype(F32)
    scaled = (weight_ref[...] * back).astype(BF16)
    refs[-1][...] = mm(pick_ref[...], scaled, ((0,), (0,))).astype(BF16)


def scatter_kernel(half, pick_ref, *refs):
    back = returned(*refs[:2], refs[2 : half + 1])
    refs[-1][...] = mm(pick_ref[...], back, ((0,), (0,))).astype(BF16)


def grads_kernel(count, left_ref, *refs):
    left = left_ref[...].T
    for right_ref, out_ref in zip(refs[:count], refs[-count:]):
        out_ref[...] = mm(left, right_ref[...], ((1,), (0,))).astype(BF16)


def partner(value, axis, k):
    size = lax.axis_size(axis)
    return lax.ppermute(value, axis, [(i, i ^ k) for i in range(size)])


def trade(values):
    far_first = reversed(range(1, len(values)))
    return [values[0]] + [partner(values[k], "dp", k) for k in far_first][::-1]


def body(tokens, grad_out, expert_ids, gates, w_gate, w_up, w_down):
    experts = lax.axis_size("expert")
    dp = lax.axis_size("dp")
    tok_rows, features = tokens.shape
    capacity = tok_rows // 16
    slots = experts * capacity
    hidden = w_gate.shape[2]
    chunk = slots // dp
    gate_mat, up_mat, down_mat = w_gate[0], w_up[0], w_down[0]
    shape = jax.ShapeDtypeStruct
    product = 2 * slots * features * hidden
    weights = 2 * features * hidden

    half = experts // 2
    sized = shape((slots, features), BF16)
    wide = shape((slots, hidden), BF16)
    both = shape((2, half, capacity, features), BF16)
    one = shape((half, capacity, features), BF16)
    near = shape((2, 2, capacity, features), BF16)
    far = [shape((2, capacity, features), BF16)] * (half - 2)
    in_order = [pltpu.VMEM((slots, features), BF16)]

    ins = (expert_ids.T, gates.T, tokens, grad_out)
    outs = (shape((slots, tok_rows), BF16), shape((slots, 1), F32), both, both)
    pick, weight, keep, swap = call(
        functools.partial(route_kernel, experts),
        outs,
        4 * slots * tok_rows * features,
        8 * tok_rows * features,
        limit=ROUTE_LIMIT,
        in_specs=[ANY] * 4,
        scratch_shapes=[
            *[pltpu.VMEM(array.shape, array.dtype) for array in ins],
            pltpu.SemaphoreType.DMA((4,)),
        ],
    )(*ins)
    swap_to, up_mat = lax.optimization_barrier((swap, up_mat))
    swap = partner(swap_to, "expert", 1)
    up_mat = call(load_kernel, shape(up_mat.shape, BF16), 0, 2 * weights)(up_mat)
    swap, up_mat = lax.optimization_barrier((swap, up_mat))
    near_to, *far_to = call(functools.partial(pack_kernel, half), (near, *far, *far), 0, 8 * slots)(
        keep, swap
    )
    far_rows = [partner(far_to[k], "expert", 2 * (2 + k)) for k in reversed(range(half - 2))][::-1]
    near_in = partner(near_to, "expert", 2)
    far_grads = [partner(far_to[half - 2 + k], "expert", 2 * (2 + k)) for k in range(half - 2)]
    rows, *part_pre = call(
        functools.partial(gate_up_kernel, half),
        (sized, *[shape((2, chunk, hidden), BF16)] * dp),
        2 * product,
        2 * weights,
        scratch_shapes=in_order,
    )(keep, swap, *far_rows[::-1], near_in, gate_mat, up_mat)
    sums = trade(part_pre)
    act_mine = call(
        functools.partial(act_kernel, dp),
        shape((chunk, hidden), BF16),
        0,
        4 * dp * chunk * hidden,
    )(*sums)
    acts = trade([act_mine] * dp)
    far_grads, act_mine = lax.optimization_barrier((far_grads, act_mine))
    grads, *part_grad = call(
        functools.partial(grad_act_kernel, half),
        (sized, *[shape((chunk, hidden), BF16)] * dp),
        product,
        weights,
        scratch_shapes=in_order,
    )(keep, swap, *far_grads[::-1], near_in, down_mat)
    grad_sums = trade(part_grad)
    pre_mine = call(
        functools.partial(grad_pre_kernel, dp),
        shape((2, chunk, hidden), BF16),
        0,
        6 * dp * chunk * hidden,
    )(*sums, *grad_sums)
    pre = trade([pre_mine] * dp)
    act, out_keep, out_swap = call(
        functools.partial(expert_out_kernel, dp),
        (wide, one, one),
        product,
        weights,
        scratch_shapes=in_order,
    )(*acts, down_mat)
    back = [far[0]] * (half - 1)
    out_swap = partner(out_swap, "expert", 1)
    out_near, *out_far = call(pack_back_kernel, back, 0, 8 * slots)(out_keep, out_swap)
    out_far = [partner(value, "expert", 2 * (2 + k)) for k, value in enumerate(out_far)]
    pre, out_far = lax.optimization_barrier((pre, out_far))
    gate_pre, up_pre, grad_keep, grad_swap = call(
        functools.partial(row_grad_kernel, dp),
        (wide, wide, one, one),
        2 * product,
        2 * weights,
        scratch_shapes=in_order,
    )(*pre, gate_mat, up_mat)
    grad_swap = partner(grad_swap, "expert", 1)
    out_near = partner(out_near, "expert", 2)
    grad_to = call(pack_back_kernel, back, 0, 8 * slots)(grad_keep, grad_swap)
    grad_back = [partner(value, "expert", 2 * (1 + k)) for k, value in enumerate(grad_to)]

    (grad_down,) = call(
        functools.partial(grads_kernel, 1),
        [shape((hidden, features), BF16)],
        product,
        weights,
    )(act, grads)
    grad_gate, grad_up = call(
        functools.partial(grads_kernel, 2),
        [shape((features, hidden), BF16)] * 2,
        2 * product,
        2 * weights,
        in_specs=[HERE] * 3 + [ANY],
    )(rows, gate_pre, up_pre, grad_to[0])

    full = shape((tok_rows, features), BF16)
    mixed = call(
        functools.partial(scatter_scaled_kernel, half),
        full,
        2 * slots * tok_rows * features,
        4 * tok_rows * features,
        in_specs=[HERE] * (half + 3) + [ANY],
    )(pick, weight, out_keep, out_swap, *out_far[::-1], out_near, grad_to[0])
    grad_tokens = call(
        functools.partial(scatter_kernel, half),
        full,
        2 * slots * tok_rows * features,
        4 * tok_rows * features,
    )(pick, grad_keep, grad_swap, *grad_back[::-1])
    return (mixed, grad_tokens, grad_gate[None], grad_up[None], grad_down[None])


def solution(mesh):
    placed = (
        P("expert", "dp"),
        P("expert", "dp"),
        P("expert", None),
        P("expert", None),
        P("expert", "dp", None),
        P("expert", "dp", None),
        P("expert", None, "dp"),
    )
    return jax.shard_map(
        body,
        mesh=mesh,
        in_specs=placed,
        out_specs=(
            P("expert", "dp"),
            P("expert", "dp"),
            P("expert", "dp", None),
            P("expert", "dp", None),
            P("expert", None, "dp"),
        ),
        check_vma=False,
    )
```

```python
import functools

import jax
import jax.numpy as jnp
from jax import lax
from jax.experimental import pallas as pl
from jax.experimental.pallas import tpu as pltpu
from jax.sharding import PartitionSpec as P

F32 = jnp.float32
BF16 = jnp.bfloat16
MIB = 1024 * 1024
ANY = pl.BlockSpec(memory_space=pl.ANY)
HERE = pl.BlockSpec()
VMEM_LIMIT = 24 * MIB
ROUTE_LIMIT = 59 * MIB


def mm(left, right, dims):
    return lax.dot_general(left, right, (dims, ((), ())), preferred_element_type=F32)


def call(kernel, out_shape, flops=0, moved=0, limit=VMEM_LIMIT, **kwargs):
    return pl.pallas_call(
        kernel,
        out_shape=out_shape,
        cost_estimate=pl.CostEstimate(flops=flops, bytes_accessed=moved, transcendentals=0),
        compiler_params=pltpu.CompilerParams(vmem_limit_bytes=limit),
        **kwargs,
    )


def split_rows(refs, value):
    rows = value.shape[0] // len(refs)
    for k, ref in enumerate(refs):
        ref[...] = value[k * rows : (k + 1) * rows]


def join_rows(refs):
    return jnp.concatenate([ref[...] for ref in refs], axis=0)


def split_cores(keep_ref, swap_ref, value, *at):
    half, rows = keep_ref.shape[-3:-1]
    for k in range(half):
        keep_ref[(*at, k)] = value[2 * k * rows : (2 * k + 1) * rows]
        swap_ref[(*at, k)] = value[(2 * k + 1) * rows : (2 * k + 2) * rows]


def route_kernel(experts, *refs):
    pick_ref, weight_ref, keep_ref, swap_ref = refs[4:8]
    ids_ref, gates_ref, tokens_ref, grad_ref, sems = refs[8:]
    copies = [
        pltpu.make_async_copy(refs[k], refs[8 + k], sems.at[k]) for k in range(4)
    ]
    for copy in copies:
        copy.start()
    copies[0].wait()
    copies[1].wait()
    ids = ids_ref[...]
    tok_rows = ids.shape[1]
    slots = pick_ref.shape[0]
    inside = ids < experts
    routed = jnp.max(inside.astype(jnp.int32), axis=0, keepdims=True)
    chosen = jnp.sum(jnp.where(inside, ids, 0), axis=0, keepdims=True)
    weight = jnp.sum(jnp.where(inside, gates_ref[...], 0.0), axis=0, keepdims=True)
    key = jnp.where(routed > 0, chosen ^ lax.axis_index("expert"), experts)
    hot = lax.broadcasted_iota(jnp.int32, (experts, tok_rows), 0) == key
    earlier = lax.broadcasted_iota(jnp.int32, (tok_rows, tok_rows), 0) < lax.broadcasted_iota(
        jnp.int32, (tok_rows, tok_rows), 1
    )
    before = mm(hot.astype(F32).astype(BF16), earlier.astype(F32).astype(BF16), ((1,), (0,)))
    position = jnp.sum(jnp.where(hot, before, 0.0), axis=0, keepdims=True).astype(jnp.int32)
    slot = jnp.where(routed > 0, key * (slots // experts) + position, slots)
    pick = lax.broadcasted_iota(jnp.int32, (slots, tok_rows), 0) == slot
    slot_weight = jnp.sum(jnp.where(pick, weight, 0.0), axis=1, keepdims=True)
    weight_ref[...] = slot_weight
    pick = pick.astype(F32).astype(BF16)
    pick_ref[...] = pick
    copies[2].wait()
    rows = mm(pick, tokens_ref[...], ((1,), (0,))).astype(BF16)
    split_cores(keep_ref, swap_ref, rows, 0)
    copies[3].wait()
    rows = (slot_weight * mm(pick, grad_ref[...], ((1,), (0,)))).astype(BF16)
    split_cores(keep_ref, swap_ref, rows, 1)


def load_kernel(*refs):
    half = len(refs) // 2
    for from_ref, to_ref in zip(refs[:half], refs[half:]):
        to_ref[...] = from_ref[...]


def pack_kernel(keep_ref, swap_ref, *out_refs):
    for k, out_ref in enumerate(out_refs):
        for at in range(2):
            out_ref[at, 0] = keep_ref[at, k + 1]
            out_ref[at, 1] = swap_ref[at, k + 1]


def pack_back_kernel(keep_ref, swap_ref, *out_refs):
    for k, out_ref in enumerate(out_refs):
        out_ref[0] = keep_ref[k + 1]
        out_ref[1] = swap_ref[k + 1]


def part_rows(rows, dp, k):
    part = rows // dp
    mine = lax.axis_index("dp")
    return pl.ds(pl.multiple_of((mine ^ k) * part, part), part)


def local_order(found, scratch, dp):
    scratch[...] = jnp.concatenate(found, axis=0)
    rows = scratch.shape[0]
    return jnp.concatenate([scratch[part_rows(rows, dp, k), :] for k in range(dp)], axis=0)


def natural_order(parts, scratch):
    for k, part in enumerate(parts):
        scratch[part_rows(scratch.shape[0], len(parts), k), :] = part
    return scratch[...]


def partial_kernel(dp, own, count, *refs):
    gate_ref, up_ref, down_ref = refs[count : count + 3]
    rows_ref, grads_ref, *out_refs, scratch = refs[-dp - 3 :]
    local = []
    for at in range(2):
        found = [ref[at, 0] for ref in refs[:2]] if own else []
        found += [ref[at, k] for ref in refs[2 * own : count] for k in range(2)]
        local.append(local_order(found, scratch, dp))
    rows_ref[...], grads_ref[...] = local
    part = scratch.shape[0] // dp
    for at, (left, mat, dims) in enumerate(
        (
            (local[0], gate_ref, ((1,), (0,))),
            (local[0], up_ref, ((1,), (0,))),
            (local[1], down_ref, ((1,), (1,))),
        )
    ):
        sums = mm(left, mat[...], dims).astype(BF16)
        for k, out_ref in enumerate(out_refs):
            out_ref[at] = sums[k * part : (k + 1) * part]


def group_sum(refs, at):
    total = refs[0][at].astype(F32)
    for ref in refs[1:]:
        total = total + ref[at].astype(F32)
    return total


def logistic(value):
    return 1.0 / (1.0 + jnp.exp(-value))


def act_kernel(dp, *refs):
    for at in range(2):
        sums = refs[at * dp : (at + 1) * dp]
        gate = group_sum(sums, 0)
        refs[-1][at] = (gate * logistic(gate) * group_sum(sums, 1)).astype(BF16)


def grad_pre_kernel(dp, *refs):
    out_ref = refs[-1]
    for at in range(2):
        sums = refs[at * dp : (at + 1) * dp]
        gate, up, grad = [group_sum(sums, k) for k in range(3)]
        soft = logistic(gate)
        out_ref[0, at] = (grad * up * (soft * (1.0 + gate * (1.0 - soft)))).astype(BF16)
        out_ref[1, at] = (grad * (gate * soft)).astype(BF16)


def send_back(keep_ref, swap_ref, scratch, rows, dp):
    part = rows.shape[0] // (2 * dp)
    half, block = keep_ref.shape[:2]
    parts = [rows[k * part : (k + 1) * part] for k in range(2 * dp)]
    for at in range(2):
        value = natural_order(parts[at * dp : (at + 1) * dp], scratch)
        for k in range(half // 2):
            keep_ref[at * half // 2 + k] = value[2 * k * block : (2 * k + 1) * block]
            swap_ref[at * half // 2 + k] = value[(2 * k + 1) * block : (2 * k + 2) * block]


def expert_out_kernel(dp, *refs):
    down_ref, act_ref, keep_ref, swap_ref, scratch = refs[dp:]
    act = jnp.concatenate([ref[at] for at in range(2) for ref in refs[:dp]], axis=0)
    act_ref[...] = act
    rows = mm(act, down_ref[...], ((1,), (0,))).astype(BF16)
    send_back(keep_ref, swap_ref, scratch, rows, dp)


def row_grad_kernel(dp, *refs):
    gate_ref, up_ref, gate_pre_ref, up_pre_ref, keep_ref, swap_ref, scratch = refs[dp:]
    gate_pre, up_pre = [
        jnp.concatenate([ref[k, at] for at in range(2) for ref in refs[:dp]], axis=0)
        for k in range(2)
    ]
    gate_pre_ref[...] = gate_pre
    up_pre_ref[...] = up_pre
    total = mm(gate_pre, gate_ref[...], ((1,), (1,))) + mm(up_pre, up_ref[...], ((1,), (1,)))
    send_back(keep_ref, swap_ref, scratch, total.astype(BF16), dp)


def returned(keep_ref, swap_ref, refs):
    found = [keep_ref[0], swap_ref[0]]
    for ref in refs[::-1]:
        found += [ref[0], ref[1]]
    return jnp.concatenate(found, axis=0)


def scatter_scaled_kernel(half, pick_ref, weight_ref, *refs):
    back = returned(*refs[:2], refs[2 : half + 1]).astype(F32)
    scaled = (weight_ref[...] * back).astype(BF16)
    refs[-1][...] = mm(pick_ref[...], scaled, ((0,), (0,))).astype(BF16)


def scatter_kernel(half, pick_ref, *refs):
    back = returned(*refs[:2], refs[2 : half + 1])
    refs[-1][...] = mm(pick_ref[...], back, ((0,), (0,))).astype(BF16)


def grad_down_kernel(act_ref, early_ref, late_ref, out_ref):
    right = join_rows([early_ref, late_ref])
    out_ref[...] = mm(act_ref[...].T, right, ((1,), (0,))).astype(BF16)


def grad_gate_up_kernel(early_ref, late_ref, gate_pre_ref, up_pre_ref, _, gate_ref, up_ref):
    left = join_rows([early_ref, late_ref]).T
    for right_ref, out_ref in ((gate_pre_ref, gate_ref), (up_pre_ref, up_ref)):
        out_ref[...] = mm(left, right_ref[...], ((1,), (0,))).astype(BF16)


def partner(value, axis, k):
    size = lax.axis_size(axis)
    return lax.ppermute(value, axis, [(i, i ^ k) for i in range(size)])


def trade(values):
    far_first = reversed(range(1, len(values)))
    return [values[0]] + [partner(values[k], "dp", k) for k in far_first][::-1]


def body(tokens, grad_out, expert_ids, gates, w_gate, w_up, w_down):
    experts = lax.axis_size("expert")
    dp = lax.axis_size("dp")
    tok_rows, features = tokens.shape
    capacity = tok_rows // 16
    slots = experts * capacity
    hidden = w_gate.shape[2]
    chunk = slots // dp
    gate_mat, up_mat, down_mat = w_gate[0], w_up[0], w_down[0]
    shape = jax.ShapeDtypeStruct
    product = 2 * slots * features * hidden
    weights = 2 * features * hidden

    half = experts // 2
    early = half // 2
    part = chunk // 2
    sized = shape((slots, features), BF16)
    cut = shape((slots // 2, features), BF16)
    wide = shape((slots, hidden), BF16)
    both = shape((2, half, capacity, features), BF16)
    one = shape((half, capacity, features), BF16)
    pair = shape((2, capacity, features), BF16)
    pairs = shape((2, 2, capacity, features), BF16)
    in_order = [pltpu.VMEM((slots // 2, features), BF16)]

    ins = (expert_ids.T, gates.T, tokens, grad_out)
    outs = (shape((slots, tok_rows), BF16), shape((slots, 1), F32), both, both)
    pick, weight, keep, swap = call(
        functools.partial(route_kernel, experts),
        outs,
        4 * slots * tok_rows * features,
        8 * tok_rows * features,
        limit=ROUTE_LIMIT,
        in_specs=[ANY] * 4,
        scratch_shapes=[
            *[pltpu.VMEM(array.shape, array.dtype) for array in ins],
            pltpu.SemaphoreType.DMA((4,)),
        ],
    )(*ins)
    swap_to, up_mat, down_mat = lax.optimization_barrier((swap, up_mat, down_mat))
    swap = partner(swap_to, "expert", 1)
    up_mat, down_mat = call(
        load_kernel, (shape(up_mat.shape, BF16), shape(down_mat.shape, BF16)), 0, 4 * weights
    )(up_mat, down_mat)
    swap, up_mat, down_mat = lax.optimization_barrier((swap, up_mat, down_mat))
    mats = (gate_mat, up_mat, down_mat)
    sent = call(pack_kernel, [pairs] * (half - 1), 0, 8 * slots)(keep, swap)
    arrived = [partner(value, "expert", 2 * (1 + k)) for k, value in enumerate(sent)]

    def partial_sums(own, found, *after):
        return call(
            functools.partial(partial_kernel, dp, own, len(found)),
            (cut, cut, *[shape((3, part, hidden), BF16)] * dp),
            3 * product // 2,
            3 * weights,
            in_specs=[HERE] * (len(found) + 3) + [ANY] * len(after),
            scratch_shapes=in_order,
        )(*found, *mats, *after)

    rows_early, grads_early, *sums = partial_sums(True, (keep, swap, *arrived[: early - 1]))
    sums_early = trade(sums)
    rows_late, grads_late, *sums = partial_sums(False, arrived[early - 1 :], rows_early)
    sums_late = trade(sums)
    act_mine = call(
        functools.partial(act_kernel, dp), shape((2, part, hidden), BF16), 0, 4 * slots * hidden
    )(*sums_early, *sums_late)
    acts = trade([act_mine] * dp)
    pre_mine = call(
        functools.partial(grad_pre_kernel, dp),
        shape((2, 2, part, hidden), BF16),
        0,
        6 * slots * hidden,
    )(*sums_early, *sums_late)
    pre = trade([pre_mine] * dp)
    act, out_keep, out_swap = call(
        functools.partial(expert_out_kernel, dp),
        (wide, one, one),
        product,
        weights,
        scratch_shapes=in_order,
    )(*acts, down_mat)
    back = [pair] * (half - 1)
    out_swap = partner(out_swap, "expert", 1)
    out_near, *out_far = call(pack_back_kernel, back, 0, 8 * slots)(out_keep, out_swap)
    out_far = [partner(value, "expert", 2 * (2 + k)) for k, value in enumerate(out_far)]
    pre, out_far = lax.optimization_barrier((pre, out_far))
    gate_pre, up_pre, grad_keep, grad_swap = call(
        functools.partial(row_grad_kernel, dp),
        (wide, wide, one, one),
        2 * product,
        2 * weights,
        scratch_shapes=in_order,
    )(*pre, gate_mat, up_mat)
    grad_swap = partner(grad_swap, "expert", 1)
    out_near = partner(out_near, "expert", 2)
    grad_to = call(pack_back_kernel, back, 0, 8 * slots)(grad_keep, grad_swap)
    grad_back = [partner(value, "expert", 2 * (1 + k)) for k, value in enumerate(grad_to)]

    grad_down = call(
        grad_down_kernel, shape((hidden, features), BF16), product, weights
    )(act, grads_early, grads_late)
    grad_gate, grad_up = call(
        grad_gate_up_kernel,
        [shape((features, hidden), BF16)] * 2,
        2 * product,
        2 * weights,
        in_specs=[HERE] * 4 + [ANY],
    )(rows_early, rows_late, gate_pre, up_pre, grad_to[0])

    full = shape((tok_rows, features), BF16)
    mixed = call(
        functools.partial(scatter_scaled_kernel, half),
        full,
        2 * slots * tok_rows * features,
        4 * tok_rows * features,
        in_specs=[HERE] * (half + 3) + [ANY],
    )(pick, weight, out_keep, out_swap, *out_far[::-1], out_near, grad_to[0])
    grad_tokens = call(
        functools.partial(scatter_kernel, half),
        full,
        2 * slots * tok_rows * features,
        4 * tok_rows * features,
    )(pick, grad_keep, grad_swap, *grad_back[::-1])
    return (mixed, grad_tokens, grad_gate[None], grad_up[None], grad_down[None])


def solution(mesh):
    placed = (
        P("expert", "dp"),
        P("expert", "dp"),
        P("expert", None),
        P("expert", None),
        P("expert", "dp", None),
        P("expert", "dp", None),
        P("expert", None, "dp"),
    )
    return jax.shard_map(
        body,
        mesh=mesh,
        in_specs=placed,
        out_specs=(
            P("expert", "dp"),
            P("expert", "dp"),
            P("expert", "dp", None),
            P("expert", "dp", None),
            P("expert", None, "dp"),
        ),
        check_vma=False,
    )
```

```python
import functools

import jax
import jax.numpy as jnp
from jax import lax
from jax.experimental import pallas as pl
from jax.experimental.pallas import tpu as pltpu
from jax.sharding import PartitionSpec as P

F32 = jnp.float32
BF16 = jnp.bfloat16
MIB = 1024 * 1024
ANY = pl.BlockSpec(memory_space=pl.ANY)
HERE = pl.BlockSpec()
VMEM_LIMIT = 24 * MIB
STAGE = 2 * 10**10
ROUTE_LIMIT = 59 * MIB


def mm(left, right, dims):
    return lax.dot_general(left, right, (dims, ((), ())), preferred_element_type=F32)


def call(kernel, out_shape, flops=0, moved=0, limit=VMEM_LIMIT, **kwargs):
    return pl.pallas_call(
        kernel,
        out_shape=out_shape,
        cost_estimate=pl.CostEstimate(flops=flops, bytes_accessed=moved, transcendentals=0),
        compiler_params=pltpu.CompilerParams(vmem_limit_bytes=limit),
        **kwargs,
    )


def split_rows(refs, value):
    rows = value.shape[0] // len(refs)
    for k, ref in enumerate(refs):
        ref[...] = value[k * rows : (k + 1) * rows]


def join_rows(refs):
    return jnp.concatenate([ref[...] for ref in refs], axis=0)


def split_cores(keep_ref, swap_ref, value, *at):
    half, rows = keep_ref.shape[-3:-1]
    for k in range(half):
        keep_ref[(*at, k)] = value[2 * k * rows : (2 * k + 1) * rows]
        swap_ref[(*at, k)] = value[(2 * k + 1) * rows : (2 * k + 2) * rows]


def own_blocks(own_refs, value):
    for k, own_ref in enumerate(own_refs):
        rows = own_ref.shape[0]
        own_ref[...] = value[(2 * k + 4) * rows : (2 * k + 5) * rows]


def route_kernel(experts, *refs):
    pick_ref, weight_ref, keep_ref, swap_ref, *own_refs = refs[4:-5]
    ids_ref, gates_ref, tokens_ref, grad_ref, sems = refs[-5:]
    copies = [
        pltpu.make_async_copy(refs[k], refs[k - 5], sems.at[k]) for k in range(4)
    ]
    for copy in copies:
        copy.start()
    copies[0].wait()
    copies[1].wait()
    ids = ids_ref[...]
    tok_rows = ids.shape[1]
    slots = pick_ref.shape[0]
    inside = ids < experts
    routed = jnp.max(inside.astype(jnp.int32), axis=0, keepdims=True)
    chosen = jnp.sum(jnp.where(inside, ids, 0), axis=0, keepdims=True)
    weight = jnp.sum(jnp.where(inside, gates_ref[...], 0.0), axis=0, keepdims=True)
    key = jnp.where(routed > 0, chosen ^ lax.axis_index("expert"), experts)
    hot = lax.broadcasted_iota(jnp.int32, (experts, tok_rows), 0) == key
    earlier = lax.broadcasted_iota(jnp.int32, (tok_rows, tok_rows), 0) < lax.broadcasted_iota(
        jnp.int32, (tok_rows, tok_rows), 1
    )
    before = mm(hot.astype(F32).astype(BF16), earlier.astype(F32).astype(BF16), ((1,), (0,)))
    position = jnp.sum(jnp.where(hot, before, 0.0), axis=0, keepdims=True).astype(jnp.int32)
    slot = jnp.where(routed > 0, key * (slots // experts) + position, slots)
    pick = lax.broadcasted_iota(jnp.int32, (slots, tok_rows), 0) == slot
    slot_weight = jnp.sum(jnp.where(pick, weight, 0.0), axis=1, keepdims=True)
    weight_ref[...] = slot_weight
    pick = pick.astype(F32).astype(BF16)
    pick_ref[...] = pick
    copies[2].wait()
    rows = mm(pick, tokens_ref[...], ((1,), (0,))).astype(BF16)
    split_cores(keep_ref, swap_ref, rows, 0)
    own_blocks(own_refs, rows)
    copies[3].wait()
    rows = (slot_weight * mm(pick, grad_ref[...], ((1,), (0,)))).astype(BF16)
    split_cores(keep_ref, swap_ref, rows, 1)


def load_kernel(from_ref, to_ref):
    to_ref[...] = from_ref[...]


def stage_kernel(*refs):
    rows = refs[0].shape[0]
    refs[-1][...] = join_rows(refs[: refs[-1].shape[0] // rows])


def pack_kernel(half, keep_ref, swap_ref, near_ref, *far_refs):
    for at in range(2):
        near_ref[at, 0] = keep_ref[at, 1]
        near_ref[at, 1] = swap_ref[at, 1]
    for k in range(2, half):
        far_refs[k - 2][...] = swap_ref[0, k]
        far_refs[half + k - 4][0] = keep_ref[1, k]
        far_refs[half + k - 4][1] = swap_ref[1, k]


def pack_back_kernel(keep_ref, swap_ref, *out_refs):
    for k, out_ref in enumerate(out_refs):
        out_ref[0] = keep_ref[k + 2]
        out_ref[1] = swap_ref[k + 2]


def pack_last_kernel(out_keep_ref, out_swap_ref, keep_ref, swap_ref, near_ref, *far_refs):
    near_ref[0, 0] = out_keep_ref[1]
    near_ref[0, 1] = out_swap_ref[1]
    near_ref[1, 0] = keep_ref[1]
    near_ref[1, 1] = swap_ref[1]
    for k, far_ref in enumerate(far_refs):
        far_ref[...] = swap_ref[k + 2]


def rows_in_order(half, keep_ref, swap_ref, own_ref, *refs):
    far_refs, near_ref = refs[:-1], refs[-1]
    found = [keep_ref[0, 0], swap_ref[0, 0], near_ref[0, 0], near_ref[0, 1]]
    rows = far_refs[0].shape[0]
    for k in range(half - 2):
        found += [own_ref[k * rows : (k + 1) * rows], far_refs[k][...]]
    return found


def grads_in_order(keep_ref, swap_ref, *refs):
    far_refs, near_ref = refs[:-1], refs[-1]
    found = [keep_ref[1, 0], swap_ref[1, 0], near_ref[1, 0], near_ref[1, 1]]
    for ref in far_refs[::-1]:
        found += [ref[0], ref[1]]
    return found


def chunk_rows(rows, dp, k):
    chunk = rows // dp
    mine = lax.axis_index("dp")
    return pl.ds(pl.multiple_of((mine ^ k) * chunk, chunk), chunk)


def local_order(found, scratch, dp):
    scratch[...] = jnp.concatenate(found, axis=0)
    rows = scratch.shape[0]
    return jnp.concatenate([scratch[chunk_rows(rows, dp, k), :] for k in range(dp)], axis=0)


def gate_up_kernel(half, *refs):
    count = half + 2
    gate_ref, up_ref, local_ref, *out_refs, scratch = refs[count:]
    dp = len(out_refs)
    rows = local_order(rows_in_order(half, *refs[:count]), scratch, dp)
    local_ref[...] = rows
    chunk = rows.shape[0] // dp
    for at, mat in enumerate((gate_ref, up_ref)):
        part = mm(rows, mat[...], ((1,), (0,))).astype(BF16)
        for k, out_ref in enumerate(out_refs):
            out_ref[at] = part[k * chunk : (k + 1) * chunk]


def grad_act_kernel(half, *refs):
    down_ref, local_ref, *out_refs, scratch = refs[half + 1 :]
    dp = len(out_refs)
    rows = local_order(grads_in_order(*refs[: half + 1]), scratch, dp)
    local_ref[...] = rows
    split_rows(out_refs, mm(rows, down_ref[...], ((1,), (1,))).astype(BF16))


def group_sum(refs, *at):
    total = refs[0][at].astype(F32)
    for ref in refs[1:]:
        total = total + ref[at].astype(F32)
    return total


def logistic(value):
    return 1.0 / (1.0 + jnp.exp(-value))


def act_kernel(dp, *refs):
    gate = group_sum(refs[:dp], 0)
    up = group_sum(refs[:dp], 1)
    refs[dp][...] = (gate * logistic(gate) * up).astype(BF16)


def grad_pre_kernel(dp, *refs):
    gate = group_sum(refs[:dp], 0)
    up = group_sum(refs[:dp], 1)
    grad = group_sum(refs[dp : 2 * dp], Ellipsis)
    out_ref = refs[2 * dp]
    soft = logistic(gate)
    out_ref[0] = (grad * up * (soft * (1.0 + gate * (1.0 - soft)))).astype(BF16)
    out_ref[1] = (grad * (gate * soft)).astype(BF16)


def send_back(keep_ref, swap_ref, scratch, rows, dp):
    chunk = rows.shape[0] // dp
    for k in range(dp):
        scratch[chunk_rows(rows.shape[0], dp, k), :] = rows[k * chunk : (k + 1) * chunk]
    rows = scratch[...]
    split_cores(keep_ref, swap_ref, rows)
    return rows


def expert_out_kernel(dp, *refs):
    down_ref, act_ref, keep_ref, swap_ref, scratch = refs[dp:]
    act = join_rows(refs[:dp])
    act_ref[...] = act
    rows = mm(act, down_ref[...], ((1,), (0,))).astype(BF16)
    send_back(keep_ref, swap_ref, scratch, rows, dp)


def row_grad_kernel(dp, *refs):
    gate_ref, up_ref, gate_pre_ref, up_pre_ref, keep_ref, swap_ref, *own_refs, scratch = refs[dp:]
    gate_pre = jnp.concatenate([ref[0] for ref in refs[:dp]], axis=0)
    up_pre = jnp.concatenate([ref[1] for ref in refs[:dp]], axis=0)
    gate_pre_ref[...] = gate_pre
    up_pre_ref[...] = up_pre
    total = mm(gate_pre, gate_ref[...], ((1,), (1,))) + mm(up_pre, up_ref[...], ((1,), (1,)))
    own_blocks(own_refs, send_back(keep_ref, swap_ref, scratch, total.astype(BF16), dp))


def scatter_kernel(half, pick_ref, weight_ref, *refs):
    near_ref, mixed_ref, tokens_ref = refs[-3:]
    out_keep_ref, out_swap_ref, *out_refs = refs[:half]
    keep_ref, swap_ref, own_ref, *far_refs = refs[half:-3]
    outs = [out_keep_ref[0], out_swap_ref[0], near_ref[0, 0], near_ref[0, 1]]
    outs += [ref[k] for ref in out_refs for k in range(2)]
    found = [keep_ref[0], swap_ref[0], near_ref[1, 0], near_ref[1, 1]]
    rows = keep_ref.shape[1]
    for k in range(half - 2):
        found += [own_ref[k * rows : (k + 1) * rows], far_refs[k][...]]
    scaled = (weight_ref[...] * jnp.concatenate(outs, axis=0).astype(F32)).astype(BF16)
    pick = pick_ref[...].T
    mixed_ref[...] = mm(pick, scaled, ((1,), (0,))).astype(BF16)
    tokens_ref[...] = mm(pick, jnp.concatenate(found, axis=0), ((1,), (0,))).astype(BF16)


def grads_kernel(count, left_ref, *refs):
    left = left_ref[...].T
    *out_refs, token_ref = refs[-count - 1 :]
    for right_ref, out_ref in zip(refs[:count], out_refs):
        out_ref[...] = mm(left, right_ref[...], ((1,), (0,))).astype(BF16)
    token_ref[...] = jnp.zeros_like(token_ref)


def partner(value, axis, k):
    size = lax.axis_size(axis)
    return lax.ppermute(value, axis, [(i, i ^ k) for i in range(size)])


def trade(values):
    far_first = reversed(range(1, len(values)))
    return [values[0]] + [partner(values[k], "dp", k) for k in far_first][::-1]


def body(tokens, grad_out, expert_ids, gates, w_gate, w_up, w_down):
    experts = lax.axis_size("expert")
    dp = lax.axis_size("dp")
    tok_rows, features = tokens.shape
    capacity = tok_rows // 16
    slots = experts * capacity
    hidden = w_gate.shape[2]
    chunk = slots // dp
    gate_mat, up_mat, down_mat = w_gate[0], w_up[0], w_down[0]
    shape = jax.ShapeDtypeStruct
    product = 2 * slots * features * hidden
    weights = 2 * features * hidden

    half = experts // 2
    sized = shape((slots, features), BF16)
    token = shape((8, 128), F32)
    staged = shape(((half - 2) * capacity, features), BF16)
    wide = shape((slots, hidden), BF16)
    both = shape((2, half, capacity, features), BF16)
    one = shape((half, capacity, features), BF16)
    near = shape((2, 2, capacity, features), BF16)
    pair = shape((2, capacity, features), BF16)
    far = [pair] * (half - 2)
    in_order = [pltpu.VMEM((slots, features), BF16)]

    ins = (expert_ids.T, gates.T, tokens, grad_out)
    block = [shape((capacity, features), BF16)] * (half - 2)
    outs = (shape((slots, tok_rows), BF16), shape((slots, 1), F32), both, both, *block)
    pick, weight, keep, swap, *own_to = call(
        functools.partial(route_kernel, experts),
        outs,
        4 * slots * tok_rows * features,
        8 * tok_rows * features,
        limit=ROUTE_LIMIT,
        in_specs=[ANY] * 4,
        scratch_shapes=[
            *[pltpu.VMEM(array.shape, array.dtype) for array in ins],
            pltpu.SemaphoreType.DMA((4,)),
        ],
    )(*ins)
    swap_to, up_mat = lax.optimization_barrier((swap, up_mat))
    swap = partner(swap_to, "expert", 1)
    up_mat = call(load_kernel, shape(up_mat.shape, BF16), 0, 2 * weights)(up_mat)
    swap, up_mat = lax.optimization_barrier((swap, up_mat))
    far_own = [partner(value, "expert", 2 * (2 + k)) for k, value in enumerate(own_to)]
    near_to, *far_to = call(
        functools.partial(pack_kernel, half), (near, *block, *far), 0, 8 * slots
    )(keep, swap)
    far_other = [partner(value, "expert", 2 * (2 + k)) for k, value in enumerate(far_to[: half - 2])]
    near_in = partner(near_to, "expert", 2)
    far_grads = [partner(value, "expert", 2 * (2 + k)) for k, value in enumerate(far_to[half - 2 :])]
    far_own = call(stage_kernel, staged, STAGE, STAGE // 256)(*far_own)
    rows, *part_pre = call(
        functools.partial(gate_up_kernel, half),
        (sized, *[shape((2, chunk, hidden), BF16)] * dp),
        2 * product,
        2 * weights,
        scratch_shapes=in_order,
    )(keep, swap, far_own, *far_other, near_in, gate_mat, up_mat)
    sums = trade(part_pre)
    act_mine = call(
        functools.partial(act_kernel, dp),
        shape((chunk, hidden), BF16),
        0,
        4 * dp * chunk * hidden,
    )(*sums)
    acts = trade([act_mine] * dp)
    far_grads, act_mine = lax.optimization_barrier((far_grads, act_mine))
    grads, *part_grad = call(
        functools.partial(grad_act_kernel, half),
        (sized, *[shape((chunk, hidden), BF16)] * dp),
        product,
        weights,
        scratch_shapes=in_order,
    )(keep, swap, *far_grads[::-1], near_in, down_mat)
    grad_sums = trade(part_grad)
    pre_mine = call(
        functools.partial(grad_pre_kernel, dp),
        shape((2, chunk, hidden), BF16),
        0,
        6 * dp * chunk * hidden,
    )(*sums, *grad_sums)
    pre = trade([pre_mine] * dp)
    act, out_keep, out_swap = call(
        functools.partial(expert_out_kernel, dp),
        (wide, one, one),
        product,
        weights,
        scratch_shapes=in_order,
    )(*acts, down_mat)
    out_swap = partner(out_swap, "expert", 1)
    out_far = call(pack_back_kernel, far, 0, 8 * slots)(out_keep, out_swap)
    out_far = [partner(value, "expert", 2 * (2 + k)) for k, value in enumerate(out_far)]
    pre, out_far = lax.optimization_barrier((pre, out_far))
    gate_pre, up_pre, grad_keep, grad_swap, *own_to = call(
        functools.partial(row_grad_kernel, dp),
        (wide, wide, one, one, *block),
        2 * product,
        2 * weights,
        scratch_shapes=in_order,
    )(*pre, gate_mat, up_mat)
    grad_swap = partner(grad_swap, "expert", 1)
    back_own = [partner(value, "expert", 2 * (2 + k)) for k, value in enumerate(own_to)]
    near_to, *far_to = call(pack_last_kernel, (near, *block), 0, 8 * slots)(
        out_keep, out_swap, grad_keep, grad_swap
    )
    back_other = [partner(value, "expert", 2 * (2 + k)) for k, value in enumerate(far_to)]
    back_near = partner(near_to, "expert", 2)

    grad_down, _ = call(
        functools.partial(grads_kernel, 1),
        [shape((hidden, features), BF16), token],
        0,
        0,
    )(act, grads)
    grad_gate, grad_up, grads_done = call(
        functools.partial(grads_kernel, 2),
        [shape((features, hidden), BF16)] * 2 + [token],
        0,
        0,
        in_specs=[HERE] * 3 + [ANY],
    )(rows, gate_pre, up_pre, near_to)

    full = shape((tok_rows, features), BF16)
    back_own = call(
        stage_kernel,
        staged,
        STAGE,
        STAGE // 256,
        in_specs=[HERE] * (half - 2) + [ANY],
    )(*back_own, grads_done)
    mixed, grad_tokens = call(functools.partial(scatter_kernel, half), (full, full), 0, 0)(
        pick,
        weight,
        out_keep,
        out_swap,
        *out_far,
        grad_keep,
        grad_swap,
        back_own,
        *back_other,
        back_near,
    )
    return (mixed, grad_tokens, grad_gate[None], grad_up[None], grad_down[None])


def solution(mesh):
    placed = (
        P("expert", "dp"),
        P("expert", "dp"),
        P("expert", None),
        P("expert", None),
        P("expert", "dp", None),
        P("expert", "dp", None),
        P("expert", None, "dp"),
    )
    return jax.shard_map(
        body,
        mesh=mesh,
        in_specs=placed,
        out_specs=(
            P("expert", "dp"),
            P("expert", "dp"),
            P("expert", "dp", None),
            P("expert", "dp", None),
            P("expert", None, "dp"),
        ),
        check_vma=False,
    )
```

```python
import functools

import jax
import jax.numpy as jnp
from jax import lax
from jax.experimental import pallas as pl
from jax.experimental.pallas import tpu as pltpu
from jax.sharding import PartitionSpec as P

F32 = jnp.float32
BF16 = jnp.bfloat16
MIB = 1024 * 1024
ANY = pl.BlockSpec(memory_space=pl.ANY)
HERE = pl.BlockSpec()
VMEM_LIMIT = 24 * MIB
ROUTE_LIMIT = 59 * MIB


def mm(left, right, dims):
    return lax.dot_general(left, right, (dims, ((), ())), preferred_element_type=F32)


def call(kernel, out_shape, flops=0, moved=0, limit=VMEM_LIMIT, **kwargs):
    return pl.pallas_call(
        kernel,
        out_shape=out_shape,
        cost_estimate=pl.CostEstimate(flops=flops, bytes_accessed=moved, transcendentals=0),
        compiler_params=pltpu.CompilerParams(vmem_limit_bytes=limit),
        **kwargs,
    )


def split_rows(refs, value):
    rows = value.shape[0] // len(refs)
    for k, ref in enumerate(refs):
        ref[...] = value[k * rows : (k + 1) * rows]


def join_rows(refs):
    return jnp.concatenate([ref[...] for ref in refs], axis=0)


def split_cores(keep_ref, swap_ref, value, *at):
    half, rows = keep_ref.shape[-3:-1]
    for k in range(half):
        keep_ref[(*at, k)] = value[2 * k * rows : (2 * k + 1) * rows]
        swap_ref[(*at, k)] = value[(2 * k + 1) * rows : (2 * k + 2) * rows]


def route_kernel(experts, *refs):
    pick_ref, weight_ref, keep_ref, swap_ref = refs[4:8]
    ids_ref, gates_ref, tokens_ref, grad_ref, sems = refs[8:]
    copies = [
        pltpu.make_async_copy(refs[k], refs[8 + k], sems.at[k]) for k in range(4)
    ]
    for copy in copies:
        copy.start()
    copies[0].wait()
    copies[1].wait()
    ids = ids_ref[...]
    tok_rows = ids.shape[1]
    slots = pick_ref.shape[0]
    inside = ids < experts
    routed = jnp.max(inside.astype(jnp.int32), axis=0, keepdims=True)
    chosen = jnp.sum(jnp.where(inside, ids, 0), axis=0, keepdims=True)
    weight = jnp.sum(jnp.where(inside, gates_ref[...], 0.0), axis=0, keepdims=True)
    key = jnp.where(routed > 0, chosen ^ lax.axis_index("expert"), experts)
    hot = lax.broadcasted_iota(jnp.int32, (experts, tok_rows), 0) == key
    earlier = lax.broadcasted_iota(jnp.int32, (tok_rows, tok_rows), 0) < lax.broadcasted_iota(
        jnp.int32, (tok_rows, tok_rows), 1
    )
    before = mm(hot.astype(F32).astype(BF16), earlier.astype(F32).astype(BF16), ((1,), (0,)))
    position = jnp.sum(jnp.where(hot, before, 0.0), axis=0, keepdims=True).astype(jnp.int32)
    slot = jnp.where(routed > 0, key * (slots // experts) + position, slots)
    pick = lax.broadcasted_iota(jnp.int32, (slots, tok_rows), 0) == slot
    slot_weight = jnp.sum(jnp.where(pick, weight, 0.0), axis=1, keepdims=True)
    weight_ref[...] = slot_weight
    pick = pick.astype(F32).astype(BF16)
    pick_ref[...] = pick
    copies[2].wait()
    rows = mm(pick, tokens_ref[...], ((1,), (0,))).astype(BF16)
    split_cores(keep_ref, swap_ref, rows, 0)
    copies[3].wait()
    rows = (slot_weight * mm(pick, grad_ref[...], ((1,), (0,)))).astype(BF16)
    split_cores(keep_ref, swap_ref, rows, 1)


def load_kernel(from_ref, to_ref):
    to_ref[...] = from_ref[...]


def pack_kernel(keep_ref, swap_ref, *out_refs):
    half = keep_ref.shape[1]
    for at in range(2):
        for k in range(1, half):
            out_refs[at * (half - 1) + k - 1][0] = keep_ref[at, k]
            out_refs[at * (half - 1) + k - 1][1] = swap_ref[at, k]


def pack_back_kernel(keep_ref, swap_ref, *out_refs):
    for k, out_ref in enumerate(out_refs):
        out_ref[0] = keep_ref[k + 1]
        out_ref[1] = swap_ref[k + 1]


def pieces(at, keep_ref, swap_ref, *refs):
    found = [keep_ref[at, 0], swap_ref[at, 0]]
    for ref in refs[::-1]:
        found += [ref[0], ref[1]]
    return found


def chunk_rows(rows, dp, k):
    chunk = rows // dp
    mine = lax.axis_index("dp")
    return pl.ds(pl.multiple_of((mine ^ k) * chunk, chunk), chunk)


def local_order(found, scratch, dp):
    scratch[...] = jnp.concatenate(found, axis=0)
    rows = scratch.shape[0]
    return jnp.concatenate([scratch[chunk_rows(rows, dp, k), :] for k in range(dp)], axis=0)


def gate_up_kernel(half, *refs):
    gate_ref, up_ref, local_ref, *out_refs, scratch = refs[half + 1 :]
    dp = len(out_refs)
    rows = local_order(pieces(0, *refs[: half + 1]), scratch, dp)
    local_ref[...] = rows
    chunk = rows.shape[0] // dp
    for at, mat in enumerate((gate_ref, up_ref)):
        part = mm(rows, mat[...], ((1,), (0,))).astype(BF16)
        for k, out_ref in enumerate(out_refs):
            out_ref[at] = part[k * chunk : (k + 1) * chunk]


def grad_act_kernel(half, *refs):
    down_ref, local_ref, *out_refs, scratch = refs[half + 1 :]
    dp = len(out_refs)
    rows = local_order(pieces(1, *refs[: half + 1]), scratch, dp)
    local_ref[...] = rows
    split_rows(out_refs, mm(rows, down_ref[...], ((1,), (1,))).astype(BF16))


def group_sum(refs, *at):
    total = refs[0][at].astype(F32)
    for ref in refs[1:]:
        total = total + ref[at].astype(F32)
    return total


def logistic(value):
    return 1.0 / (1.0 + jnp.exp(-value))


def act_kernel(dp, *refs):
    gate = group_sum(refs[:dp], 0)
    up = group_sum(refs[:dp], 1)
    refs[dp][...] = (gate * logistic(gate) * up).astype(BF16)


def grad_pre_kernel(dp, *refs):
    gate = group_sum(refs[:dp], 0)
    up = group_sum(refs[:dp], 1)
    grad = group_sum(refs[dp : 2 * dp], Ellipsis)
    out_ref = refs[2 * dp]
    soft = logistic(gate)
    out_ref[0] = (grad * up * (soft * (1.0 + gate * (1.0 - soft)))).astype(BF16)
    out_ref[1] = (grad * (gate * soft)).astype(BF16)


def send_back(keep_ref, swap_ref, scratch, rows, dp):
    chunk = rows.shape[0] // dp
    for k in range(dp):
        scratch[chunk_rows(rows.shape[0], dp, k), :] = rows[k * chunk : (k + 1) * chunk]
    split_cores(keep_ref, swap_ref, scratch[...])


def expert_out_kernel(dp, *refs):
    down_ref, act_ref, keep_ref, swap_ref, scratch = refs[dp:]
    act = join_rows(refs[:dp])
    act_ref[...] = act
    rows = mm(act, down_ref[...], ((1,), (0,))).astype(BF16)
    send_back(keep_ref, swap_ref, scratch, rows, dp)


def row_grad_kernel(dp, *refs):
    gate_ref, up_ref, gate_pre_ref, up_pre_ref, keep_ref, swap_ref, scratch = refs[dp:]
    gate_pre = jnp.concatenate([ref[0] for ref in refs[:dp]], axis=0)
    up_pre = jnp.concatenate([ref[1] for ref in refs[:dp]], axis=0)
    gate_pre_ref[...] = gate_pre
    up_pre_ref[...] = up_pre
    total = mm(gate_pre, gate_ref[...], ((1,), (1,))) + mm(up_pre, up_ref[...], ((1,), (1,)))
    send_back(keep_ref, swap_ref, scratch, total.astype(BF16), dp)


def returned(keep_ref, swap_ref, refs):
    found = [keep_ref[0], swap_ref[0]]
    for ref in refs[::-1]:
        found += [ref[0], ref[1]]
    return jnp.concatenate(found, axis=0)


def turn_kernel(pick_ref, out_ref):
    out_ref[...] = pick_ref[...].T


def scatter_out(pick_ref, rows, out_ref, scratch, sems):
    parts = sems.shape[0]
    size = pick_ref.shape[0] // parts
    copies = []
    for k in range(parts):
        at = pl.ds(k * size, size)
        scratch[at, :] = mm(pick_ref[at, :], rows, ((1,), (0,))).astype(BF16)
        copies.append(pltpu.make_async_copy(scratch.at[at, :], out_ref.at[at, :], sems.at[k]))
        copies[-1].start()
    for copy in copies:
        copy.wait()


def scatter_scaled_kernel(half, pick_ref, weight_ref, *refs):
    back = returned(*refs[:2], refs[2 : half + 1]).astype(F32)
    scaled = (weight_ref[...] * back).astype(BF16)
    scatter_out(pick_ref, scaled, *refs[-3:])


def scatter_kernel(half, pick_ref, *refs):
    scatter_out(pick_ref, returned(*refs[:2], refs[2 : half + 1]), *refs[-3:])


def grads_kernel(count, left_ref, *refs):
    left = left_ref[...].T
    for right_ref, out_ref in zip(refs[:count], refs[-count:]):
        out_ref[...] = mm(left, right_ref[...], ((1,), (0,))).astype(BF16)


def partner(value, axis, k):
    size = lax.axis_size(axis)
    return lax.ppermute(value, axis, [(i, i ^ k) for i in range(size)])


def trade(values):
    far_first = reversed(range(1, len(values)))
    return [values[0]] + [partner(values[k], "dp", k) for k in far_first][::-1]


def body(tokens, grad_out, expert_ids, gates, w_gate, w_up, w_down):
    experts = lax.axis_size("expert")
    dp = lax.axis_size("dp")
    tok_rows, features = tokens.shape
    capacity = tok_rows // 16
    slots = experts * capacity
    hidden = w_gate.shape[2]
    chunk = slots // dp
    gate_mat, up_mat, down_mat = w_gate[0], w_up[0], w_down[0]
    shape = jax.ShapeDtypeStruct
    product = 2 * slots * features * hidden
    weights = 2 * features * hidden

    half = experts // 2
    sized = shape((slots, features), BF16)
    wide = shape((slots, hidden), BF16)
    both = shape((2, half, capacity, features), BF16)
    one = shape((half, capacity, features), BF16)
    pair = shape((2, capacity, features), BF16)
    in_order = [pltpu.VMEM((slots, features), BF16)]

    ins = (expert_ids.T, gates.T, tokens, grad_out)
    outs = (shape((slots, tok_rows), BF16), shape((slots, 1), F32), both, both)
    pick, weight, keep, swap = call(
        functools.partial(route_kernel, experts),
        outs,
        4 * slots * tok_rows * features,
        8 * tok_rows * features,
        limit=ROUTE_LIMIT,
        in_specs=[ANY] * 4,
        scratch_shapes=[
            *[pltpu.VMEM(array.shape, array.dtype) for array in ins],
            pltpu.SemaphoreType.DMA((4,)),
        ],
    )(*ins)
    swap_to, up_mat = lax.optimization_barrier((swap, up_mat))
    swap = partner(swap_to, "expert", 1)
    up_mat = call(load_kernel, shape(up_mat.shape, BF16), 0, 2 * weights)(up_mat)
    swap, up_mat = lax.optimization_barrier((swap, up_mat))
    sent = call(pack_kernel, [pair] * (2 * half - 2), 0, 8 * slots)(keep, swap)
    arrived = [
        partner(value, "expert", 2 * (1 + k % (half - 1))) for k, value in enumerate(sent)
    ]
    row_blocks, grad_blocks = arrived[: half - 1][::-1], arrived[half - 1 :][::-1]
    rows, *part_pre = call(
        functools.partial(gate_up_kernel, half),
        (sized, *[shape((2, chunk, hidden), BF16)] * dp),
        2 * product,
        2 * weights,
        scratch_shapes=in_order,
    )(keep, swap, *row_blocks, gate_mat, up_mat)
    sums = trade(part_pre)
    act_mine = call(
        functools.partial(act_kernel, dp),
        shape((chunk, hidden), BF16),
        0,
        4 * dp * chunk * hidden,
    )(*sums)
    acts = trade([act_mine] * dp)
    grad_blocks, act_mine = lax.optimization_barrier((grad_blocks, act_mine))
    grads, *part_grad = call(
        functools.partial(grad_act_kernel, half),
        (sized, *[shape((chunk, hidden), BF16)] * dp),
        product,
        weights,
        scratch_shapes=in_order,
    )(keep, swap, *grad_blocks, down_mat)
    grad_sums = trade(part_grad)
    pre_mine = call(
        functools.partial(grad_pre_kernel, dp),
        shape((2, chunk, hidden), BF16),
        0,
        6 * dp * chunk * hidden,
    )(*sums, *grad_sums)
    pre = trade([pre_mine] * dp)
    act, out_keep, out_swap = call(
        functools.partial(expert_out_kernel, dp),
        (wide, one, one),
        product,
        weights,
        scratch_shapes=in_order,
    )(*acts, down_mat)
    back = [pair] * (half - 1)
    out_swap = partner(out_swap, "expert", 1)
    out_near, *out_far = call(pack_back_kernel, back, 0, 8 * slots)(out_keep, out_swap)
    out_far = [partner(value, "expert", 2 * (2 + k)) for k, value in enumerate(out_far)]
    pre, out_far = lax.optimization_barrier((pre, out_far))
    gate_pre, up_pre, grad_keep, grad_swap = call(
        functools.partial(row_grad_kernel, dp),
        (wide, wide, one, one),
        2 * product,
        2 * weights,
        scratch_shapes=in_order,
    )(*pre, gate_mat, up_mat)
    grad_swap = partner(grad_swap, "expert", 1)
    out_near = partner(out_near, "expert", 2)
    grad_to = call(pack_back_kernel, back, 0, 8 * slots)(grad_keep, grad_swap)
    grad_back = [partner(value, "expert", 2 * (1 + k)) for k, value in enumerate(grad_to)]

    (grad_down,) = call(
        functools.partial(grads_kernel, 1),
        [shape((hidden, features), BF16)],
        product,
        weights,
    )(act, grads)
    grad_gate, grad_up = call(
        functools.partial(grads_kernel, 2),
        [shape((features, hidden), BF16)] * 2,
        2 * product,
        2 * weights,
        in_specs=[HERE] * 3 + [ANY],
    )(rows, gate_pre, up_pre, grad_to[0])

    full = shape((tok_rows, features), BF16)
    turned = call(turn_kernel, shape((tok_rows, slots), BF16))(pick)
    flight = dict(
        out_specs=ANY,
        scratch_shapes=[pltpu.VMEM(full.shape, BF16), pltpu.SemaphoreType.DMA((4,))],
    )
    mixed = call(
        functools.partial(scatter_scaled_kernel, half),
        full,
        2 * slots * tok_rows * features,
        4 * tok_rows * features,
        in_specs=[HERE] * (half + 3) + [ANY],
        **flight,
    )(turned, weight, out_keep, out_swap, *out_far[::-1], out_near, grad_to[0])
    grad_tokens = call(
        functools.partial(scatter_kernel, half),
        full,
        2 * slots * tok_rows * features,
        4 * tok_rows * features,
        **flight,
    )(turned, grad_keep, grad_swap, *grad_back[::-1])
    return (mixed, grad_tokens, grad_gate[None], grad_up[None], grad_down[None])


def solution(mesh):
    placed = (
        P("expert", "dp"),
        P("expert", "dp"),
        P("expert", None),
        P("expert", None),
        P("expert", "dp", None),
        P("expert", "dp", None),
        P("expert", None, "dp"),
    )
    return jax.shard_map(
        body,
        mesh=mesh,
        in_specs=placed,
        out_specs=(
            P("expert", "dp"),
            P("expert", "dp"),
            P("expert", "dp", None),
            P("expert", "dp", None),
            P("expert", None, "dp"),
        ),
        check_vma=False,
    )
```

```python
import functools

import jax
import jax.numpy as jnp
from jax import lax
from jax.experimental import pallas as pl
from jax.experimental.pallas import tpu as pltpu
from jax.sharding import PartitionSpec as P

F32 = jnp.float32
BF16 = jnp.bfloat16
MIB = 1024 * 1024
ANY = pl.BlockSpec(memory_space=pl.ANY)
HERE = pl.BlockSpec()
VMEM_LIMIT = 24 * MIB
ROUTE_LIMIT = 59 * MIB


def mm(left, right, dims):
    return lax.dot_general(left, right, (dims, ((), ())), preferred_element_type=F32)


def call(kernel, out_shape, flops=0, moved=0, limit=VMEM_LIMIT, **kwargs):
    return pl.pallas_call(
        kernel,
        out_shape=out_shape,
        cost_estimate=pl.CostEstimate(flops=flops, bytes_accessed=moved, transcendentals=0),
        compiler_params=pltpu.CompilerParams(vmem_limit_bytes=limit),
        **kwargs,
    )


def split_rows(refs, value):
    rows = value.shape[0] // len(refs)
    for k, ref in enumerate(refs):
        ref[...] = value[k * rows : (k + 1) * rows]


def join_rows(refs):
    return jnp.concatenate([ref[...] for ref in refs], axis=0)


def split_cores(keep_ref, swap_ref, value, *at):
    half, rows = keep_ref.shape[-3:-1]
    for k in range(half):
        keep_ref[(*at, k)] = value[2 * k * rows : (2 * k + 1) * rows]
        swap_ref[(*at, k)] = value[(2 * k + 1) * rows : (2 * k + 2) * rows]


def route_kernel(experts, *refs):
    outs, scratch, (earlier_ref, in_sems, out_sems) = refs[4:8], refs[8:16], refs[16:]
    ids_ref, gates_ref, tokens_ref, grad_ref, pick_ref, weight_ref, keep_ref, swap_ref = scratch
    copies = [pltpu.make_async_copy(refs[k], scratch[k], in_sems.at[k]) for k in range(4)]
    for copy in copies:
        copy.start()
    sent = []

    def send(from_ref, to_ref):
        sent.append(pltpu.make_async_copy(from_ref, to_ref, out_sems.at[len(sent)]))
        sent[-1].start()

    tok_rows = ids_ref.shape[1]
    slots = pick_ref.shape[0]
    earlier = lax.broadcasted_iota(jnp.int32, (tok_rows, tok_rows), 0) < lax.broadcasted_iota(
        jnp.int32, (tok_rows, tok_rows), 1
    )
    earlier_ref[...] = earlier.astype(F32).astype(BF16)
    copies[0].wait()
    copies[1].wait()
    ids = ids_ref[...]
    inside = ids < experts
    routed = jnp.max(inside.astype(jnp.int32), axis=0, keepdims=True)
    chosen = jnp.sum(jnp.where(inside, ids, 0), axis=0, keepdims=True)
    weight = jnp.sum(jnp.where(inside, gates_ref[...], 0.0), axis=0, keepdims=True)
    key = jnp.where(routed > 0, chosen ^ lax.axis_index("expert"), experts)
    hot = lax.broadcasted_iota(jnp.int32, (experts, tok_rows), 0) == key
    before = mm(hot.astype(F32).astype(BF16), earlier_ref[...], ((1,), (0,)))
    position = jnp.sum(jnp.where(hot, before, 0.0), axis=0, keepdims=True).astype(jnp.int32)
    slot = jnp.where(routed > 0, key * (slots // experts) + position, slots)
    match = lax.broadcasted_iota(jnp.int32, (slots, tok_rows), 0) == slot
    pick = match.astype(F32).astype(BF16)
    pick_ref[...] = pick
    copies[2].wait()
    rows = mm(pick, tokens_ref[...], ((1,), (0,))).astype(BF16)
    split_cores(keep_ref, swap_ref, rows, 0)
    send(swap_ref.at[0], outs[3].at[0])
    send(keep_ref.at[0], outs[2].at[0])
    send(pick_ref, outs[0])
    slot_weight = jnp.sum(jnp.where(match, weight, 0.0), axis=1, keepdims=True)
    weight_ref[...] = slot_weight
    send(weight_ref, outs[1])
    copies[3].wait()
    rows = (slot_weight * mm(pick, grad_ref[...], ((1,), (0,)))).astype(BF16)
    split_cores(keep_ref, swap_ref, rows, 1)
    send(swap_ref.at[1], outs[3].at[1])
    send(keep_ref.at[1], outs[2].at[1])
    for copy in sent:
        copy.wait()


def load_kernel(from_ref, to_ref):
    to_ref[...] = from_ref[...]


def pack_kernel(keep_ref, swap_ref, *out_refs):
    half = keep_ref.shape[1]
    for at in range(2):
        for k in range(1, half):
            out_refs[at * (half - 1) + k - 1][0] = keep_ref[at, k]
            out_refs[at * (half - 1) + k - 1][1] = swap_ref[at, k]


def pack_back_kernel(keep_ref, swap_ref, *out_refs):
    for k, out_ref in enumerate(out_refs):
        out_ref[0] = keep_ref[k + 1]
        out_ref[1] = swap_ref[k + 1]


def pieces(at, keep_ref, swap_ref, *refs):
    found = [keep_ref[at, 0], swap_ref[at, 0]]
    for ref in refs[::-1]:
        found += [ref[0], ref[1]]
    return found


def chunk_rows(rows, dp, k):
    chunk = rows // dp
    mine = lax.axis_index("dp")
    return pl.ds(pl.multiple_of((mine ^ k) * chunk, chunk), chunk)


def local_order(found, scratch, dp):
    scratch[...] = jnp.concatenate(found, axis=0)
    rows = scratch.shape[0]
    return jnp.concatenate([scratch[chunk_rows(rows, dp, k), :] for k in range(dp)], axis=0)


def gate_up_kernel(half, *refs):
    gate_ref, up_ref, local_ref, *out_refs, scratch = refs[half + 1 :]
    dp = len(out_refs)
    rows = local_order(pieces(0, *refs[: half + 1]), scratch, dp)
    local_ref[...] = rows
    chunk = rows.shape[0] // dp
    for at, mat in enumerate((gate_ref, up_ref)):
        part = mm(rows, mat[...], ((1,), (0,))).astype(BF16)
        for k, out_ref in enumerate(out_refs):
            out_ref[at] = part[k * chunk : (k + 1) * chunk]


def grad_act_kernel(half, *refs):
    down_ref, local_ref, *out_refs, scratch = refs[half + 1 :]
    dp = len(out_refs)
    rows = local_order(pieces(1, *refs[: half + 1]), scratch, dp)
    local_ref[...] = rows
    split_rows(out_refs, mm(rows, down_ref[...], ((1,), (1,))).astype(BF16))


def group_sum(refs, *at):
    total = refs[0][at].astype(F32)
    for ref in refs[1:]:
        total = total + ref[at].astype(F32)
    return total


def logistic(value):
    return 1.0 / (1.0 + jnp.exp(-value))


def act_kernel(dp, *refs):
    gate = group_sum(refs[:dp], 0)
    up = group_sum(refs[:dp], 1)
    refs[dp][...] = (gate * logistic(gate) * up).astype(BF16)


def grad_pre_kernel(dp, *refs):
    gate = group_sum(refs[:dp], 0)
    up = group_sum(refs[:dp], 1)
    grad = group_sum(refs[dp : 2 * dp], Ellipsis)
    out_ref = refs[2 * dp]
    soft = logistic(gate)
    out_ref[0] = (grad * up * (soft * (1.0 + gate * (1.0 - soft)))).astype(BF16)
    out_ref[1] = (grad * (gate * soft)).astype(BF16)


def send_back(keep_ref, swap_ref, scratch, rows, dp):
    chunk = rows.shape[0] // dp
    for k in range(dp):
        scratch[chunk_rows(rows.shape[0], dp, k), :] = rows[k * chunk : (k + 1) * chunk]
    split_cores(keep_ref, swap_ref, scratch[...])


def expert_out_kernel(dp, *refs):
    down_ref, act_ref, keep_ref, swap_ref, scratch = refs[dp:]
    act = join_rows(refs[:dp])
    act_ref[...] = act
    rows = mm(act, down_ref[...], ((1,), (0,))).astype(BF16)
    send_back(keep_ref, swap_ref, scratch, rows, dp)


def row_grad_kernel(dp, *refs):
    gate_ref, up_ref, gate_pre_ref, up_pre_ref, keep_ref, swap_ref, scratch = refs[dp:]
    gate_pre = jnp.concatenate([ref[0] for ref in refs[:dp]], axis=0)
    up_pre = jnp.concatenate([ref[1] for ref in refs[:dp]], axis=0)
    gate_pre_ref[...] = gate_pre
    up_pre_ref[...] = up_pre
    total = mm(gate_pre, gate_ref[...], ((1,), (1,))) + mm(up_pre, up_ref[...], ((1,), (1,)))
    send_back(keep_ref, swap_ref, scratch, total.astype(BF16), dp)


def returned(keep_ref, swap_ref, refs):
    found = [keep_ref[0], swap_ref[0]]
    for ref in refs[::-1]:
        found += [ref[0], ref[1]]
    return jnp.concatenate(found, axis=0)


def turn_kernel(pick_ref, out_ref):
    out_ref[...] = pick_ref[...].T


def scatter_out(pick_ref, rows, out_ref, scratch, sems):
    parts = sems.shape[0]
    size = pick_ref.shape[0] // parts
    copies = []
    for k in range(parts):
        at = pl.ds(k * size, size)
        scratch[at, :] = mm(pick_ref[at, :], rows, ((1,), (0,))).astype(BF16)
        copies.append(pltpu.make_async_copy(scratch.at[at, :], out_ref.at[at, :], sems.at[k]))
        copies[-1].start()
    for copy in copies:
        copy.wait()


def scatter_scaled_kernel(half, pick_ref, weight_ref, *refs):
    back = returned(*refs[:2], refs[2 : half + 1]).astype(F32)
    scaled = (weight_ref[...] * back).astype(BF16)
    scatter_out(pick_ref, scaled, *refs[-3:])


def scatter_kernel(half, pick_ref, *refs):
    scatter_out(pick_ref, returned(*refs[:2], refs[2 : half + 1]), *refs[-3:])


def grads_kernel(count, left_ref, *refs):
    left = left_ref[...].T
    for right_ref, out_ref in zip(refs[:count], refs[-count:]):
        out_ref[...] = mm(left, right_ref[...], ((1,), (0,))).astype(BF16)


def partner(value, axis, k):
    size = lax.axis_size(axis)
    return lax.ppermute(value, axis, [(i, i ^ k) for i in range(size)])


def trade(values):
    far_first = reversed(range(1, len(values)))
    return [values[0]] + [partner(values[k], "dp", k) for k in far_first][::-1]


def body(tokens, grad_out, expert_ids, gates, w_gate, w_up, w_down):
    experts = lax.axis_size("expert")
    dp = lax.axis_size("dp")
    tok_rows, features = tokens.shape
    capacity = tok_rows // 16
    slots = experts * capacity
    hidden = w_gate.shape[2]
    chunk = slots // dp
    gate_mat, up_mat, down_mat = w_gate[0], w_up[0], w_down[0]
    shape = jax.ShapeDtypeStruct
    product = 2 * slots * features * hidden
    weights = 2 * features * hidden

    half = experts // 2
    sized = shape((slots, features), BF16)
    wide = shape((slots, hidden), BF16)
    both = shape((2, half, capacity, features), BF16)
    one = shape((half, capacity, features), BF16)
    pair = shape((2, capacity, features), BF16)
    in_order = [pltpu.VMEM((slots, features), BF16)]

    ins = (expert_ids.T, gates.T, tokens, grad_out)
    outs = (shape((slots, tok_rows), BF16), shape((slots, 1), F32), both, both)
    pick, weight, keep, swap = call(
        functools.partial(route_kernel, experts),
        outs,
        4 * slots * tok_rows * features,
        8 * tok_rows * features,
        limit=ROUTE_LIMIT,
        in_specs=[ANY] * 4,
        out_specs=(ANY,) * 4,
        scratch_shapes=[
            *[pltpu.VMEM(array.shape, array.dtype) for array in (*ins, *outs)],
            pltpu.VMEM((tok_rows, tok_rows), BF16),
            pltpu.SemaphoreType.DMA((4,)),
            pltpu.SemaphoreType.DMA((6,)),
        ],
    )(*ins)
    swap_to, up_mat = lax.optimization_barrier((swap, up_mat))
    swap = partner(swap_to, "expert", 1)
    up_mat = call(load_kernel, shape(up_mat.shape, BF16), 0, 2 * weights)(up_mat)
    swap, up_mat = lax.optimization_barrier((swap, up_mat))
    sent = call(pack_kernel, [pair] * (2 * half - 2), 0, 8 * slots)(keep, swap)
    arrived = [
        partner(value, "expert", 2 * (1 + k % (half - 1))) for k, value in enumerate(sent)
    ]
    row_blocks, grad_blocks = arrived[: half - 1][::-1], arrived[half - 1 :][::-1]
    rows, *part_pre = call(
        functools.partial(gate_up_kernel, half),
        (sized, *[shape((2, chunk, hidden), BF16)] * dp),
        2 * product,
        2 * weights,
        scratch_shapes=in_order,
    )(keep, swap, *row_blocks, gate_mat, up_mat)
    sums = trade(part_pre)
    act_mine = call(
        functools.partial(act_kernel, dp),
        shape((chunk, hidden), BF16),
        0,
        4 * dp * chunk * hidden,
    )(*sums)
    acts = trade([act_mine] * dp)
    grad_blocks, act_mine = lax.optimization_barrier((grad_blocks, act_mine))
    grads, *part_grad = call(
        functools.partial(grad_act_kernel, half),
        (sized, *[shape((chunk, hidden), BF16)] * dp),
        product,
        weights,
        scratch_shapes=in_order,
    )(keep, swap, *grad_blocks, down_mat)
    grad_sums = trade(part_grad)
    pre_mine = call(
        functools.partial(grad_pre_kernel, dp),
        shape((2, chunk, hidden), BF16),
        0,
        6 * dp * chunk * hidden,
    )(*sums, *grad_sums)
    pre = trade([pre_mine] * dp)
    act, out_keep, out_swap = call(
        functools.partial(expert_out_kernel, dp),
        (wide, one, one),
        product,
        weights,
        scratch_shapes=in_order,
    )(*acts, down_mat)
    back = [pair] * (half - 1)
    out_swap = partner(out_swap, "expert", 1)
    out_near, *out_far = call(pack_back_kernel, back, 0, 8 * slots)(out_keep, out_swap)
    out_far = [partner(value, "expert", 2 * (2 + k)) for k, value in enumerate(out_far)]
    out_near = partner(out_near, "expert", 2)
    pre, out_far, out_near = lax.optimization_barrier((pre, out_far, out_near))
    gate_pre, up_pre, grad_keep, grad_swap = call(
        functools.partial(row_grad_kernel, dp),
        (wide, wide, one, one),
        2 * product,
        2 * weights,
        scratch_shapes=in_order,
    )(*pre, gate_mat, up_mat)
    grad_swap = partner(grad_swap, "expert", 1)
    grad_to = call(pack_back_kernel, back, 0, 8 * slots)(grad_keep, grad_swap)
    grad_back = [partner(value, "expert", 2 * (1 + k)) for k, value in enumerate(grad_to)]

    (grad_down,) = call(
        functools.partial(grads_kernel, 1),
        [shape((hidden, features), BF16)],
        product,
        weights,
    )(act, grads)
    grad_gate, grad_up = call(
        functools.partial(grads_kernel, 2),
        [shape((features, hidden), BF16)] * 2,
        2 * product,
        2 * weights,
        in_specs=[HERE] * 3 + [ANY],
    )(rows, gate_pre, up_pre, grad_to[0])

    full = shape((tok_rows, features), BF16)
    turned = call(turn_kernel, shape((tok_rows, slots), BF16))(pick)
    flight = dict(
        out_specs=ANY,
        scratch_shapes=[pltpu.VMEM(full.shape, BF16), pltpu.SemaphoreType.DMA((4,))],
    )
    mixed = call(
        functools.partial(scatter_scaled_kernel, half),
        full,
        2 * slots * tok_rows * features,
        4 * tok_rows * features,
        in_specs=[HERE] * (half + 3) + [ANY],
        **flight,
    )(turned, weight, out_keep, out_swap, *out_far[::-1], out_near, grad_to[0])
    grad_tokens = call(
        functools.partial(scatter_kernel, half),
        full,
        2 * slots * tok_rows * features,
        4 * tok_rows * features,
        **flight,
    )(turned, grad_keep, grad_swap, *grad_back[::-1])
    return (mixed, grad_tokens, grad_gate[None], grad_up[None], grad_down[None])


def solution(mesh):
    placed = (
        P("expert", "dp"),
        P("expert", "dp"),
        P("expert", None),
        P("expert", None),
        P("expert", "dp", None),
        P("expert", "dp", None),
        P("expert", None, "dp"),
    )
    return jax.shard_map(
        body,
        mesh=mesh,
        in_specs=placed,
        out_specs=(
            P("expert", "dp"),
            P("expert", "dp"),
            P("expert", "dp", None),
            P("expert", "dp", None),
            P("expert", None, "dp"),
        ),
        check_vma=False,
    )
```

```python
import functools

import jax
import jax.numpy as jnp
from jax import lax
from jax.experimental import pallas as pl
from jax.experimental.pallas import tpu as pltpu
from jax.sharding import PartitionSpec as P

F32 = jnp.float32
BF16 = jnp.bfloat16
MIB = 1024 * 1024
ANY = pl.BlockSpec(memory_space=pl.ANY)
HERE = pl.BlockSpec()
VMEM_LIMIT = 24 * MIB
ROUTE_LIMIT = 59 * MIB


def mm(left, right, dims):
    return lax.dot_general(left, right, (dims, ((), ())), preferred_element_type=F32)


def call(kernel, out_shape, flops=0, moved=0, limit=VMEM_LIMIT, **kwargs):
    return pl.pallas_call(
        kernel,
        out_shape=out_shape,
        cost_estimate=pl.CostEstimate(flops=flops, bytes_accessed=moved, transcendentals=0),
        compiler_params=pltpu.CompilerParams(vmem_limit_bytes=limit),
        **kwargs,
    )


def split_rows(refs, value):
    rows = value.shape[0] // len(refs)
    for k, ref in enumerate(refs):
        ref[...] = value[k * rows : (k + 1) * rows]


def join_rows(refs):
    return jnp.concatenate([ref[...] for ref in refs], axis=0)


def split_cores(keep_ref, swap_ref, value, *at):
    half, rows = keep_ref.shape[-3:-1]
    for k in range(half):
        keep_ref[(*at, k)] = value[2 * k * rows : (2 * k + 1) * rows]
        swap_ref[(*at, k)] = value[(2 * k + 1) * rows : (2 * k + 2) * rows]


def route_kernel(experts, *refs):
    pick_ref, weight_ref, keep_ref, swap_ref = refs[4:8]
    ids_ref, gates_ref, tokens_ref, grad_ref, sems = refs[8:]
    copies = [
        pltpu.make_async_copy(refs[k], refs[8 + k], sems.at[k]) for k in range(4)
    ]
    for copy in copies:
        copy.start()
    copies[0].wait()
    copies[1].wait()
    ids = ids_ref[...]
    tok_rows = ids.shape[1]
    slots = pick_ref.shape[0]
    inside = ids < experts
    routed = jnp.max(inside.astype(jnp.int32), axis=0, keepdims=True)
    chosen = jnp.sum(jnp.where(inside, ids, 0), axis=0, keepdims=True)
    weight = jnp.sum(jnp.where(inside, gates_ref[...], 0.0), axis=0, keepdims=True)
    key = jnp.where(routed > 0, chosen ^ lax.axis_index("expert"), experts)
    hot = lax.broadcasted_iota(jnp.int32, (experts, tok_rows), 0) == key
    earlier = lax.broadcasted_iota(jnp.int32, (tok_rows, tok_rows), 0) < lax.broadcasted_iota(
        jnp.int32, (tok_rows, tok_rows), 1
    )
    before = mm(hot.astype(F32).astype(BF16), earlier.astype(F32).astype(BF16), ((1,), (0,)))
    position = jnp.sum(jnp.where(hot, before, 0.0), axis=0, keepdims=True).astype(jnp.int32)
    slot = jnp.where(routed > 0, key * (slots // experts) + position, slots)
    pick = lax.broadcasted_iota(jnp.int32, (slots, tok_rows), 0) == slot
    slot_weight = jnp.sum(jnp.where(pick, weight, 0.0), axis=1, keepdims=True)
    weight_ref[...] = slot_weight
    pick = pick.astype(F32).astype(BF16)
    pick_ref[...] = pick
    copies[2].wait()
    rows = mm(pick, tokens_ref[...], ((1,), (0,))).astype(BF16)
    split_cores(keep_ref, swap_ref, rows, 0)
    copies[3].wait()
    rows = (slot_weight * mm(pick, grad_ref[...], ((1,), (0,)))).astype(BF16)
    split_cores(keep_ref, swap_ref, rows, 1)


def load_kernel(from_ref, to_ref):
    to_ref[...] = from_ref[...]


def pack_kernel(keep_ref, swap_ref, *out_refs):
    half = keep_ref.shape[1]
    for at in range(2):
        for k in range(1, half):
            out_refs[at * (half - 1) + k - 1][0] = keep_ref[at, k]
            out_refs[at * (half - 1) + k - 1][1] = swap_ref[at, k]


def pack_back_kernel(keep_ref, swap_ref, *out_refs):
    for k, out_ref in enumerate(out_refs):
        out_ref[0] = keep_ref[k + 1]
        out_ref[1] = swap_ref[k + 1]


def pieces(at, keep_ref, swap_ref, *refs):
    found = [keep_ref[at, 0], swap_ref[at, 0]]
    for ref in refs[::-1]:
        found += [ref[0], ref[1]]
    return found


def chunk_rows(rows, dp, k):
    chunk = rows // dp
    mine = lax.axis_index("dp")
    return pl.ds(pl.multiple_of((mine ^ k) * chunk, chunk), chunk)


def local_order(found, scratch, dp):
    scratch[...] = jnp.concatenate(found, axis=0)
    rows = scratch.shape[0]
    return jnp.concatenate([scratch[chunk_rows(rows, dp, k), :] for k in range(dp)], axis=0)


def gate_up_kernel(half, *refs):
    gate_ref, up_ref, local_ref, *out_refs, scratch = refs[half + 1 :]
    dp = len(out_refs)
    rows = local_order(pieces(0, *refs[: half + 1]), scratch, dp)
    local_ref[...] = rows
    chunk = rows.shape[0] // dp
    for at, mat in enumerate((gate_ref, up_ref)):
        part = mm(rows, mat[...], ((1,), (0,))).astype(BF16)
        for k, out_ref in enumerate(out_refs):
            out_ref[at] = part[k * chunk : (k + 1) * chunk]


def grad_act_kernel(half, *refs):
    down_ref, local_ref, *out_refs, scratch = refs[half + 1 :]
    dp = len(out_refs)
    rows = local_order(pieces(1, *refs[: half + 1]), scratch, dp)
    local_ref[...] = rows
    split_rows(out_refs, mm(rows, down_ref[...], ((1,), (1,))).astype(BF16))


def group_sum(refs, *at):
    total = refs[0][at].astype(F32)
    for ref in refs[1:]:
        total = total + ref[at].astype(F32)
    return total


def logistic(value):
    return 1.0 / (1.0 + jnp.exp(-value))


def act_kernel(dp, *refs):
    gate = group_sum(refs[:dp], 0)
    up = group_sum(refs[:dp], 1)
    refs[dp][...] = (gate * logistic(gate) * up).astype(BF16)


def grad_pre_kernel(dp, *refs):
    gate = group_sum(refs[:dp], 0)
    up = group_sum(refs[:dp], 1)
    grad = group_sum(refs[dp : 2 * dp], Ellipsis)
    out_ref = refs[-1]
    soft = logistic(gate)
    out_ref[0] = (grad * up * (soft * (1.0 + gate * (1.0 - soft)))).astype(BF16)
    out_ref[1] = (grad * (gate * soft)).astype(BF16)


def send_back(keep_ref, swap_ref, scratch, rows, dp):
    chunk = rows.shape[0] // dp
    for k in range(dp):
        scratch[chunk_rows(rows.shape[0], dp, k), :] = rows[k * chunk : (k + 1) * chunk]
    split_cores(keep_ref, swap_ref, scratch[...])


def expert_out_kernel(dp, *refs):
    down_ref, act_ref, keep_ref, swap_ref, scratch = refs[dp:]
    act = join_rows(refs[:dp])
    act_ref[...] = act
    rows = mm(act, down_ref[...], ((1,), (0,))).astype(BF16)
    send_back(keep_ref, swap_ref, scratch, rows, dp)


def row_grad_kernel(dp, *refs):
    gate_ref, up_ref, gate_pre_ref, up_pre_ref, keep_ref, swap_ref, scratch = refs[dp:]
    gate_pre = jnp.concatenate([ref[0] for ref in refs[:dp]], axis=0)
    up_pre = jnp.concatenate([ref[1] for ref in refs[:dp]], axis=0)
    gate_pre_ref[...] = gate_pre
    up_pre_ref[...] = up_pre
    total = mm(gate_pre, gate_ref[...], ((1,), (1,))) + mm(up_pre, up_ref[...], ((1,), (1,)))
    send_back(keep_ref, swap_ref, scratch, total.astype(BF16), dp)


def returned(keep_ref, swap_ref, refs):
    found = [keep_ref[0], swap_ref[0]]
    for ref in refs[::-1]:
        found += [ref[0], ref[1]]
    return jnp.concatenate(found, axis=0)


def turn_kernel(pick_ref, out_ref):
    out_ref[...] = pick_ref[...].T


def scatter_out(pick_ref, rows, out_ref, scratch, sems):
    parts = sems.shape[0]
    size = pick_ref.shape[0] // parts
    copies = []
    for k in range(parts):
        at = pl.ds(k * size, size)
        scratch[at, :] = mm(pick_ref[at, :], rows, ((1,), (0,))).astype(BF16)
        copies.append(pltpu.make_async_copy(scratch.at[at, :], out_ref.at[at, :], sems.at[k]))
        copies[-1].start()
    for copy in copies:
        copy.wait()


def scatter_scaled_kernel(half, pick_ref, weight_ref, *refs):
    back = returned(*refs[:2], refs[2 : half + 1]).astype(F32)
    scaled = (weight_ref[...] * back).astype(BF16)
    scatter_out(pick_ref, scaled, *refs[-3:])


def scatter_kernel(half, pick_ref, *refs):
    scatter_out(pick_ref, returned(*refs[:2], refs[2 : half + 1]), *refs[-3:])


def grads_kernel(count, left_ref, *refs):
    left = left_ref[...].T
    for right_ref, out_ref in zip(refs[:count], refs[-count:]):
        out_ref[...] = mm(left, right_ref[...], ((1,), (0,))).astype(BF16)


def partner(value, axis, k):
    size = lax.axis_size(axis)
    return lax.ppermute(value, axis, [(i, i ^ k) for i in range(size)])


def trade(values):
    far_first = reversed(range(1, len(values)))
    return [values[0]] + [partner(values[k], "dp", k) for k in far_first][::-1]


def body(tokens, grad_out, expert_ids, gates, w_gate, w_up, w_down):
    experts = lax.axis_size("expert")
    dp = lax.axis_size("dp")
    tok_rows, features = tokens.shape
    capacity = tok_rows // 16
    slots = experts * capacity
    hidden = w_gate.shape[2]
    chunk = slots // dp
    gate_mat, up_mat, down_mat = w_gate[0], w_up[0], w_down[0]
    shape = jax.ShapeDtypeStruct
    product = 2 * slots * features * hidden
    weights = 2 * features * hidden

    half = experts // 2
    sized = shape((slots, features), BF16)
    wide = shape((slots, hidden), BF16)
    both = shape((2, half, capacity, features), BF16)
    one = shape((half, capacity, features), BF16)
    pair = shape((2, capacity, features), BF16)
    in_order = [pltpu.VMEM((slots, features), BF16)]

    ins = (expert_ids.T, gates.T, tokens, grad_out)
    outs = (shape((slots, tok_rows), BF16), shape((slots, 1), F32), both, both)
    pick, weight, keep, swap = call(
        functools.partial(route_kernel, experts),
        outs,
        4 * slots * tok_rows * features,
        8 * tok_rows * features,
        limit=ROUTE_LIMIT,
        in_specs=[ANY] * 4,
        scratch_shapes=[
            *[pltpu.VMEM(array.shape, array.dtype) for array in ins],
            pltpu.SemaphoreType.DMA((4,)),
        ],
    )(*ins)
    swap_to, up_mat = lax.optimization_barrier((swap, up_mat))
    swap = partner(swap_to, "expert", 1)
    up_mat = call(load_kernel, shape(up_mat.shape, BF16), 0, 2 * weights)(up_mat)
    swap, up_mat = lax.optimization_barrier((swap, up_mat))
    sent = call(pack_kernel, [pair] * (2 * half - 2), 0, 8 * slots)(keep, swap)
    arrived = [
        partner(value, "expert", 2 * (1 + k % (half - 1))) for k, value in enumerate(sent)
    ]
    row_blocks, grad_blocks = arrived[: half - 1][::-1], arrived[half - 1 :][::-1]
    rows, *part_pre = call(
        functools.partial(gate_up_kernel, half),
        (sized, *[shape((2, chunk, hidden), BF16)] * dp),
        2 * product,
        2 * weights,
        scratch_shapes=in_order,
    )(keep, swap, *row_blocks, gate_mat, up_mat)
    sums = trade(part_pre)
    act_mine = call(
        functools.partial(act_kernel, dp),
        shape((chunk, hidden), BF16),
        0,
        4 * dp * chunk * hidden,
    )(*sums)
    acts = trade([act_mine] * dp)
    grad_blocks, act_mine = lax.optimization_barrier((grad_blocks, act_mine))
    grads, *part_grad = call(
        functools.partial(grad_act_kernel, half),
        (sized, *[shape((chunk, hidden), BF16)] * dp),
        product,
        weights,
        scratch_shapes=in_order,
    )(keep, swap, *grad_blocks, down_mat)
    grad_sums = trade(part_grad)
    act, out_keep, out_swap = call(
        functools.partial(expert_out_kernel, dp),
        (wide, one, one),
        product,
        weights,
        scratch_shapes=in_order,
    )(*acts, down_mat)
    pre_mine = call(
        functools.partial(grad_pre_kernel, dp),
        shape((2, chunk, hidden), BF16),
        0,
        6 * dp * chunk * hidden,
        in_specs=[HERE] * (2 * dp) + [ANY],
    )(*sums, *grad_sums, out_keep)
    pre = trade([pre_mine] * dp)
    back = [pair] * (half - 1)
    out_swap = partner(out_swap, "expert", 1)
    out_near, *out_far = call(pack_back_kernel, back, 0, 8 * slots)(out_keep, out_swap)
    out_far = [partner(value, "expert", 2 * (2 + k)) for k, value in enumerate(out_far)]
    out_near = partner(out_near, "expert", 2)
    pre, out_far, out_near = lax.optimization_barrier((pre, out_far, out_near))
    gate_pre, up_pre, grad_keep, grad_swap = call(
        functools.partial(row_grad_kernel, dp),
        (wide, wide, one, one),
        2 * product,
        2 * weights,
        scratch_shapes=in_order,
    )(*pre, gate_mat, up_mat)
    grad_swap = partner(grad_swap, "expert", 1)
    grad_to = call(pack_back_kernel, back, 0, 8 * slots)(grad_keep, grad_swap)
    grad_back = [partner(value, "expert", 2 * (1 + k)) for k, value in enumerate(grad_to)]

    (grad_down,) = call(
        functools.partial(grads_kernel, 1),
        [shape((hidden, features), BF16)],
        product,
        weights,
    )(act, grads)
    grad_gate, grad_up = call(
        functools.partial(grads_kernel, 2),
        [shape((features, hidden), BF16)] * 2,
        2 * product,
        2 * weights,
        in_specs=[HERE] * 3 + [ANY],
    )(rows, gate_pre, up_pre, grad_to[0])

    full = shape((tok_rows, features), BF16)
    turned = call(turn_kernel, shape((tok_rows, slots), BF16))(pick)
    flight = dict(
        out_specs=ANY,
        scratch_shapes=[pltpu.VMEM(full.shape, BF16), pltpu.SemaphoreType.DMA((4,))],
    )
    mixed = call(
        functools.partial(scatter_scaled_kernel, half),
        full,
        2 * slots * tok_rows * features,
        4 * tok_rows * features,
        in_specs=[HERE] * (half + 3) + [ANY],
        **flight,
    )(turned, weight, out_keep, out_swap, *out_far[::-1], out_near, grad_to[0])
    grad_tokens = call(
        functools.partial(scatter_kernel, half),
        full,
        2 * slots * tok_rows * features,
        4 * tok_rows * features,
        **flight,
    )(turned, grad_keep, grad_swap, *grad_back[::-1])
    return (mixed, grad_tokens, grad_gate[None], grad_up[None], grad_down[None])


def solution(mesh):
    placed = (
        P("expert", "dp"),
        P("expert", "dp"),
        P("expert", None),
        P("expert", None),
        P("expert", "dp", None),
        P("expert", "dp", None),
        P("expert", None, "dp"),
    )
    return jax.shard_map(
        body,
        mesh=mesh,
        in_specs=placed,
        out_specs=(
            P("expert", "dp"),
            P("expert", "dp"),
            P("expert", "dp", None),
            P("expert", "dp", None),
            P("expert", None, "dp"),
        ),
        check_vma=False,
    )
```

```python
import functools

import jax
import jax.numpy as jnp
from jax import lax
from jax.experimental import pallas as pl
from jax.experimental.pallas import tpu as pltpu
from jax.sharding import PartitionSpec as P

F32 = jnp.float32
BF16 = jnp.bfloat16
MIB = 1024 * 1024
ANY = pl.BlockSpec(memory_space=pl.ANY)
HERE = pl.BlockSpec()
VMEM_LIMIT = 24 * MIB
ROUTE_LIMIT = 59 * MIB


def mm(left, right, dims):
    return lax.dot_general(left, right, (dims, ((), ())), preferred_element_type=F32)


def call(kernel, out_shape, flops=0, moved=0, limit=VMEM_LIMIT, **kwargs):
    return pl.pallas_call(
        kernel,
        out_shape=out_shape,
        cost_estimate=pl.CostEstimate(flops=flops, bytes_accessed=moved, transcendentals=0),
        compiler_params=pltpu.CompilerParams(vmem_limit_bytes=limit),
        **kwargs,
    )


def split_rows(refs, value):
    rows = value.shape[0] // len(refs)
    for k, ref in enumerate(refs):
        ref[...] = value[k * rows : (k + 1) * rows]


def join_rows(refs):
    return jnp.concatenate([ref[...] for ref in refs], axis=0)


def split_cores(keep_ref, swap_ref, value, *at):
    half, rows = keep_ref.shape[-3:-1]
    for k in range(half):
        keep_ref[(*at, k)] = value[2 * k * rows : (2 * k + 1) * rows]
        swap_ref[(*at, k)] = value[(2 * k + 1) * rows : (2 * k + 2) * rows]


def route_kernel(experts, *refs):
    pick_ref, weight_ref, keep_ref, swap_ref = refs[3:7]
    ids_ref, gates_ref, tokens_ref, sems = refs[7:]
    copies = [
        pltpu.make_async_copy(refs[k], refs[7 + k], sems.at[k]) for k in range(3)
    ]
    for copy in copies:
        copy.start()
    copies[0].wait()
    copies[1].wait()
    ids = ids_ref[...]
    tok_rows = ids.shape[1]
    slots = pick_ref.shape[0]
    inside = ids < experts
    routed = jnp.max(inside.astype(jnp.int32), axis=0, keepdims=True)
    chosen = jnp.sum(jnp.where(inside, ids, 0), axis=0, keepdims=True)
    weight = jnp.sum(jnp.where(inside, gates_ref[...], 0.0), axis=0, keepdims=True)
    key = jnp.where(routed > 0, chosen ^ lax.axis_index("expert"), experts)
    hot = lax.broadcasted_iota(jnp.int32, (experts, tok_rows), 0) == key
    earlier = lax.broadcasted_iota(jnp.int32, (tok_rows, tok_rows), 0) < lax.broadcasted_iota(
        jnp.int32, (tok_rows, tok_rows), 1
    )
    before = mm(hot.astype(F32).astype(BF16), earlier.astype(F32).astype(BF16), ((1,), (0,)))
    position = jnp.sum(jnp.where(hot, before, 0.0), axis=0, keepdims=True).astype(jnp.int32)
    slot = jnp.where(routed > 0, key * (slots // experts) + position, slots)
    pick = lax.broadcasted_iota(jnp.int32, (slots, tok_rows), 0) == slot
    slot_weight = jnp.sum(jnp.where(pick, weight, 0.0), axis=1, keepdims=True)
    weight_ref[...] = slot_weight
    pick = pick.astype(F32).astype(BF16)
    pick_ref[...] = pick
    copies[2].wait()
    rows = mm(pick, tokens_ref[...], ((1,), (0,))).astype(BF16)
    split_cores(keep_ref, swap_ref, rows)


def gather_scaled_kernel(pick_ref, weight_ref, grad_ref, keep_ref, swap_ref):
    rows = mm(pick_ref[...], grad_ref[...], ((1,), (0,)))
    split_cores(keep_ref, swap_ref, (weight_ref[...] * rows).astype(BF16))


def load_kernel(from_ref, to_ref):
    to_ref[...] = from_ref[...]


def pack_back_kernel(keep_ref, swap_ref, *out_refs):
    for k, out_ref in enumerate(out_refs):
        out_ref[0] = keep_ref[k + 1]
        out_ref[1] = swap_ref[k + 1]


def pieces(keep_ref, swap_ref, *refs):
    found = [keep_ref[0], swap_ref[0]]
    for ref in refs[::-1]:
        found += [ref[0], ref[1]]
    return found


def chunk_rows(rows, dp, k):
    chunk = rows // dp
    mine = lax.axis_index("dp")
    return pl.ds(pl.multiple_of((mine ^ k) * chunk, chunk), chunk)


def local_order(found, scratch, dp):
    scratch[...] = jnp.concatenate(found, axis=0)
    rows = scratch.shape[0]
    return jnp.concatenate([scratch[chunk_rows(rows, dp, k), :] for k in range(dp)], axis=0)


def gate_up_kernel(half, *refs):
    gate_ref, up_ref, local_ref, *out_refs, scratch = refs[half + 1 :]
    dp = len(out_refs)
    rows = local_order(pieces(*refs[: half + 1]), scratch, dp)
    local_ref[...] = rows
    chunk = rows.shape[0] // dp
    for at, mat in enumerate((gate_ref, up_ref)):
        part = mm(rows, mat[...], ((1,), (0,))).astype(BF16)
        for k, out_ref in enumerate(out_refs):
            out_ref[at] = part[k * chunk : (k + 1) * chunk]


def grad_act_kernel(half, *refs):
    down_ref, local_ref, *out_refs, scratch = refs[half + 1 :]
    dp = len(out_refs)
    rows = local_order(pieces(*refs[: half + 1]), scratch, dp)
    local_ref[...] = rows
    split_rows(out_refs, mm(rows, down_ref[...], ((1,), (1,))).astype(BF16))


def group_sum(refs, *at):
    total = refs[0][at].astype(F32)
    for ref in refs[1:]:
        total = total + ref[at].astype(F32)
    return total


def logistic(value):
    return 1.0 / (1.0 + jnp.exp(-value))


def act_kernel(dp, *refs):
    gate = group_sum(refs[:dp], 0)
    up = group_sum(refs[:dp], 1)
    refs[dp][...] = (gate * logistic(gate) * up).astype(BF16)


def grad_pre_kernel(dp, *refs):
    gate = group_sum(refs[:dp], 0)
    up = group_sum(refs[:dp], 1)
    grad = group_sum(refs[dp : 2 * dp], Ellipsis)
    out_ref = refs[2 * dp]
    soft = logistic(gate)
    out_ref[0] = (grad * up * (soft * (1.0 + gate * (1.0 - soft)))).astype(BF16)
    out_ref[1] = (grad * (gate * soft)).astype(BF16)


def send_back(keep_ref, swap_ref, scratch, rows, dp):
    chunk = rows.shape[0] // dp
    for k in range(dp):
        scratch[chunk_rows(rows.shape[0], dp, k), :] = rows[k * chunk : (k + 1) * chunk]
    split_cores(keep_ref, swap_ref, scratch[...])


def expert_out_kernel(dp, *refs):
    down_ref, act_ref, keep_ref, swap_ref, scratch = refs[dp:]
    act = join_rows(refs[:dp])
    act_ref[...] = act
    rows = mm(act, down_ref[...], ((1,), (0,))).astype(BF16)
    send_back(keep_ref, swap_ref, scratch, rows, dp)


def row_grad_kernel(dp, *refs):
    gate_ref, up_ref, gate_pre_ref, up_pre_ref, keep_ref, swap_ref, scratch = refs[dp:]
    gate_pre = jnp.concatenate([ref[0] for ref in refs[:dp]], axis=0)
    up_pre = jnp.concatenate([ref[1] for ref in refs[:dp]], axis=0)
    gate_pre_ref[...] = gate_pre
    up_pre_ref[...] = up_pre
    total = mm(gate_pre, gate_ref[...], ((1,), (1,))) + mm(up_pre, up_ref[...], ((1,), (1,)))
    send_back(keep_ref, swap_ref, scratch, total.astype(BF16), dp)


def returned(keep_ref, swap_ref, refs):
    found = [keep_ref[0], swap_ref[0]]
    for ref in refs[::-1]:
        found += [ref[0], ref[1]]
    return jnp.concatenate(found, axis=0)


def turn_kernel(pick_ref, out_ref):
    out_ref[...] = pick_ref[...].T


def scatter_out(pick_ref, rows, out_ref, scratch, sems):
    parts = sems.shape[0]
    size = pick_ref.shape[0] // parts
    copies = []
    for k in range(parts):
        at = pl.ds(k * size, size)
        scratch[at, :] = mm(pick_ref[at, :], rows, ((1,), (0,))).astype(BF16)
        copies.append(pltpu.make_async_copy(scratch.at[at, :], out_ref.at[at, :], sems.at[k]))
        copies[-1].start()
    for copy in copies:
        copy.wait()


def scatter_scaled_kernel(half, pick_ref, weight_ref, *refs):
    back = returned(*refs[:2], refs[2 : half + 1]).astype(F32)
    scaled = (weight_ref[...] * back).astype(BF16)
    scatter_out(pick_ref, scaled, *refs[-3:])


def scatter_kernel(half, pick_ref, *refs):
    scatter_out(pick_ref, returned(*refs[:2], refs[2 : half + 1]), *refs[-3:])


def grads_kernel(count, left_ref, *refs):
    left = left_ref[...].T
    for right_ref, out_ref in zip(refs[:count], refs[-count:]):
        out_ref[...] = mm(left, right_ref[...], ((1,), (0,))).astype(BF16)


def partner(value, axis, k):
    size = lax.axis_size(axis)
    return lax.ppermute(value, axis, [(i, i ^ k) for i in range(size)])


def trade(values):
    far_first = reversed(range(1, len(values)))
    return [values[0]] + [partner(values[k], "dp", k) for k in far_first][::-1]


def body(tokens, grad_out, expert_ids, gates, w_gate, w_up, w_down):
    experts = lax.axis_size("expert")
    dp = lax.axis_size("dp")
    tok_rows, features = tokens.shape
    capacity = tok_rows // 16
    slots = experts * capacity
    hidden = w_gate.shape[2]
    chunk = slots // dp
    gate_mat, up_mat, down_mat = w_gate[0], w_up[0], w_down[0]
    shape = jax.ShapeDtypeStruct
    product = 2 * slots * features * hidden
    weights = 2 * features * hidden

    half = experts // 2
    sized = shape((slots, features), BF16)
    wide = shape((slots, hidden), BF16)
    one = shape((half, capacity, features), BF16)
    pair = shape((2, capacity, features), BF16)
    in_order = [pltpu.VMEM((slots, features), BF16)]

    ins = (expert_ids.T, gates.T, tokens)
    outs = (shape((slots, tok_rows), BF16), shape((slots, 1), F32), one, one)
    pick, weight, keep, swap = call(
        functools.partial(route_kernel, experts),
        outs,
        4 * slots * tok_rows * features,
        8 * tok_rows * features,
        limit=ROUTE_LIMIT,
        in_specs=[ANY] * 3,
        scratch_shapes=[
            *[pltpu.VMEM(array.shape, array.dtype) for array in ins],
            pltpu.SemaphoreType.DMA((3,)),
        ],
    )(*ins)
    swap_to, up_mat = lax.optimization_barrier((swap, up_mat))
    swap = partner(swap_to, "expert", 1)
    up_mat = call(load_kernel, shape(up_mat.shape, BF16), 0, 2 * weights)(up_mat)
    swap, up_mat = lax.optimization_barrier((swap, up_mat))
    sent = call(pack_back_kernel, [pair] * (half - 1), 0, 8 * slots)(keep, swap)
    row_blocks = [partner(value, "expert", 2 * (1 + k)) for k, value in enumerate(sent)][::-1]
    grad_keep, grad_swap = call(gather_scaled_kernel, (one, one), 0, 0)(pick, weight, grad_out)
    grad_swap = partner(grad_swap, "expert", 1)
    sent = call(pack_back_kernel, [pair] * (half - 1), 0, 8 * slots)(grad_keep, grad_swap)
    grad_blocks = [partner(value, "expert", 2 * (1 + k)) for k, value in enumerate(sent)][::-1]
    rows, *part_pre = call(
        functools.partial(gate_up_kernel, half),
        (sized, *[shape((2, chunk, hidden), BF16)] * dp),
        2 * product,
        2 * weights,
        scratch_shapes=in_order,
    )(keep, swap, *row_blocks, gate_mat, up_mat)
    sums = trade(part_pre)
    act_mine = call(
        functools.partial(act_kernel, dp),
        shape((chunk, hidden), BF16),
        0,
        4 * dp * chunk * hidden,
    )(*sums)
    acts = trade([act_mine] * dp)
    grad_blocks, act_mine = lax.optimization_barrier((grad_blocks, act_mine))
    grads, *part_grad = call(
        functools.partial(grad_act_kernel, half),
        (sized, *[shape((chunk, hidden), BF16)] * dp),
        product,
        weights,
        scratch_shapes=in_order,
    )(grad_keep, grad_swap, *grad_blocks, down_mat)
    grad_sums = trade(part_grad)
    pre_mine = call(
        functools.partial(grad_pre_kernel, dp),
        shape((2, chunk, hidden), BF16),
        0,
        6 * dp * chunk * hidden,
    )(*sums, *grad_sums)
    pre = trade([pre_mine] * dp)
    act, out_keep, out_swap = call(
        functools.partial(expert_out_kernel, dp),
        (wide, one, one),
        product,
        weights,
        scratch_shapes=in_order,
    )(*acts, down_mat)
    back = [pair] * (half - 1)
    out_swap = partner(out_swap, "expert", 1)
    out_near, *out_far = call(pack_back_kernel, back, 0, 8 * slots)(out_keep, out_swap)
    out_far = [partner(value, "expert", 2 * (2 + k)) for k, value in enumerate(out_far)]
    pre, out_far = lax.optimization_barrier((pre, out_far))
    gate_pre, up_pre, grad_keep, grad_swap = call(
        functools.partial(row_grad_kernel, dp),
        (wide, wide, one, one),
        2 * product,
        2 * weights,
        scratch_shapes=in_order,
    )(*pre, gate_mat, up_mat)
    grad_swap = partner(grad_swap, "expert", 1)
    out_near = partner(out_near, "expert", 2)
    grad_to = call(pack_back_kernel, back, 0, 8 * slots)(grad_keep, grad_swap)
    grad_back = [partner(value, "expert", 2 * (1 + k)) for k, value in enumerate(grad_to)]

    (grad_down,) = call(
        functools.partial(grads_kernel, 1),
        [shape((hidden, features), BF16)],
        product,
        weights,
    )(act, grads)
    grad_gate, grad_up = call(
        functools.partial(grads_kernel, 2),
        [shape((features, hidden), BF16)] * 2,
        2 * product,
        2 * weights,
        in_specs=[HERE] * 3 + [ANY],
    )(rows, gate_pre, up_pre, grad_to[0])

    full = shape((tok_rows, features), BF16)
    turned = call(turn_kernel, shape((tok_rows, slots), BF16))(pick)
    flight = dict(
        out_specs=ANY,
        scratch_shapes=[pltpu.VMEM(full.shape, BF16), pltpu.SemaphoreType.DMA((4,))],
    )
    mixed = call(
        functools.partial(scatter_scaled_kernel, half),
        full,
        2 * slots * tok_rows * features,
        4 * tok_rows * features,
        in_specs=[HERE] * (half + 3) + [ANY],
        **flight,
    )(turned, weight, out_keep, out_swap, *out_far[::-1], out_near, grad_to[0])
    grad_tokens = call(
        functools.partial(scatter_kernel, half),
        full,
        2 * slots * tok_rows * features,
        4 * tok_rows * features,
        **flight,
    )(turned, grad_keep, grad_swap, *grad_back[::-1])
    return (mixed, grad_tokens, grad_gate[None], grad_up[None], grad_down[None])


def solution(mesh):
    placed = (
        P("expert", "dp"),
        P("expert", "dp"),
        P("expert", None),
        P("expert", None),
        P("expert", "dp", None),
        P("expert", "dp", None),
        P("expert", None, "dp"),
    )
    return jax.shard_map(
        body,
        mesh=mesh,
        in_specs=placed,
        out_specs=(
            P("expert", "dp"),
            P("expert", "dp"),
            P("expert", "dp", None),
            P("expert", "dp", None),
            P("expert", None, "dp"),
        ),
        check_vma=False,
    )
```

```python
import functools

import jax
import jax.numpy as jnp
from jax import lax
from jax.experimental import pallas as pl
from jax.experimental.pallas import tpu as pltpu
from jax.sharding import PartitionSpec as P

F32 = jnp.float32
BF16 = jnp.bfloat16
MIB = 1024 * 1024
ANY = pl.BlockSpec(memory_space=pl.ANY)
HERE = pl.BlockSpec()
VMEM_LIMIT = 24 * MIB
ROUTE_LIMIT = 59 * MIB


def mm(left, right, dims):
    return lax.dot_general(left, right, (dims, ((), ())), preferred_element_type=F32)


def call(kernel, out_shape, flops=0, moved=0, limit=VMEM_LIMIT, **kwargs):
    return pl.pallas_call(
        kernel,
        out_shape=out_shape,
        cost_estimate=pl.CostEstimate(flops=flops, bytes_accessed=moved, transcendentals=0),
        compiler_params=pltpu.CompilerParams(vmem_limit_bytes=limit),
        **kwargs,
    )


def split_rows(refs, value):
    rows = value.shape[0] // len(refs)
    for k, ref in enumerate(refs):
        ref[...] = value[k * rows : (k + 1) * rows]


def join_rows(refs):
    return jnp.concatenate([ref[...] for ref in refs], axis=0)


def split_cores(keep_ref, swap_ref, value, *at):
    half, rows = keep_ref.shape[-3:-1]
    for k in range(half):
        keep_ref[(*at, k)] = value[2 * k * rows : (2 * k + 1) * rows]
        swap_ref[(*at, k)] = value[(2 * k + 1) * rows : (2 * k + 2) * rows]


def route_kernel(experts, *refs):
    pick_ref, weight_ref, keep_ref, swap_ref = refs[3:7]
    ids_ref, gates_ref, tokens_ref, sems = refs[7:]
    copies = [
        pltpu.make_async_copy(refs[k], refs[7 + k], sems.at[k]) for k in range(3)
    ]
    for copy in copies:
        copy.start()
    copies[0].wait()
    copies[1].wait()
    ids = ids_ref[...]
    tok_rows = ids.shape[1]
    slots = pick_ref.shape[0]
    inside = ids < experts
    routed = jnp.max(inside.astype(jnp.int32), axis=0, keepdims=True)
    chosen = jnp.sum(jnp.where(inside, ids, 0), axis=0, keepdims=True)
    weight = jnp.sum(jnp.where(inside, gates_ref[...], 0.0), axis=0, keepdims=True)
    key = jnp.where(routed > 0, chosen ^ lax.axis_index("expert"), experts)
    hot = lax.broadcasted_iota(jnp.int32, (experts, tok_rows), 0) == key
    earlier = lax.broadcasted_iota(jnp.int32, (tok_rows, tok_rows), 0) < lax.broadcasted_iota(
        jnp.int32, (tok_rows, tok_rows), 1
    )
    before = mm(hot.astype(F32).astype(BF16), earlier.astype(F32).astype(BF16), ((1,), (0,)))
    position = jnp.sum(jnp.where(hot, before, 0.0), axis=0, keepdims=True).astype(jnp.int32)
    slot = jnp.where(routed > 0, key * (slots // experts) + position, slots)
    pick = lax.broadcasted_iota(jnp.int32, (slots, tok_rows), 0) == slot
    slot_weight = jnp.sum(jnp.where(pick, weight, 0.0), axis=1, keepdims=True)
    weight_ref[...] = slot_weight
    pick = pick.astype(F32).astype(BF16)
    pick_ref[...] = pick
    copies[2].wait()
    rows = mm(pick, tokens_ref[...], ((1,), (0,))).astype(BF16)
    split_cores(keep_ref, swap_ref, rows)


def gather_scaled_kernel(pick_ref, weight_ref, grad_ref, mat_ref, keep_ref, swap_ref, held_ref):
    held_ref[...] = mat_ref[...]
    rows = mm(pick_ref[...], grad_ref[...], ((1,), (0,)))
    split_cores(keep_ref, swap_ref, (weight_ref[...] * rows).astype(BF16))


def hold_kernel(from_ref, to_ref):
    to_ref[...] = from_ref[...]


def pack_back_kernel(keep_ref, swap_ref, *out_refs):
    for k, out_ref in enumerate(out_refs):
        out_ref[0] = keep_ref[k + 1]
        out_ref[1] = swap_ref[k + 1]


def pieces(keep_ref, swap_ref, *refs):
    found = [keep_ref[0], swap_ref[0]]
    for ref in refs[::-1]:
        found += [ref[0], ref[1]]
    return found


def chunk_rows(rows, dp, k):
    chunk = rows // dp
    mine = lax.axis_index("dp")
    return pl.ds(pl.multiple_of((mine ^ k) * chunk, chunk), chunk)


def local_order(found, scratch, dp):
    scratch[...] = jnp.concatenate(found, axis=0)
    rows = scratch.shape[0]
    return jnp.concatenate([scratch[chunk_rows(rows, dp, k), :] for k in range(dp)], axis=0)


def gate_up_kernel(half, *refs):
    gate_ref, up_ref, local_ref, *out_refs, scratch = refs[half + 1 :]
    dp = len(out_refs)
    rows = local_order(pieces(*refs[: half + 1]), scratch, dp)
    local_ref[...] = rows
    chunk = rows.shape[0] // dp
    for at, mat in enumerate((gate_ref, up_ref)):
        part = mm(rows, mat[...], ((1,), (0,))).astype(BF16)
        for k, out_ref in enumerate(out_refs):
            out_ref[at] = part[k * chunk : (k + 1) * chunk]


def grad_act_kernel(half, *refs):
    down_ref, local_ref, *out_refs, scratch = refs[half + 1 :]
    dp = len(out_refs)
    rows = local_order(pieces(*refs[: half + 1]), scratch, dp)
    local_ref[...] = rows
    split_rows(out_refs, mm(rows, down_ref[...], ((1,), (1,))).astype(BF16))


def group_sum(refs, *at):
    total = refs[0][at].astype(F32)
    for ref in refs[1:]:
        total = total + ref[at].astype(F32)
    return total


def logistic(value):
    return 1.0 / (1.0 + jnp.exp(-value))


def act_kernel(dp, *refs):
    gate = group_sum(refs[:dp], 0)
    up = group_sum(refs[:dp], 1)
    refs[dp][...] = (gate * logistic(gate) * up).astype(BF16)


def grad_pre_kernel(dp, *refs):
    gate = group_sum(refs[:dp], 0)
    up = group_sum(refs[:dp], 1)
    grad = group_sum(refs[dp : 2 * dp], Ellipsis)
    out_ref = refs[2 * dp]
    soft = logistic(gate)
    out_ref[0] = (grad * up * (soft * (1.0 + gate * (1.0 - soft)))).astype(BF16)
    out_ref[1] = (grad * (gate * soft)).astype(BF16)


def send_back(keep_ref, swap_ref, scratch, rows, dp):
    chunk = rows.shape[0] // dp
    for k in range(dp):
        scratch[chunk_rows(rows.shape[0], dp, k), :] = rows[k * chunk : (k + 1) * chunk]
    split_cores(keep_ref, swap_ref, scratch[...])


def expert_out_kernel(dp, *refs):
    down_ref, act_ref, keep_ref, swap_ref, scratch = refs[dp:]
    act = join_rows(refs[:dp])
    act_ref[...] = act
    rows = mm(act, down_ref[...], ((1,), (0,))).astype(BF16)
    send_back(keep_ref, swap_ref, scratch, rows, dp)


def row_grad_kernel(dp, *refs):
    gate_ref, up_ref, gate_pre_ref, up_pre_ref, keep_ref, swap_ref, scratch = refs[dp:]
    gate_pre = jnp.concatenate([ref[0] for ref in refs[:dp]], axis=0)
    up_pre = jnp.concatenate([ref[1] for ref in refs[:dp]], axis=0)
    gate_pre_ref[...] = gate_pre
    up_pre_ref[...] = up_pre
    total = mm(gate_pre, gate_ref[...], ((1,), (1,))) + mm(up_pre, up_ref[...], ((1,), (1,)))
    send_back(keep_ref, swap_ref, scratch, total.astype(BF16), dp)


def returned(keep_ref, swap_ref, refs):
    found = [keep_ref[0], swap_ref[0]]
    for ref in refs[::-1]:
        found += [ref[0], ref[1]]
    return jnp.concatenate(found, axis=0)


def turn_kernel(pick_ref, out_ref):
    out_ref[...] = pick_ref[...].T


def scatter_out(pick_ref, rows, out_ref, scratch, sems):
    parts = sems.shape[0]
    size = pick_ref.shape[0] // parts
    copies = []
    for k in range(parts):
        at = pl.ds(k * size, size)
        scratch[at, :] = mm(pick_ref[at, :], rows, ((1,), (0,))).astype(BF16)
        copies.append(pltpu.make_async_copy(scratch.at[at, :], out_ref.at[at, :], sems.at[k]))
        copies[-1].start()
    for copy in copies:
        copy.wait()


def scatter_scaled_kernel(half, pick_ref, weight_ref, *refs):
    back = returned(*refs[:2], refs[2 : half + 1]).astype(F32)
    scaled = (weight_ref[...] * back).astype(BF16)
    scatter_out(pick_ref, scaled, *refs[-3:])


def scatter_kernel(half, pick_ref, *refs):
    scatter_out(pick_ref, returned(*refs[:2], refs[2 : half + 1]), *refs[-3:])


def grads_kernel(count, left_ref, *refs):
    left = left_ref[...].T
    for right_ref, out_ref in zip(refs[:count], refs[-count:]):
        out_ref[...] = mm(left, right_ref[...], ((1,), (0,))).astype(BF16)


def partner(value, axis, k):
    size = lax.axis_size(axis)
    return lax.ppermute(value, axis, [(i, i ^ k) for i in range(size)])


def trade(values):
    far_first = reversed(range(1, len(values)))
    return [values[0]] + [partner(values[k], "dp", k) for k in far_first][::-1]


def body(tokens, grad_out, expert_ids, gates, w_gate, w_up, w_down):
    experts = lax.axis_size("expert")
    dp = lax.axis_size("dp")
    tok_rows, features = tokens.shape
    capacity = tok_rows // 16
    slots = experts * capacity
    hidden = w_gate.shape[2]
    chunk = slots // dp
    gate_mat, up_mat, down_mat = w_gate[0], w_up[0], w_down[0]
    shape = jax.ShapeDtypeStruct
    product = 2 * slots * features * hidden
    weights = 2 * features * hidden

    half = experts // 2
    sized = shape((slots, features), BF16)
    wide = shape((slots, hidden), BF16)
    one = shape((half, capacity, features), BF16)
    pair = shape((2, capacity, features), BF16)
    in_order = [pltpu.VMEM((slots, features), BF16)]

    ins = (expert_ids.T, gates.T, tokens)
    outs = (shape((slots, tok_rows), BF16), shape((slots, 1), F32), one, one)
    pick, weight, keep, swap = call(
        functools.partial(route_kernel, experts),
        outs,
        4 * slots * tok_rows * features,
        8 * tok_rows * features,
        limit=ROUTE_LIMIT,
        in_specs=[ANY] * 3,
        scratch_shapes=[
            *[pltpu.VMEM(array.shape, array.dtype) for array in ins],
            pltpu.SemaphoreType.DMA((3,)),
        ],
    )(*ins)
    swap = partner(swap, "expert", 1)
    keep = call(hold_kernel, one)(keep)
    swap, keep = lax.optimization_barrier((swap, keep))
    sent = call(pack_back_kernel, [pair] * (half - 1), 0, 8 * slots)(keep, swap)
    row_blocks = [partner(value, "expert", 2 * (1 + k)) for k, value in enumerate(sent)][::-1]
    grad_keep, grad_swap, up_mat = call(
        gather_scaled_kernel, (one, one, shape(up_mat.shape, BF16)), 0, 0
    )(pick, weight, grad_out, up_mat)
    grad_swap = partner(grad_swap, "expert", 1)
    sent = call(pack_back_kernel, [pair] * (half - 1), 0, 8 * slots)(grad_keep, grad_swap)
    grad_blocks = [partner(value, "expert", 2 * (1 + k)) for k, value in enumerate(sent)][::-1]
    rows, *part_pre = call(
        functools.partial(gate_up_kernel, half),
        (sized, *[shape((2, chunk, hidden), BF16)] * dp),
        2 * product,
        2 * weights,
        scratch_shapes=in_order,
    )(keep, swap, *row_blocks, gate_mat, up_mat)
    sums = trade(part_pre)
    act_mine = call(
        functools.partial(act_kernel, dp),
        shape((chunk, hidden), BF16),
        0,
        4 * dp * chunk * hidden,
    )(*sums)
    acts = trade([act_mine] * dp)
    grad_blocks, act_mine = lax.optimization_barrier((grad_blocks, act_mine))
    grads, *part_grad = call(
        functools.partial(grad_act_kernel, half),
        (sized, *[shape((chunk, hidden), BF16)] * dp),
        product,
        weights,
        scratch_shapes=in_order,
    )(grad_keep, grad_swap, *grad_blocks, down_mat)
    grad_sums = trade(part_grad)
    pre_mine = call(
        functools.partial(grad_pre_kernel, dp),
        shape((2, chunk, hidden), BF16),
        0,
        6 * dp * chunk * hidden,
    )(*sums, *grad_sums)
    pre = trade([pre_mine] * dp)
    act, out_keep, out_swap = call(
        functools.partial(expert_out_kernel, dp),
        (wide, one, one),
        product,
        weights,
        scratch_shapes=in_order,
    )(*acts, down_mat)
    back = [pair] * (half - 1)
    out_swap = partner(out_swap, "expert", 1)
    out_near, *out_far = call(pack_back_kernel, back, 0, 8 * slots)(out_keep, out_swap)
    out_far = [partner(value, "expert", 2 * (2 + k)) for k, value in enumerate(out_far)]
    pre, out_far = lax.optimization_barrier((pre, out_far))
    gate_pre, up_pre, grad_keep, grad_swap = call(
        functools.partial(row_grad_kernel, dp),
        (wide, wide, one, one),
        2 * product,
        2 * weights,
        scratch_shapes=in_order,
    )(*pre, gate_mat, up_mat)
    grad_swap = partner(grad_swap, "expert", 1)
    out_near = partner(out_near, "expert", 2)
    grad_to = call(pack_back_kernel, back, 0, 8 * slots)(grad_keep, grad_swap)
    grad_back = [partner(value, "expert", 2 * (1 + k)) for k, value in enumerate(grad_to)]

    (grad_down,) = call(
        functools.partial(grads_kernel, 1),
        [shape((hidden, features), BF16)],
        product,
        weights,
    )(act, grads)
    grad_gate, grad_up = call(
        functools.partial(grads_kernel, 2),
        [shape((features, hidden), BF16)] * 2,
        2 * product,
        2 * weights,
        in_specs=[HERE] * 3 + [ANY],
    )(rows, gate_pre, up_pre, grad_to[0])

    full = shape((tok_rows, features), BF16)
    turned = call(turn_kernel, shape((tok_rows, slots), BF16))(pick)
    flight = dict(
        out_specs=ANY,
        scratch_shapes=[pltpu.VMEM(full.shape, BF16), pltpu.SemaphoreType.DMA((4,))],
    )
    mixed = call(
        functools.partial(scatter_scaled_kernel, half),
        full,
        2 * slots * tok_rows * features,
        4 * tok_rows * features,
        in_specs=[HERE] * (half + 3) + [ANY],
        **flight,
    )(turned, weight, out_keep, out_swap, *out_far[::-1], out_near, grad_to[0])
    grad_tokens = call(
        functools.partial(scatter_kernel, half),
        full,
        2 * slots * tok_rows * features,
        4 * tok_rows * features,
        **flight,
    )(turned, grad_keep, grad_swap, *grad_back[::-1])
    return (mixed, grad_tokens, grad_gate[None], grad_up[None], grad_down[None])


def solution(mesh):
    placed = (
        P("expert", "dp"),
        P("expert", "dp"),
        P("expert", None),
        P("expert", None),
        P("expert", "dp", None),
        P("expert", "dp", None),
        P("expert", None, "dp"),
    )
    return jax.shard_map(
        body,
        mesh=mesh,
        in_specs=placed,
        out_specs=(
            P("expert", "dp"),
            P("expert", "dp"),
            P("expert", "dp", None),
            P("expert", "dp", None),
            P("expert", None, "dp"),
        ),
        check_vma=False,
    )
```

```python
import functools

import jax
import jax.numpy as jnp
from jax import lax
from jax.experimental import pallas as pl
from jax.experimental.pallas import tpu as pltpu
from jax.sharding import PartitionSpec as P

F32 = jnp.float32
BF16 = jnp.bfloat16
MIB = 1024 * 1024
ANY = pl.BlockSpec(memory_space=pl.ANY)
HERE = pl.BlockSpec()
VMEM_LIMIT = 24 * MIB
ROUTE_LIMIT = 59 * MIB


def mm(left, right, dims):
    return lax.dot_general(left, right, (dims, ((), ())), preferred_element_type=F32)


def call(kernel, out_shape, flops=0, moved=0, limit=VMEM_LIMIT, **kwargs):
    return pl.pallas_call(
        kernel,
        out_shape=out_shape,
        cost_estimate=pl.CostEstimate(flops=flops, bytes_accessed=moved, transcendentals=0),
        compiler_params=pltpu.CompilerParams(vmem_limit_bytes=limit),
        **kwargs,
    )


def split_rows(refs, value):
    rows = value.shape[0] // len(refs)
    for k, ref in enumerate(refs):
        ref[...] = value[k * rows : (k + 1) * rows]


def join_rows(refs):
    return jnp.concatenate([ref[...] for ref in refs], axis=0)


def split_cores(keep_ref, swap_ref, value, *at):
    half, rows = keep_ref.shape[-3:-1]
    for k in range(half):
        keep_ref[(*at, k)] = value[2 * k * rows : (2 * k + 1) * rows]
        swap_ref[(*at, k)] = value[(2 * k + 1) * rows : (2 * k + 2) * rows]


def route_kernel(experts, *refs):
    pick_ref, weight_ref, keep_ref, swap_ref = refs[3:7]
    ids_ref, gates_ref, tokens_ref, sems = refs[7:]
    copies = [
        pltpu.make_async_copy(refs[k], refs[7 + k], sems.at[k]) for k in range(3)
    ]
    for copy in copies:
        copy.start()
    copies[0].wait()
    copies[1].wait()
    ids = ids_ref[...]
    tok_rows = ids.shape[1]
    slots = pick_ref.shape[0]
    inside = ids < experts
    routed = jnp.max(inside.astype(jnp.int32), axis=0, keepdims=True)
    chosen = jnp.sum(jnp.where(inside, ids, 0), axis=0, keepdims=True)
    weight = jnp.sum(jnp.where(inside, gates_ref[...], 0.0), axis=0, keepdims=True)
    key = jnp.where(routed > 0, chosen ^ lax.axis_index("expert"), experts)
    hot = lax.broadcasted_iota(jnp.int32, (experts, tok_rows), 0) == key
    earlier = lax.broadcasted_iota(jnp.int32, (tok_rows, tok_rows), 0) < lax.broadcasted_iota(
        jnp.int32, (tok_rows, tok_rows), 1
    )
    before = mm(hot.astype(F32).astype(BF16), earlier.astype(F32).astype(BF16), ((1,), (0,)))
    position = jnp.sum(jnp.where(hot, before, 0.0), axis=0, keepdims=True).astype(jnp.int32)
    slot = jnp.where(routed > 0, key * (slots // experts) + position, slots)
    pick = lax.broadcasted_iota(jnp.int32, (slots, tok_rows), 0) == slot
    slot_weight = jnp.sum(jnp.where(pick, weight, 0.0), axis=1, keepdims=True)
    weight_ref[...] = slot_weight
    pick = pick.astype(F32).astype(BF16)
    pick_ref[...] = pick
    copies[2].wait()
    rows = mm(pick, tokens_ref[...], ((1,), (0,))).astype(BF16)
    split_cores(keep_ref, swap_ref, rows)


def gather_scaled_kernel(
    pick_ref, weight_ref, grad_ref, mat_ref, keep_ref, swap_ref, held_ref, turned_ref
):
    held_ref[...] = mat_ref[...]
    pick = pick_ref[...]
    turned_ref[...] = pick.T
    rows = mm(pick, grad_ref[...], ((1,), (0,)))
    split_cores(keep_ref, swap_ref, (weight_ref[...] * rows).astype(BF16))


def hold_kernel(from_ref, to_ref):
    to_ref[...] = from_ref[...]


def pack_back_kernel(keep_ref, swap_ref, *out_refs):
    for k, out_ref in enumerate(out_refs):
        out_ref[0] = keep_ref[k + 1]
        out_ref[1] = swap_ref[k + 1]


def pieces(keep_ref, swap_ref, *refs):
    found = [keep_ref[0], swap_ref[0]]
    for ref in refs[::-1]:
        found += [ref[0], ref[1]]
    return found


def chunk_rows(rows, dp, k):
    chunk = rows // dp
    mine = lax.axis_index("dp")
    return pl.ds(pl.multiple_of((mine ^ k) * chunk, chunk), chunk)


def local_order(found, scratch, dp):
    scratch[...] = jnp.concatenate(found, axis=0)
    rows = scratch.shape[0]
    return jnp.concatenate([scratch[chunk_rows(rows, dp, k), :] for k in range(dp)], axis=0)


def gate_up_kernel(half, *refs):
    gate_ref, up_ref, local_ref, *out_refs, scratch = refs[half + 1 :]
    dp = len(out_refs)
    rows = local_order(pieces(*refs[: half + 1]), scratch, dp)
    local_ref[...] = rows
    chunk = rows.shape[0] // dp
    for at, mat in enumerate((gate_ref, up_ref)):
        part = mm(rows, mat[...], ((1,), (0,))).astype(BF16)
        for k, out_ref in enumerate(out_refs):
            out_ref[at] = part[k * chunk : (k + 1) * chunk]


def grad_act_kernel(half, *refs):
    down_ref, local_ref, *out_refs, scratch = refs[half + 1 :]
    dp = len(out_refs)
    rows = local_order(pieces(*refs[: half + 1]), scratch, dp)
    local_ref[...] = rows
    split_rows(out_refs, mm(rows, down_ref[...], ((1,), (1,))).astype(BF16))


def group_sum(refs, *at):
    total = refs[0][at].astype(F32)
    for ref in refs[1:]:
        total = total + ref[at].astype(F32)
    return total


def logistic(value):
    return 1.0 / (1.0 + jnp.exp(-value))


def act_kernel(dp, *refs):
    gate = group_sum(refs[:dp], 0)
    up = group_sum(refs[:dp], 1)
    refs[dp][...] = (gate * logistic(gate) * up).astype(BF16)


def grad_pre_kernel(dp, *refs):
    gate = group_sum(refs[:dp], 0)
    up = group_sum(refs[:dp], 1)
    grad = group_sum(refs[dp : 2 * dp], Ellipsis)
    out_ref = refs[2 * dp]
    soft = logistic(gate)
    out_ref[0] = (grad * up * (soft * (1.0 + gate * (1.0 - soft)))).astype(BF16)
    out_ref[1] = (grad * (gate * soft)).astype(BF16)


def send_back(keep_ref, swap_ref, scratch, rows, dp):
    chunk = rows.shape[0] // dp
    for k in range(dp):
        scratch[chunk_rows(rows.shape[0], dp, k), :] = rows[k * chunk : (k + 1) * chunk]
    split_cores(keep_ref, swap_ref, scratch[...])


def expert_out_kernel(dp, *refs):
    down_ref, act_ref, keep_ref, swap_ref, scratch = refs[dp:]
    act = join_rows(refs[:dp])
    act_ref[...] = act
    rows = mm(act, down_ref[...], ((1,), (0,))).astype(BF16)
    send_back(keep_ref, swap_ref, scratch, rows, dp)


def row_grad_kernel(dp, *refs):
    gate_ref, up_ref, gate_pre_ref, up_pre_ref, keep_ref, swap_ref, scratch = refs[dp:]
    gate_pre = jnp.concatenate([ref[0] for ref in refs[:dp]], axis=0)
    up_pre = jnp.concatenate([ref[1] for ref in refs[:dp]], axis=0)
    gate_pre_ref[...] = gate_pre
    up_pre_ref[...] = up_pre
    total = mm(gate_pre, gate_ref[...], ((1,), (1,))) + mm(up_pre, up_ref[...], ((1,), (1,)))
    send_back(keep_ref, swap_ref, scratch, total.astype(BF16), dp)


def returned(keep_ref, swap_ref, refs):
    found = [keep_ref[0], swap_ref[0]]
    for ref in refs[::-1]:
        found += [ref[0], ref[1]]
    return jnp.concatenate(found, axis=0)


def scatter_out(pick_ref, rows, out_ref, scratch, sems):
    parts = sems.shape[0]
    size = pick_ref.shape[0] // parts
    copies = []
    for k in range(parts):
        at = pl.ds(k * size, size)
        scratch[at, :] = mm(pick_ref[at, :], rows, ((1,), (0,))).astype(BF16)
        copies.append(pltpu.make_async_copy(scratch.at[at, :], out_ref.at[at, :], sems.at[k]))
        copies[-1].start()
    for copy in copies:
        copy.wait()


def scatter_scaled_kernel(half, pick_ref, weight_ref, *refs):
    back = returned(*refs[:2], refs[2 : half + 1]).astype(F32)
    scaled = (weight_ref[...] * back).astype(BF16)
    scatter_out(pick_ref, scaled, *refs[-3:])


def scatter_kernel(half, pick_ref, *refs):
    scatter_out(pick_ref, returned(*refs[:2], refs[2 : half + 1]), *refs[-3:])


def grads_kernel(count, left_ref, *refs):
    left = left_ref[...].T
    for right_ref, out_ref in zip(refs[:count], refs[-count:]):
        out_ref[...] = mm(left, right_ref[...], ((1,), (0,))).astype(BF16)


def partner(value, axis, k):
    size = lax.axis_size(axis)
    return lax.ppermute(value, axis, [(i, i ^ k) for i in range(size)])


def trade(values):
    far_first = reversed(range(1, len(values)))
    return [values[0]] + [partner(values[k], "dp", k) for k in far_first][::-1]


def body(tokens, grad_out, expert_ids, gates, w_gate, w_up, w_down):
    experts = lax.axis_size("expert")
    dp = lax.axis_size("dp")
    tok_rows, features = tokens.shape
    capacity = tok_rows // 16
    slots = experts * capacity
    hidden = w_gate.shape[2]
    chunk = slots // dp
    gate_mat, up_mat, down_mat = w_gate[0], w_up[0], w_down[0]
    shape = jax.ShapeDtypeStruct
    product = 2 * slots * features * hidden
    weights = 2 * features * hidden

    half = experts // 2
    sized = shape((slots, features), BF16)
    wide = shape((slots, hidden), BF16)
    one = shape((half, capacity, features), BF16)
    pair = shape((2, capacity, features), BF16)
    in_order = [pltpu.VMEM((slots, features), BF16)]

    ins = (expert_ids.T, gates.T, tokens)
    outs = (shape((slots, tok_rows), BF16), shape((slots, 1), F32), one, one)
    pick, weight, keep, swap = call(
        functools.partial(route_kernel, experts),
        outs,
        4 * slots * tok_rows * features,
        8 * tok_rows * features,
        limit=ROUTE_LIMIT,
        in_specs=[ANY] * 3,
        scratch_shapes=[
            *[pltpu.VMEM(array.shape, array.dtype) for array in ins],
            pltpu.SemaphoreType.DMA((3,)),
        ],
    )(*ins)
    swap = partner(swap, "expert", 1)
    keep = call(hold_kernel, one)(keep)
    swap, keep = lax.optimization_barrier((swap, keep))
    sent = call(pack_back_kernel, [pair] * (half - 1), 0, 8 * slots)(keep, swap)
    row_blocks = [partner(value, "expert", 2 * (1 + k)) for k, value in enumerate(sent)][::-1]
    grad_keep, grad_swap, up_mat, turned = call(
        gather_scaled_kernel,
        (one, one, shape(up_mat.shape, BF16), shape((tok_rows, slots), BF16)),
        0,
        0,
    )(pick, weight, grad_out, up_mat)
    grad_swap = partner(grad_swap, "expert", 1)
    sent = call(pack_back_kernel, [pair] * (half - 1), 0, 8 * slots)(grad_keep, grad_swap)
    grad_blocks = [partner(value, "expert", 2 * (1 + k)) for k, value in enumerate(sent)][::-1]
    rows, *part_pre = call(
        functools.partial(gate_up_kernel, half),
        (sized, *[shape((2, chunk, hidden), BF16)] * dp),
        2 * product,
        2 * weights,
        scratch_shapes=in_order,
    )(keep, swap, *row_blocks, gate_mat, up_mat)
    sums = trade(part_pre)
    act_mine = call(
        functools.partial(act_kernel, dp),
        shape((chunk, hidden), BF16),
        0,
        4 * dp * chunk * hidden,
    )(*sums)
    acts = trade([act_mine] * dp)
    grad_blocks, act_mine = lax.optimization_barrier((grad_blocks, act_mine))
    grads, *part_grad = call(
        functools.partial(grad_act_kernel, half),
        (sized, *[shape((chunk, hidden), BF16)] * dp),
        product,
        weights,
        scratch_shapes=in_order,
    )(grad_keep, grad_swap, *grad_blocks, down_mat)
    grad_sums = trade(part_grad)
    pre_mine = call(
        functools.partial(grad_pre_kernel, dp),
        shape((2, chunk, hidden), BF16),
        0,
        6 * dp * chunk * hidden,
    )(*sums, *grad_sums)
    pre = trade([pre_mine] * dp)
    act, out_keep, out_swap = call(
        functools.partial(expert_out_kernel, dp),
        (wide, one, one),
        product,
        weights,
        scratch_shapes=in_order,
    )(*acts, down_mat)
    back = [pair] * (half - 1)
    out_swap = partner(out_swap, "expert", 1)
    out_near, *out_far = call(pack_back_kernel, back, 0, 8 * slots)(out_keep, out_swap)
    out_far = [partner(value, "expert", 2 * (2 + k)) for k, value in enumerate(out_far)]
    pre, out_far = lax.optimization_barrier((pre, out_far))
    gate_pre, up_pre, grad_keep, grad_swap = call(
        functools.partial(row_grad_kernel, dp),
        (wide, wide, one, one),
        2 * product,
        2 * weights,
        scratch_shapes=in_order,
    )(*pre, gate_mat, up_mat)
    grad_swap = partner(grad_swap, "expert", 1)
    out_near = partner(out_near, "expert", 2)
    grad_to = call(pack_back_kernel, back, 0, 8 * slots)(grad_keep, grad_swap)
    grad_back = [partner(value, "expert", 2 * (1 + k)) for k, value in enumerate(grad_to)]

    (grad_down,) = call(
        functools.partial(grads_kernel, 1),
        [shape((hidden, features), BF16)],
        product,
        weights,
    )(act, grads)
    grad_gate, grad_up = call(
        functools.partial(grads_kernel, 2),
        [shape((features, hidden), BF16)] * 2,
        2 * product,
        2 * weights,
        in_specs=[HERE] * 3 + [ANY],
    )(rows, gate_pre, up_pre, grad_to[0])

    full = shape((tok_rows, features), BF16)
    flight = dict(
        out_specs=ANY,
        scratch_shapes=[pltpu.VMEM(full.shape, BF16), pltpu.SemaphoreType.DMA((4,))],
    )
    mixed = call(
        functools.partial(scatter_scaled_kernel, half),
        full,
        2 * slots * tok_rows * features,
        4 * tok_rows * features,
        in_specs=[HERE] * (half + 3) + [ANY],
        **flight,
    )(turned, weight, out_keep, out_swap, *out_far[::-1], out_near, grad_to[0])
    grad_tokens = call(
        functools.partial(scatter_kernel, half),
        full,
        2 * slots * tok_rows * features,
        4 * tok_rows * features,
        **flight,
    )(turned, grad_keep, grad_swap, *grad_back[::-1])
    return (mixed, grad_tokens, grad_gate[None], grad_up[None], grad_down[None])


def solution(mesh):
    placed = (
        P("expert", "dp"),
        P("expert", "dp"),
        P("expert", None),
        P("expert", None),
        P("expert", "dp", None),
        P("expert", "dp", None),
        P("expert", None, "dp"),
    )
    return jax.shard_map(
        body,
        mesh=mesh,
        in_specs=placed,
        out_specs=(
            P("expert", "dp"),
            P("expert", "dp"),
            P("expert", "dp", None),
            P("expert", "dp", None),
            P("expert", None, "dp"),
        ),
        check_vma=False,
    )
```

```python
import functools

import jax
import jax.numpy as jnp
from jax import lax
from jax.experimental import pallas as pl
from jax.experimental.pallas import tpu as pltpu
from jax.sharding import PartitionSpec as P

F32 = jnp.float32
BF16 = jnp.bfloat16
MIB = 1024 * 1024
ANY = pl.BlockSpec(memory_space=pl.ANY)
HERE = pl.BlockSpec()
VMEM_LIMIT = 24 * MIB
ROUTE_LIMIT = 59 * MIB


def mm(left, right, dims):
    return lax.dot_general(left, right, (dims, ((), ())), preferred_element_type=F32)


def call(kernel, out_shape, flops=0, moved=0, limit=VMEM_LIMIT, **kwargs):
    return pl.pallas_call(
        kernel,
        out_shape=out_shape,
        cost_estimate=pl.CostEstimate(flops=flops, bytes_accessed=moved, transcendentals=0),
        compiler_params=pltpu.CompilerParams(vmem_limit_bytes=limit),
        **kwargs,
    )


def split_rows(refs, value):
    rows = value.shape[0] // len(refs)
    for k, ref in enumerate(refs):
        ref[...] = value[k * rows : (k + 1) * rows]


def join_rows(refs):
    return jnp.concatenate([ref[...] for ref in refs], axis=0)


def split_cores(keep_ref, swap_ref, value, *at):
    half, rows = keep_ref.shape[-3:-1]
    for k in range(half):
        keep_ref[(*at, k)] = value[2 * k * rows : (2 * k + 1) * rows]
        swap_ref[(*at, k)] = value[(2 * k + 1) * rows : (2 * k + 2) * rows]


def route_kernel(experts, *refs):
    pick_ref, weight_ref, keep_ref, swap_ref = refs[3:7]
    ids_ref, gates_ref, tokens_ref, sems = refs[7:]
    copies = [
        pltpu.make_async_copy(refs[k], refs[7 + k], sems.at[k]) for k in range(3)
    ]
    for copy in copies:
        copy.start()
    copies[0].wait()
    copies[1].wait()
    ids = ids_ref[...]
    tok_rows = ids.shape[1]
    slots = pick_ref.shape[0]
    inside = ids < experts
    routed = jnp.max(inside.astype(jnp.int32), axis=0, keepdims=True)
    chosen = jnp.sum(jnp.where(inside, ids, 0), axis=0, keepdims=True)
    weight = jnp.sum(jnp.where(inside, gates_ref[...], 0.0), axis=0, keepdims=True)
    key = jnp.where(routed > 0, chosen ^ lax.axis_index("expert"), experts)
    hot = lax.broadcasted_iota(jnp.int32, (experts, tok_rows), 0) == key
    earlier = lax.broadcasted_iota(jnp.int32, (tok_rows, tok_rows), 0) < lax.broadcasted_iota(
        jnp.int32, (tok_rows, tok_rows), 1
    )
    before = mm(hot.astype(F32).astype(BF16), earlier.astype(F32).astype(BF16), ((1,), (0,)))
    position = jnp.sum(jnp.where(hot, before, 0.0), axis=0, keepdims=True).astype(jnp.int32)
    slot = jnp.where(routed > 0, key * (slots // experts) + position, slots)
    pick = lax.broadcasted_iota(jnp.int32, (slots, tok_rows), 0) == slot
    slot_weight = jnp.sum(jnp.where(pick, weight, 0.0), axis=1, keepdims=True)
    weight_ref[...] = slot_weight
    pick = pick.astype(F32).astype(BF16)
    pick_ref[...] = pick
    copies[2].wait()
    rows = mm(pick, tokens_ref[...], ((1,), (0,))).astype(BF16)
    split_cores(keep_ref, swap_ref, rows)


def gather_scaled_kernel(
    pick_ref, weight_ref, grad_ref, mat_ref, keep_ref, swap_ref, held_ref, turned_ref
):
    held_ref[...] = mat_ref[...]
    pick = pick_ref[...]
    turned_ref[...] = pick.T
    rows = mm(pick, grad_ref[...], ((1,), (0,)))
    split_cores(keep_ref, swap_ref, (weight_ref[...] * rows).astype(BF16))


def hold_kernel(from_ref, to_ref):
    to_ref[...] = from_ref[...]


def pack_back_kernel(keep_ref, swap_ref, *out_refs):
    for k, out_ref in enumerate(out_refs):
        out_ref[0] = keep_ref[k + 1]
        out_ref[1] = swap_ref[k + 1]


def pieces(keep_ref, swap_ref, *refs):
    found = [keep_ref[0], swap_ref[0]]
    for ref in refs[::-1]:
        found += [ref[0], ref[1]]
    return found


def turned_step(dp, k):
    bits = dp.bit_length() - 1
    low = bits // 2
    return ((k << low) | (k >> (bits - low))) & (dp - 1)


def chunk_rows(rows, dp, k):
    chunk = rows // dp
    mine = lax.axis_index("dp")
    step = jnp.where(lax.axis_index("expert") % 2 == 0, k, turned_step(dp, k))
    return pl.ds(pl.multiple_of((mine ^ step) * chunk, chunk), chunk)


def local_order(found, scratch, dp):
    scratch[...] = jnp.concatenate(found, axis=0)
    rows = scratch.shape[0]
    return jnp.concatenate([scratch[chunk_rows(rows, dp, k), :] for k in range(dp)], axis=0)


def gate_up_kernel(half, *refs):
    gate_ref, up_ref, local_ref, *out_refs, scratch = refs[half + 1 :]
    dp = len(out_refs)
    rows = local_order(pieces(*refs[: half + 1]), scratch, dp)
    local_ref[...] = rows
    chunk = rows.shape[0] // dp
    for at, mat in enumerate((gate_ref, up_ref)):
        part = mm(rows, mat[...], ((1,), (0,))).astype(BF16)
        for k, out_ref in enumerate(out_refs):
            out_ref[at] = part[k * chunk : (k + 1) * chunk]


def grad_act_kernel(half, *refs):
    down_ref, local_ref, *out_refs, scratch = refs[half + 1 :]
    dp = len(out_refs)
    rows = local_order(pieces(*refs[: half + 1]), scratch, dp)
    local_ref[...] = rows
    split_rows(out_refs, mm(rows, down_ref[...], ((1,), (1,))).astype(BF16))


def group_sum(refs, *at):
    total = refs[0][at].astype(F32)
    for ref in refs[1:]:
        total = total + ref[at].astype(F32)
    return total


def logistic(value):
    return 1.0 / (1.0 + jnp.exp(-value))


def act_kernel(dp, *refs):
    gate = group_sum(refs[:dp], 0)
    up = group_sum(refs[:dp], 1)
    refs[dp][...] = (gate * logistic(gate) * up).astype(BF16)


def grad_pre_kernel(dp, *refs):
    gate = group_sum(refs[:dp], 0)
    up = group_sum(refs[:dp], 1)
    grad = group_sum(refs[dp : 2 * dp], Ellipsis)
    out_ref = refs[2 * dp]
    soft = logistic(gate)
    out_ref[0] = (grad * up * (soft * (1.0 + gate * (1.0 - soft)))).astype(BF16)
    out_ref[1] = (grad * (gate * soft)).astype(BF16)


def send_back(keep_ref, swap_ref, scratch, rows, dp):
    chunk = rows.shape[0] // dp
    for k in range(dp):
        scratch[chunk_rows(rows.shape[0], dp, k), :] = rows[k * chunk : (k + 1) * chunk]
    split_cores(keep_ref, swap_ref, scratch[...])


def expert_out_kernel(dp, *refs):
    down_ref, act_ref, keep_ref, swap_ref, scratch = refs[dp:]
    act = join_rows(refs[:dp])
    act_ref[...] = act
    rows = mm(act, down_ref[...], ((1,), (0,))).astype(BF16)
    send_back(keep_ref, swap_ref, scratch, rows, dp)


def row_grad_kernel(dp, *refs):
    gate_ref, up_ref, gate_pre_ref, up_pre_ref, keep_ref, swap_ref, scratch = refs[dp:]
    gate_pre = jnp.concatenate([ref[0] for ref in refs[:dp]], axis=0)
    up_pre = jnp.concatenate([ref[1] for ref in refs[:dp]], axis=0)
    gate_pre_ref[...] = gate_pre
    up_pre_ref[...] = up_pre
    total = mm(gate_pre, gate_ref[...], ((1,), (1,))) + mm(up_pre, up_ref[...], ((1,), (1,)))
    send_back(keep_ref, swap_ref, scratch, total.astype(BF16), dp)


def returned(keep_ref, swap_ref, refs):
    found = [keep_ref[0], swap_ref[0]]
    for ref in refs[::-1]:
        found += [ref[0], ref[1]]
    return jnp.concatenate(found, axis=0)


def scatter_out(pick_ref, rows, out_ref, scratch, sems):
    parts = sems.shape[0]
    size = pick_ref.shape[0] // parts
    copies = []
    for k in range(parts):
        at = pl.ds(k * size, size)
        scratch[at, :] = mm(pick_ref[at, :], rows, ((1,), (0,))).astype(BF16)
        copies.append(pltpu.make_async_copy(scratch.at[at, :], out_ref.at[at, :], sems.at[k]))
        copies[-1].start()
    for copy in copies:
        copy.wait()


def scatter_scaled_kernel(half, pick_ref, weight_ref, *refs):
    back = returned(*refs[:2], refs[2 : half + 1]).astype(F32)
    scaled = (weight_ref[...] * back).astype(BF16)
    scatter_out(pick_ref, scaled, *refs[-3:])


def scatter_kernel(half, pick_ref, *refs):
    scatter_out(pick_ref, returned(*refs[:2], refs[2 : half + 1]), *refs[-3:])


def grads_kernel(count, left_ref, *refs):
    left = left_ref[...].T
    for right_ref, out_ref in zip(refs[:count], refs[-count:]):
        out_ref[...] = mm(left, right_ref[...], ((1,), (0,))).astype(BF16)


def partner(value, axis, k):
    size = lax.axis_size(axis)
    return lax.ppermute(value, axis, [(i, i ^ k) for i in range(size)])


def dp_partner(value, k):
    size, experts = lax.axis_size("dp"), lax.axis_size("expert")
    steps = (k, turned_step(size, k))
    pairs = [
        (i * experts + e, (i ^ steps[e % 2]) * experts + e)
        for i in range(size)
        for e in range(experts)
    ]
    return lax.ppermute(value, ("dp", "expert"), pairs)


def trade(values):
    far_first = reversed(range(1, len(values)))
    return [values[0]] + [dp_partner(values[k], k) for k in far_first][::-1]


def body(tokens, grad_out, expert_ids, gates, w_gate, w_up, w_down):
    experts = lax.axis_size("expert")
    dp = lax.axis_size("dp")
    tok_rows, features = tokens.shape
    capacity = tok_rows // 16
    slots = experts * capacity
    hidden = w_gate.shape[2]
    chunk = slots // dp
    gate_mat, up_mat, down_mat = w_gate[0], w_up[0], w_down[0]
    shape = jax.ShapeDtypeStruct
    product = 2 * slots * features * hidden
    weights = 2 * features * hidden

    half = experts // 2
    sized = shape((slots, features), BF16)
    wide = shape((slots, hidden), BF16)
    one = shape((half, capacity, features), BF16)
    pair = shape((2, capacity, features), BF16)
    in_order = [pltpu.VMEM((slots, features), BF16)]

    ins = (expert_ids.T, gates.T, tokens)
    outs = (shape((slots, tok_rows), BF16), shape((slots, 1), F32), one, one)
    pick, weight, keep, swap = call(
        functools.partial(route_kernel, experts),
        outs,
        4 * slots * tok_rows * features,
        8 * tok_rows * features,
        limit=ROUTE_LIMIT,
        in_specs=[ANY] * 3,
        scratch_shapes=[
            *[pltpu.VMEM(array.shape, array.dtype) for array in ins],
            pltpu.SemaphoreType.DMA((3,)),
        ],
    )(*ins)
    swap = partner(swap, "expert", 1)
    keep = call(hold_kernel, one)(keep)
    swap, keep = lax.optimization_barrier((swap, keep))
    sent = call(pack_back_kernel, [pair] * (half - 1), 0, 8 * slots)(keep, swap)
    row_blocks = [partner(value, "expert", 2 * (1 + k)) for k, value in enumerate(sent)][::-1]
    grad_keep, grad_swap, up_mat, turned = call(
        gather_scaled_kernel,
        (one, one, shape(up_mat.shape, BF16), shape((tok_rows, slots), BF16)),
        0,
        0,
    )(pick, weight, grad_out, up_mat)
    grad_swap = partner(grad_swap, "expert", 1)
    sent = call(pack_back_kernel, [pair] * (half - 1), 0, 8 * slots)(grad_keep, grad_swap)
    grad_blocks = [partner(value, "expert", 2 * (1 + k)) for k, value in enumerate(sent)][::-1]
    rows, *part_pre = call(
        functools.partial(gate_up_kernel, half),
        (sized, *[shape((2, chunk, hidden), BF16)] * dp),
        2 * product,
        2 * weights,
        scratch_shapes=in_order,
    )(keep, swap, *row_blocks, gate_mat, up_mat)
    sums = trade(part_pre)
    act_mine = call(
        functools.partial(act_kernel, dp),
        shape((chunk, hidden), BF16),
        0,
        4 * dp * chunk * hidden,
    )(*sums)
    acts = trade([act_mine] * dp)
    grad_blocks, act_mine = lax.optimization_barrier((grad_blocks, act_mine))
    grads, *part_grad = call(
        functools.partial(grad_act_kernel, half),
        (sized, *[shape((chunk, hidden), BF16)] * dp),
        product,
        weights,
        scratch_shapes=in_order,
    )(grad_keep, grad_swap, *grad_blocks, down_mat)
    grad_sums = trade(part_grad)
    pre_mine = call(
        functools.partial(grad_pre_kernel, dp),
        shape((2, chunk, hidden), BF16),
        0,
        6 * dp * chunk * hidden,
    )(*sums, *grad_sums)
    pre = trade([pre_mine] * dp)
    act, out_keep, out_swap = call(
        functools.partial(expert_out_kernel, dp),
        (wide, one, one),
        product,
        weights,
        scratch_shapes=in_order,
    )(*acts, down_mat)
    back = [pair] * (half - 1)
    out_swap = partner(out_swap, "expert", 1)
    out_near, *out_far = call(pack_back_kernel, back, 0, 8 * slots)(out_keep, out_swap)
    out_far = [partner(value, "expert", 2 * (2 + k)) for k, value in enumerate(out_far)]
    pre, out_far = lax.optimization_barrier((pre, out_far))
    gate_pre, up_pre, grad_keep, grad_swap = call(
        functools.partial(row_grad_kernel, dp),
        (wide, wide, one, one),
        2 * product,
        2 * weights,
        scratch_shapes=in_order,
    )(*pre, gate_mat, up_mat)
    grad_swap = partner(grad_swap, "expert", 1)
    out_near = partner(out_near, "expert", 2)
    grad_to = call(pack_back_kernel, back, 0, 8 * slots)(grad_keep, grad_swap)
    grad_back = [partner(value, "expert", 2 * (1 + k)) for k, value in enumerate(grad_to)]

    (grad_down,) = call(
        functools.partial(grads_kernel, 1),
        [shape((hidden, features), BF16)],
        product,
        weights,
    )(act, grads)
    grad_gate, grad_up = call(
        functools.partial(grads_kernel, 2),
        [shape((features, hidden), BF16)] * 2,
        2 * product,
        2 * weights,
        in_specs=[HERE] * 3 + [ANY],
    )(rows, gate_pre, up_pre, grad_to[0])

    full = shape((tok_rows, features), BF16)
    flight = dict(
        out_specs=ANY,
        scratch_shapes=[pltpu.VMEM(full.shape, BF16), pltpu.SemaphoreType.DMA((4,))],
    )
    mixed = call(
        functools.partial(scatter_scaled_kernel, half),
        full,
        2 * slots * tok_rows * features,
        4 * tok_rows * features,
        in_specs=[HERE] * (half + 3) + [ANY],
        **flight,
    )(turned, weight, out_keep, out_swap, *out_far[::-1], out_near, grad_to[0])
    grad_tokens = call(
        functools.partial(scatter_kernel, half),
        full,
        2 * slots * tok_rows * features,
        4 * tok_rows * features,
        **flight,
    )(turned, grad_keep, grad_swap, *grad_back[::-1])
    return (mixed, grad_tokens, grad_gate[None], grad_up[None], grad_down[None])


def solution(mesh):
    placed = (
        P("expert", "dp"),
        P("expert", "dp"),
        P("expert", None),
        P("expert", None),
        P("expert", "dp", None),
        P("expert", "dp", None),
        P("expert", None, "dp"),
    )
    return jax.shard_map(
        body,
        mesh=mesh,
        in_specs=placed,
        out_specs=(
            P("expert", "dp"),
            P("expert", "dp"),
            P("expert", "dp", None),
            P("expert", "dp", None),
            P("expert", None, "dp"),
        ),
        check_vma=False,
    )
```

```python
import functools

import jax
import jax.numpy as jnp
from jax import lax
from jax.experimental import pallas as pl
from jax.experimental.pallas import tpu as pltpu
from jax.sharding import PartitionSpec as P

F32 = jnp.float32
BF16 = jnp.bfloat16
MIB = 1024 * 1024
ANY = pl.BlockSpec(memory_space=pl.ANY)
HERE = pl.BlockSpec()
VMEM_LIMIT = 24 * MIB
ROUTE_LIMIT = 59 * MIB


def mm(left, right, dims):
    return lax.dot_general(left, right, (dims, ((), ())), preferred_element_type=F32)


def call(kernel, out_shape, flops=0, moved=0, limit=VMEM_LIMIT, **kwargs):
    return pl.pallas_call(
        kernel,
        out_shape=out_shape,
        cost_estimate=pl.CostEstimate(flops=flops, bytes_accessed=moved, transcendentals=0),
        compiler_params=pltpu.CompilerParams(vmem_limit_bytes=limit),
        **kwargs,
    )


def split_rows(refs, value):
    rows = value.shape[0] // len(refs)
    for k, ref in enumerate(refs):
        ref[...] = value[k * rows : (k + 1) * rows]


def join_rows(refs):
    return jnp.concatenate([ref[...] for ref in refs], axis=0)


def split_cores(keep_ref, swap_ref, value, *at):
    half, rows = keep_ref.shape[-3:-1]
    for k in range(half):
        keep_ref[(*at, k)] = value[2 * k * rows : (2 * k + 1) * rows]
        swap_ref[(*at, k)] = value[(2 * k + 1) * rows : (2 * k + 2) * rows]


def route_kernel(experts, *refs):
    pick_ref, weight_ref, keep_ref, swap_ref = refs[3:7]
    ids_ref, gates_ref, tokens_ref, sems = refs[7:]
    copies = [
        pltpu.make_async_copy(refs[k], refs[7 + k], sems.at[k]) for k in range(3)
    ]
    for copy in copies:
        copy.start()
    copies[0].wait()
    copies[1].wait()
    ids = ids_ref[...]
    tok_rows = ids.shape[1]
    slots = pick_ref.shape[0]
    inside = ids < experts
    routed = jnp.max(inside.astype(jnp.int32), axis=0, keepdims=True)
    chosen = jnp.sum(jnp.where(inside, ids, 0), axis=0, keepdims=True)
    weight = jnp.sum(jnp.where(inside, gates_ref[...], 0.0), axis=0, keepdims=True)
    key = jnp.where(routed > 0, chosen ^ lax.axis_index("expert"), experts)
    hot = lax.broadcasted_iota(jnp.int32, (experts, tok_rows), 0) == key
    earlier = lax.broadcasted_iota(jnp.int32, (tok_rows, tok_rows), 0) < lax.broadcasted_iota(
        jnp.int32, (tok_rows, tok_rows), 1
    )
    before = mm(hot.astype(F32).astype(BF16), earlier.astype(F32).astype(BF16), ((1,), (0,)))
    position = jnp.sum(jnp.where(hot, before, 0.0), axis=0, keepdims=True).astype(jnp.int32)
    slot = jnp.where(routed > 0, key * (slots // experts) + position, slots)
    pick = lax.broadcasted_iota(jnp.int32, (slots, tok_rows), 0) == slot
    slot_weight = jnp.sum(jnp.where(pick, weight, 0.0), axis=1, keepdims=True)
    weight_ref[...] = slot_weight
    pick = pick.astype(F32).astype(BF16)
    pick_ref[...] = pick
    copies[2].wait()
    rows = mm(pick, tokens_ref[...], ((1,), (0,))).astype(BF16)
    split_cores(keep_ref, swap_ref, rows)


def gather_scaled_kernel(
    pick_ref, weight_ref, grad_ref, mat_ref, keep_ref, swap_ref, held_ref, turned_ref
):
    held_ref[...] = mat_ref[...]
    pick = pick_ref[...]
    turned_ref[...] = pick.T
    rows = mm(pick, grad_ref[...], ((1,), (0,)))
    split_cores(keep_ref, swap_ref, (weight_ref[...] * rows).astype(BF16))


def hold_kernel(from_ref, to_ref):
    to_ref[...] = from_ref[...]


def pack_back_kernel(keep_ref, swap_ref, *out_refs):
    for k, out_ref in enumerate(out_refs):
        out_ref[0] = keep_ref[k + 1]
        out_ref[1] = swap_ref[k + 1]


def pieces(keep_ref, swap_ref, *refs):
    found = [keep_ref[0], swap_ref[0]]
    for ref in refs[::-1]:
        found += [ref[0], ref[1]]
    return found


def chunk_rows(rows, dp, k):
    chunk = rows // dp
    mine = lax.axis_index("dp")
    return pl.ds(pl.multiple_of((mine ^ k) * chunk, chunk), chunk)


def local_order(found, scratch, dp):
    scratch[...] = jnp.concatenate(found, axis=0)
    rows = scratch.shape[0]
    return jnp.concatenate([scratch[chunk_rows(rows, dp, k), :] for k in range(dp)], axis=0)


def gate_up_kernel(half, *refs):
    gate_ref, up_ref, local_ref, *out_refs, scratch = refs[half + 1 :]
    dp = len(out_refs)
    rows = local_order(pieces(*refs[: half + 1]), scratch, dp)
    local_ref[...] = rows
    chunk = rows.shape[0] // dp
    for at, mat in enumerate((gate_ref, up_ref)):
        part = mm(rows, mat[...], ((1,), (0,))).astype(BF16)
        for k, out_ref in enumerate(out_refs):
            out_ref[at] = part[k * chunk : (k + 1) * chunk]


def grad_act_kernel(half, dp, *refs):
    sums, refs = refs[:dp], refs[dp:]
    down_ref, local_ref, *out_refs, scratch = refs[half + 1 :]
    gate = group_sum(sums, 0)
    act = (gate * logistic(gate) * group_sum(sums, 1)).astype(BF16)
    rows = local_order(pieces(*refs[: half + 1]), scratch, dp)
    local_ref[...] = rows
    part = mm(rows, down_ref[...], ((1,), (1,))).astype(BF16)
    chunk = rows.shape[0] // dp
    for k, out_ref in enumerate(out_refs):
        out_ref[0] = act
        out_ref[1] = part[k * chunk : (k + 1) * chunk]


def group_sum(refs, *at):
    total = refs[0][at].astype(F32)
    for ref in refs[1:]:
        total = total + ref[at].astype(F32)
    return total


def logistic(value):
    return 1.0 / (1.0 + jnp.exp(-value))


def grad_pre_kernel(dp, *refs):
    gate = group_sum(refs[:dp], 0)
    up = group_sum(refs[:dp], 1)
    grad = group_sum(refs[dp : 2 * dp], 1)
    out_ref = refs[2 * dp]
    soft = logistic(gate)
    out_ref[0] = (grad * up * (soft * (1.0 + gate * (1.0 - soft)))).astype(BF16)
    out_ref[1] = (grad * (gate * soft)).astype(BF16)


def send_back(keep_ref, swap_ref, scratch, rows, dp):
    chunk = rows.shape[0] // dp
    for k in range(dp):
        scratch[chunk_rows(rows.shape[0], dp, k), :] = rows[k * chunk : (k + 1) * chunk]
    split_cores(keep_ref, swap_ref, scratch[...])


def expert_out_kernel(dp, *refs):
    down_ref, act_ref, keep_ref, swap_ref, scratch = refs[dp:]
    act = jnp.concatenate([ref[0] for ref in refs[:dp]], axis=0)
    act_ref[...] = act
    rows = mm(act, down_ref[...], ((1,), (0,))).astype(BF16)
    send_back(keep_ref, swap_ref, scratch, rows, dp)


def row_grad_kernel(dp, *refs):
    gate_ref, up_ref, gate_pre_ref, up_pre_ref, keep_ref, swap_ref, scratch = refs[dp:]
    gate_pre = jnp.concatenate([ref[0] for ref in refs[:dp]], axis=0)
    up_pre = jnp.concatenate([ref[1] for ref in refs[:dp]], axis=0)
    gate_pre_ref[...] = gate_pre
    up_pre_ref[...] = up_pre
    total = mm(gate_pre, gate_ref[...], ((1,), (1,))) + mm(up_pre, up_ref[...], ((1,), (1,)))
    send_back(keep_ref, swap_ref, scratch, total.astype(BF16), dp)


def returned(keep_ref, swap_ref, refs):
    found = [keep_ref[0], swap_ref[0]]
    for ref in refs[::-1]:
        found += [ref[0], ref[1]]
    return jnp.concatenate(found, axis=0)


def scatter_out(pick_ref, rows, out_ref, scratch, sems):
    parts = sems.shape[0]
    size = pick_ref.shape[0] // parts
    copies = []
    for k in range(parts):
        at = pl.ds(k * size, size)
        scratch[at, :] = mm(pick_ref[at, :], rows, ((1,), (0,))).astype(BF16)
        copies.append(pltpu.make_async_copy(scratch.at[at, :], out_ref.at[at, :], sems.at[k]))
        copies[-1].start()
    for copy in copies:
        copy.wait()


def scatter_scaled_kernel(half, pick_ref, weight_ref, *refs):
    back = returned(*refs[:2], refs[2 : half + 1]).astype(F32)
    scaled = (weight_ref[...] * back).astype(BF16)
    scatter_out(pick_ref, scaled, *refs[-3:])


def scatter_kernel(half, pick_ref, *refs):
    scatter_out(pick_ref, returned(*refs[:2], refs[2 : half + 1]), *refs[-3:])


def grads_kernel(count, left_ref, *refs):
    left = left_ref[...].T
    for right_ref, out_ref in zip(refs[:count], refs[-count:]):
        out_ref[...] = mm(left, right_ref[...], ((1,), (0,))).astype(BF16)


def partner(value, axis, k):
    size = lax.axis_size(axis)
    return lax.ppermute(value, axis, [(i, i ^ k) for i in range(size)])


def trade(values):
    far_first = reversed(range(1, len(values)))
    return [values[0]] + [partner(values[k], "dp", k) for k in far_first][::-1]


def body(tokens, grad_out, expert_ids, gates, w_gate, w_up, w_down):
    experts = lax.axis_size("expert")
    dp = lax.axis_size("dp")
    tok_rows, features = tokens.shape
    capacity = tok_rows // 16
    slots = experts * capacity
    hidden = w_gate.shape[2]
    chunk = slots // dp
    gate_mat, up_mat, down_mat = w_gate[0], w_up[0], w_down[0]
    shape = jax.ShapeDtypeStruct
    product = 2 * slots * features * hidden
    weights = 2 * features * hidden

    half = experts // 2
    sized = shape((slots, features), BF16)
    wide = shape((slots, hidden), BF16)
    one = shape((half, capacity, features), BF16)
    pair = shape((2, capacity, features), BF16)
    in_order = [pltpu.VMEM((slots, features), BF16)]

    ins = (expert_ids.T, gates.T, tokens)
    outs = (shape((slots, tok_rows), BF16), shape((slots, 1), F32), one, one)
    pick, weight, keep, swap = call(
        functools.partial(route_kernel, experts),
        outs,
        4 * slots * tok_rows * features,
        8 * tok_rows * features,
        limit=ROUTE_LIMIT,
        in_specs=[ANY] * 3,
        scratch_shapes=[
            *[pltpu.VMEM(array.shape, array.dtype) for array in ins],
            pltpu.SemaphoreType.DMA((3,)),
        ],
    )(*ins)
    swap = partner(swap, "expert", 1)
    keep = call(hold_kernel, one)(keep)
    swap, keep = lax.optimization_barrier((swap, keep))
    sent = call(pack_back_kernel, [pair] * (half - 1), 0, 8 * slots)(keep, swap)
    row_blocks = [partner(value, "expert", 2 * (1 + k)) for k, value in enumerate(sent)][::-1]
    grad_keep, grad_swap, up_mat, turned = call(
        gather_scaled_kernel,
        (one, one, shape(up_mat.shape, BF16), shape((tok_rows, slots), BF16)),
        0,
        0,
    )(pick, weight, grad_out, up_mat)
    grad_swap = partner(grad_swap, "expert", 1)
    sent = call(pack_back_kernel, [pair] * (half - 1), 0, 8 * slots)(grad_keep, grad_swap)
    grad_blocks = [partner(value, "expert", 2 * (1 + k)) for k, value in enumerate(sent)][::-1]
    rows, *part_pre = call(
        functools.partial(gate_up_kernel, half),
        (sized, *[shape((2, chunk, hidden), BF16)] * dp),
        2 * product,
        2 * weights,
        scratch_shapes=in_order,
    )(keep, swap, *row_blocks, gate_mat, up_mat)
    sums = trade(part_pre)
    grads, *part_grad = call(
        functools.partial(grad_act_kernel, half, dp),
        (sized, *[shape((2, chunk, hidden), BF16)] * dp),
        product,
        weights,
        scratch_shapes=in_order,
    )(*sums, grad_keep, grad_swap, *grad_blocks, down_mat)
    grad_sums = trade(part_grad)
    pre_mine = call(
        functools.partial(grad_pre_kernel, dp),
        shape((2, chunk, hidden), BF16),
        0,
        6 * dp * chunk * hidden,
    )(*sums, *grad_sums)
    pre = trade([pre_mine] * dp)
    act, out_keep, out_swap = call(
        functools.partial(expert_out_kernel, dp),
        (wide, one, one),
        product,
        weights,
        scratch_shapes=in_order,
    )(*grad_sums, down_mat)
    back = [pair] * (half - 1)
    out_swap = partner(out_swap, "expert", 1)
    out_near, *out_far = call(pack_back_kernel, back, 0, 8 * slots)(out_keep, out_swap)
    out_far = [partner(value, "expert", 2 * (2 + k)) for k, value in enumerate(out_far)]
    pre, out_far = lax.optimization_barrier((pre, out_far))
    gate_pre, up_pre, grad_keep, grad_swap = call(
        functools.partial(row_grad_kernel, dp),
        (wide, wide, one, one),
        2 * product,
        2 * weights,
        scratch_shapes=in_order,
    )(*pre, gate_mat, up_mat)
    grad_swap = partner(grad_swap, "expert", 1)
    out_near = partner(out_near, "expert", 2)
    grad_to = call(pack_back_kernel, back, 0, 8 * slots)(grad_keep, grad_swap)
    grad_back = [partner(value, "expert", 2 * (1 + k)) for k, value in enumerate(grad_to)]

    (grad_down,) = call(
        functools.partial(grads_kernel, 1),
        [shape((hidden, features), BF16)],
        product,
        weights,
    )(act, grads)
    grad_gate, grad_up = call(
        functools.partial(grads_kernel, 2),
        [shape((features, hidden), BF16)] * 2,
        2 * product,
        2 * weights,
        in_specs=[HERE] * 3 + [ANY],
    )(rows, gate_pre, up_pre, grad_to[0])

    full = shape((tok_rows, features), BF16)
    flight = dict(
        out_specs=ANY,
        scratch_shapes=[pltpu.VMEM(full.shape, BF16), pltpu.SemaphoreType.DMA((4,))],
    )
    mixed = call(
        functools.partial(scatter_scaled_kernel, half),
        full,
        2 * slots * tok_rows * features,
        4 * tok_rows * features,
        in_specs=[HERE] * (half + 3) + [ANY],
        **flight,
    )(turned, weight, out_keep, out_swap, *out_far[::-1], out_near, grad_to[0])
    grad_tokens = call(
        functools.partial(scatter_kernel, half),
        full,
        2 * slots * tok_rows * features,
        4 * tok_rows * features,
        **flight,
    )(turned, grad_keep, grad_swap, *grad_back[::-1])
    return (mixed, grad_tokens, grad_gate[None], grad_up[None], grad_down[None])


def solution(mesh):
    placed = (
        P("expert", "dp"),
        P("expert", "dp"),
        P("expert", None),
        P("expert", None),
        P("expert", "dp", None),
        P("expert", "dp", None),
        P("expert", None, "dp"),
    )
    return jax.shard_map(
        body,
        mesh=mesh,
        in_specs=placed,
        out_specs=(
            P("expert", "dp"),
            P("expert", "dp"),
            P("expert", "dp", None),
            P("expert", "dp", None),
            P("expert", None, "dp"),
        ),
        check_vma=False,
    )
```
